32 devices in a mesh: cfg: 2 (over core), req: 4 (over z), seq: 4 (over y, x).
Axes of the slice: x: 2, y: 2, z: 4, core: 2. Of those that a mesh axis runs over, the one named last changes fastest.
Arguments:
- queries: bfloat16 [2, 4, 192, 1536], P('cfg', 'req', 'seq'), may hold values from -50 to 50
- text_cache: bfloat16 [2, 4, 2, 512, 1536], P('cfg', 'req'), may hold values from -6 to 6
- image_cache: bfloat16 [2, 4, 2, 192, 1536], P('cfg', 'req'), may hold values from -6 to 6
- fresh_kv: bfloat16 [2, 4, 2, 24, 1536], P('cfg', 'req', None, 'seq'), may hold values from -6 to 6
- fresh_slots: int32 [4, 24], P('req'), may hold values from 0 to 191, as said below
- fresh_pos: int32 [3, 4, 24], P(None, 'req', 'seq'), may hold values from 0 to 63
- image_len: int32 [4], replicated, may hold values from 96 to 192, as said below
- stream: bfloat16 [2, 4, 192, 3072], P('cfg', None, 'seq', 'req'), may hold values from -30 to 30
- modulation: float32 [2, 4, 4, 3072], replicated, may hold values from -4 to 4
- out_weight: bfloat16 [1536, 3072], P('seq', 'req'), may hold values from -0.15625 to 0.15625
- up_weight: bfloat16 [3072, 12288], P('seq', 'req'), may hold values from -0.109375 to 0.109375
- down_weight: bfloat16 [12288, 3072], P('req', 'seq'), may hold values from -0.0546875 to 0.0546875
- final_weight: bfloat16 [3072, 64], replicated, may hold values from -0.109375 to 0.109375
- latent: float32 [4, 96, 128], P('req', 'seq', 'cfg'), may hold values from -6 to 6
- step_index: int32 [1], replicated, may hold values from 0 to 27
Outputs:
- latent_next: float32 [4, 96, 128], P('req', 'seq', 'cfg')
- denoised: float32 [4, 96, 128], P('req', 'seq', 'cfg')
The draws below stay inside these ranges and needn't reach their ends.
Inputs may be any that keep to these rules, and one draw needn't show every extreme that they name: `fresh_slots`: columns k * 6 to (k + 1) * 6 - 1 of a row hold distinct slots from k * 48 to (k + 1) * 48 - 1. `image_len`: some request has exactly 192 image tokens and some other exactly 96.
All inputs are finite; a program needn't handle non-finite values.
Results may differ from the reference program's by a relative error of at most 0.0095.
Values may be sent and summed in bfloat16 or wider, within the bound.
No kernel may reach another device: no remote copies, remote signals or barrier semaphores. Data moves between devices by JAX's collectives and lax.ppermute only.
A program may use at most 128 MiB of HBM per device.

```python
import math
import jax
import jax.numpy as jnp
from jax import lax

D = 3072
LAT = 64
FFW = 12288
TXT = 512
STEPS = 28
IMG_DEV = 48
HD = 1536
R = 4
IMG_MAX = 192
FRESH_DEV = 6
FRESH = 24


def joint_attention_draw(key):
    query_key = jax.random.fold_in(key, 101)
    text_key = jax.random.fold_in(key, 102)
    query_shape = (2, R, IMG_MAX, HD)
    text_shape = (2, R, 2, TXT, HD)
    query_vals = jnp.clip(2.0 * jax.random.normal(query_key, query_shape, jnp.float32), -12.0, 12.0)
    text_vals = jnp.clip(jax.random.normal(text_key, text_shape, jnp.float32), -6.0, 6.0)
    return (query_vals.astype(jnp.bfloat16), text_vals.astype(jnp.bfloat16))


def draw_queries(key, part):
    return joint_attention_draw(key)[0]


def draw_text_cache(key, part):
    return joint_attention_draw(key)[1]


def draw_fresh_slots(key, part):
    blocks = FRESH // FRESH_DEV
    sub_keys = jax.random.split(jax.random.fold_in(key, 7), R * blocks)
    chosen = jax.vmap(lambda sub_key: jax.random.permutation(sub_key, IMG_DEV)[:FRESH_DEV])(sub_keys)
    offsets = jnp.arange(R * blocks, dtype=jnp.int32) % blocks * IMG_DEV
    return (chosen.astype(jnp.int32) + offsets[:, None]).reshape(R, FRESH)


def draw_image_len(key, part):
    lengths = jax.random.randint(jax.random.fold_in(key, 1), (R,), IMG_MAX // 2, IMG_MAX + 1)
    longest = jax.random.randint(jax.random.fold_in(key, 2), (), 0, R)
    row_ids = jnp.arange(R)
    lengths = jnp.where(row_ids == longest, IMG_MAX, lengths)
    lengths = jnp.where(row_ids == (longest + 1) % R, IMG_MAX // 2, lengths)
    return lengths.astype(jnp.int32)


def draw_stream(key, part):
    shape = (2, R, IMG_MAX, D)
    noise_key = jax.random.fold_in(key, 21)
    row_key = jax.random.fold_in(key, 22)
    col_key = jax.random.fold_in(key, 23)
    row_scale = jnp.exp(jax.random.uniform(row_key, (2, R, IMG_MAX, 1), jnp.float32, 0.0, math.log(10.0))) / 3.0
    col_scale = jnp.exp(jax.random.uniform(col_key, (1, 1, 1, D), jnp.float32, 0.0, math.log(10.0))) / 3.0
    noise = jnp.clip(jax.random.normal(noise_key, shape, jnp.float32), -5.0, 5.0)
    return jnp.clip(noise * row_scale * col_scale, -30.0, 30.0).astype(jnp.bfloat16)


def touch_ends(entries, own_key, least, top_value):
    longest = entries.shape.index(max(entries.shape))
    spots = []
    for shift in (0, 1):
        where = [jax.random.randint(jax.random.fold_in(own_key, axis), (), 0, length) for axis, length in enumerate(entries.shape)]
        where[longest] = (where[longest] + shift) % entries.shape[longest]
        spots.append(tuple(where))
    return entries.at[spots[0]].set(least).at[spots[1]].set(top_value)


def levels(key, extent, shards, low, high):
    def one(dim, shards_of):
        heights = jax.random.uniform(jax.random.fold_in(jax.random.fold_in(key, 6), dim), (shards_of,), jnp.float32, low / len(shards), high / len(shards))
        return jnp.repeat(jnp.exp(heights), extent[dim] // shards_of).reshape((-1,) + (1,) * (len(extent) - dim - 1))

    factor_of = one(*shards[0])
    for cut in shards[1:]:
        factor_of = factor_of * one(*cut)
    return factor_of


def gaussian(rng, dims, scale, bound, cuts=(), kind=jnp.bfloat16):
    factor_of = levels(rng, dims, cuts, -0.22, 0.18) if cuts else 1.0
    result = jax.random.normal(rng, dims, jnp.float32) * scale * factor_of
    return jnp.minimum(jnp.maximum(result, -bound), bound).astype(kind)


def setup_inputs(seed: int = 0) -> dict:
    splits = jax.random.split(jax.random.key(seed), 16)
    queries = draw_queries(jax.random.fold_in(splits[15], 71), 0)
    text_cache = draw_text_cache(jax.random.fold_in(splits[15], 71), 0)
    image_cache = gaussian(splits[2], (2, R, 2, IMG_MAX, HD), 1.0, 6.0, ((0, 2), (1, 4)))
    fresh_kv = gaussian(splits[3], (2, R, 2, FRESH, HD), 1.0, 6.0, ((0, 2), (1, 4), (3, 4)))
    fresh_slots = draw_fresh_slots(jax.random.fold_in(splits[15], 71), 0)
    fresh_pos = touch_ends(jax.random.randint(splits[5], (3, R, FRESH), 0, 64), jax.random.fold_in(splits[5], 1), 0, 63).astype(jnp.int32)
    image_len = draw_image_len(jax.random.fold_in(splits[15], 71), 0)
    stream = draw_stream(jax.random.fold_in(splits[15], 71), 0)
    modulation = gaussian(splits[8], (2, R, 4, D), 1.0, 4.0, (), jnp.float32)
    out_weight = gaussian(splits[9], (HD, D), HD ** -0.5, 0.15625, ((0, 4), (1, 4)))
    up_weight = gaussian(splits[10], (D, FFW), D ** -0.5, 0.109375, ((0, 4), (1, 4)))
    down_weight = gaussian(splits[11], (FFW, D), FFW ** -0.5, 0.0546875, ((0, 4), (1, 4)))
    final_weight = gaussian(splits[12], (D, LAT), D ** -0.5, 0.109375)
    latent = gaussian(splits[13], (R, IMG_MAX // 2, 2 * LAT), 1.0, 6.0, ((0, 4), (1, 4), (2, 2)), jnp.float32)
    step_index = jax.random.randint(splits[14], (1,), 0, STEPS).astype(jnp.int32)
    return {"queries": queries, "text_cache": text_cache, "image_cache": image_cache, "fresh_kv": fresh_kv, "fresh_slots": fresh_slots, "fresh_pos": fresh_pos, "image_len": image_len, "stream": stream, "modulation": modulation, "out_weight": out_weight, "up_weight": up_weight, "down_weight": down_weight, "final_weight": final_weight, "latent": latent, "step_index": step_index}


GUIDANCE = 3.0
SHIFT = 3.0
SCALE = 1.0 / math.sqrt(128.0)
EPSILON = 1e-06

def rope_angles(positions):
    columns = []
    for component, axis_span in ((0, 16), (1, 56), (2, 56)):
        pair_ids = jnp.arange(axis_span // 2, dtype=jnp.float32)
        frequency = jnp.exp(-(2.0 * pair_ids / axis_span) * math.log(10000.0))
        columns.append(positions[component].astype(jnp.float32)[:, None] * frequency[None, :])
    return jnp.concatenate(columns, axis=1)

def rotate(key_rows, angles):
    row_total = key_rows.shape[0]
    paired = key_rows.reshape(row_total, -1, 64, 2)
    cosine = jnp.cos(angles)[:, None, :]
    sine = jnp.sin(angles)[:, None, :]
    first = cosine * paired[..., 0] - sine * paired[..., 1]
    second = sine * paired[..., 0] + cosine * paired[..., 1]
    return jnp.stack([first, second], axis=-1).reshape(row_total, -1)

def noise_level(index):
    fraction = 1.0 - index.astype(jnp.float32) / STEPS
    return SHIFT * fraction / (SHIFT * fraction + 1.0 - fraction)

def attend(query_rows, text_kv, image_kv, length):
    query_count = query_rows.shape[0]
    query_heads = query_rows.astype(jnp.float32).reshape(query_count, -1, 128)
    key_rows = jnp.concatenate([text_kv[0], image_kv[0]], axis=0).astype(jnp.float32)
    value_rows = jnp.concatenate([text_kv[1], image_kv[1]], axis=0).astype(jnp.float32)
    key_heads = key_rows.reshape(key_rows.shape[0], -1, 128)
    value_heads = value_rows.reshape(value_rows.shape[0], -1, 128)
    scores = jnp.einsum('qhd,khd->hqk', query_heads, key_heads) * SCALE
    key_place = jnp.concatenate([jnp.zeros((TXT,), jnp.int32), jnp.arange(IMG_MAX, dtype=jnp.int32)])
    scores = jnp.where((key_place < length)[None, None, :], scores, -jnp.inf)
    row_max = lax.optimization_barrier(jnp.max(scores, axis=-1, keepdims=True))
    probs = jnp.exp(scores - row_max)
    total = lax.optimization_barrier(jnp.sum(probs, axis=-1))
    weights = lax.optimization_barrier(probs.astype(jnp.bfloat16)).astype(jnp.float32)
    mixed = jnp.einsum('hqk,khd->qhd', weights, value_heads) / jnp.transpose(total)[:, :, None]
    return mixed.reshape(query_count, -1).astype(jnp.bfloat16)

def reference(queries, text_cache, image_cache, fresh_kv, fresh_slots, fresh_pos, image_len, stream, modulation, out_weight, up_weight, down_weight, final_weight, latent, step_index):
    angles = rope_angles(fresh_pos.reshape(3, R * FRESH))
    angles = jnp.tile(angles, (2, 1))
    fresh_keys = rotate(fresh_kv[:, :, 0].astype(jnp.float32).reshape(2 * R * FRESH, HD), angles)
    fresh_keys = fresh_keys.astype(jnp.bfloat16).reshape(2, R, FRESH, HD)
    fresh_pair = jnp.stack([fresh_keys, fresh_kv[:, :, 1]], axis=2)
    slot_table = jnp.tile(fresh_slots, (2, 1)).astype(jnp.int32)
    lengths = jnp.tile(image_len, 2)

    def one_request(items):
        query_rows, text_kv, image_kv, pair_rows, slot_ids, length = items
        image_kv = image_kv.at[:, slot_ids, :].set(pair_rows)
        return attend(query_rows, text_kv, image_kv, length)
    attended = lax.map(one_request, (queries.reshape(2 * R, IMG_MAX, HD), text_cache.reshape(2 * R, 2, TXT, HD), image_cache.reshape(2 * R, 2, IMG_MAX, HD), fresh_pair.reshape(2 * R, 2, FRESH, HD), slot_table, lengths))

    def layer(items):
        attended_rows, stream_rows, mod_rows = items
        projected = jnp.dot(attended_rows, out_weight, preferred_element_type=jnp.float32)
        residual = (stream_rows.astype(jnp.float32) + mod_rows[0][None, :] * projected).astype(jnp.bfloat16)
        wide = residual.astype(jnp.float32)
        average = lax.optimization_barrier(jnp.mean(wide, axis=-1, keepdims=True))
        centered = wide - average
        spread = lax.optimization_barrier(jnp.mean(centered * centered, axis=-1, keepdims=True))
        normed = (centered * lax.rsqrt(spread + EPSILON) * (1.0 + mod_rows[2][None, :]) + mod_rows[1][None, :]).astype(jnp.bfloat16)
        activated = jax.nn.gelu(jnp.dot(normed, up_weight, preferred_element_type=jnp.float32), approximate=True).astype(jnp.bfloat16)
        mlp_out = jnp.dot(activated, down_weight, preferred_element_type=jnp.float32)
        block_out = (wide + mod_rows[3][None, :] * mlp_out).astype(jnp.bfloat16)
        return jnp.dot(block_out, final_weight, preferred_element_type=jnp.float32)
    velocity = lax.map(layer, (attended, stream.reshape(2 * R, IMG_MAX, D), modulation.reshape(2 * R, 4, D)))
    velocity = velocity.reshape(2, R, IMG_MAX // 2, 2 * LAT)
    guided = velocity[1] + GUIDANCE * (velocity[0] - velocity[1])
    level_now = noise_level(step_index[0])
    level_next = noise_level(step_index[0] + 1)
    token_ids = 2 * jnp.arange(IMG_MAX // 2, dtype=jnp.int32)[:, None] + jnp.arange(2 * LAT, dtype=jnp.int32)[None, :] // LAT
    valid = token_ids[None, :, :] < image_len[:, None, None]
    latent_next = jnp.where(valid, latent + (level_next - level_now) * guided, latent)
    denoised = jnp.where(valid, latent - level_now * guided, latent)
    return (latent_next, denoised)
```

```python
import math

import jax
import jax.numpy as jnp
from jax import lax
from jax.sharding import PartitionSpec as P

STEPS = 28
GUIDANCE = 3.0
SHIFT = 3.0
SCALE = 1.0 / math.sqrt(128.0)
EPSILON = 1e-06


def rope_angles(positions):
    columns = []
    for component, axis_span in ((0, 16), (1, 56), (2, 56)):
        pair_ids = jnp.arange(axis_span // 2, dtype=jnp.float32)
        frequency = jnp.exp(-(2.0 * pair_ids / axis_span) * math.log(10000.0))
        columns.append(positions[component].astype(jnp.float32)[:, None] * frequency[None, :])
    return jnp.concatenate(columns, axis=1)


def rotate(key_rows, angles):
    row_total = key_rows.shape[0]
    paired = key_rows.reshape(row_total, -1, 64, 2)
    cosine = jnp.cos(angles)[:, None, :]
    sine = jnp.sin(angles)[:, None, :]
    first = cosine * paired[..., 0] - sine * paired[..., 1]
    second = sine * paired[..., 0] + cosine * paired[..., 1]
    return jnp.stack([first, second], axis=-1).reshape(row_total, -1)


def noise_level(index):
    fraction = 1.0 - index.astype(jnp.float32) / STEPS
    return SHIFT * fraction / (SHIFT * fraction + 1.0 - fraction)


def head_scores(query_heads, key_rows):
    key_heads = key_rows.reshape(key_rows.shape[0], -1, 128)
    return (
        jnp.einsum("qhd,khd->hqk", query_heads, key_heads, preferred_element_type=jnp.float32)
        * SCALE
    )


def head_mix(weights, value_rows):
    value_heads = value_rows.reshape(value_rows.shape[0], -1, 128)
    return jnp.einsum("hqk,khd->qhd", weights, value_heads, preferred_element_type=jnp.float32)


def seq_grid(count):
    columns = 2 ** ((count.bit_length() - 1) // 2)
    return count // columns, columns


def send_x(block, step):
    if step == 0:
        return block
    high, wide = seq_grid(lax.axis_size("seq"))
    route = [(y * wide + x, y * wide + (x + step) % wide) for y in range(high) for x in range(wide)]
    return lax.ppermute(block, "seq", route)


def send_y(block, step):
    if step == 0:
        return block
    high, wide = seq_grid(lax.axis_size("seq"))
    route = [(y * wide + x, (y + step) % high * wide + x) for y in range(high) for x in range(wide)]
    return lax.ppermute(block, "seq", route)


def send_z(block, step):
    if step == 0:
        return block
    count = lax.axis_size("req")
    return lax.ppermute(block, "req", [(r, (r + step) % count) for r in range(count)])


def swap_core(block):
    return lax.ppermute(block, "cfg", [(0, 1), (1, 0)])


def put(buffer, block, *starts):
    return lax.dynamic_update_slice(buffer, block, starts)


def take(array, start, size, axis):
    return lax.dynamic_slice_in_dim(array, start, size, axis)


def dot(left, right):
    return jnp.dot(left, right, preferred_element_type=jnp.float32)


def per_device(
    queries,
    text_cache,
    image_cache,
    fresh_kv,
    fresh_slots,
    fresh_pos,
    image_len,
    stream,
    modulation,
    out_weight,
    up_weight,
    down_weight,
    final_weight,
    latent,
    step_index,
):
    cfg_id = lax.axis_index("cfg")
    req_id = lax.axis_index("req")
    seq_id = lax.axis_index("seq")
    requests = lax.axis_size("req")
    high, wide = seq_grid(lax.axis_size("seq"))
    y_id, x_id = seq_id // wide, seq_id % wide
    dtype = up_weight.dtype

    def x_from(step):
        return (x_id - step) % wide

    def y_from(step):
        return (y_id - step) % high

    out_rows, col_count = out_weight.shape
    out_half = col_count // 2
    own_cols = take(out_weight, cfg_id * out_half, out_half, 1)
    proj_cols = jnp.zeros((out_rows * high * wide, col_count), dtype)
    proj_cols = put(proj_cols, out_weight, seq_id * out_rows, 0)
    for dy in range(high):
        along_y = send_y(own_cols, dy)
        for dx in range(wide):
            if dy == 0 and dx == 0:
                continue
            part = send_x(along_y, dx)
            other = swap_core(part)
            row = (y_from(dy) * wide + x_from(dx)) * out_rows
            proj_cols = put(proj_cols, part, row, cfg_id * out_half)
            proj_cols = put(proj_cols, other, row, (1 - cfg_id) * out_half)

    up_rows, hidden = up_weight.shape
    up_half = up_rows // 2
    hidden_x = hidden // wide
    own_up = take(up_weight, cfg_id * up_half, up_half, 0)
    up_cols = jnp.zeros((up_rows * high * wide, hidden_x), dtype)
    up_cols = put(up_cols, take(up_weight, x_id * hidden_x, hidden_x, 1), seq_id * up_rows, 0)
    for dx in range(wide):
        along_x = send_x(take(own_up, (x_id + dx) % wide * hidden_x, hidden_x, 1), dx)
        for dy in range(high):
            if dy == 0 and dx == 0:
                continue
            part = send_y(along_x, dy)
            other = swap_core(part)
            row = (y_from(dy) * wide + x_from(dx)) * up_rows
            up_cols = put(up_cols, part, row + cfg_id * up_half, 0)
            up_cols = put(up_cols, other, row + (1 - cfg_id) * up_half, 0)

    down_cols = down_weight.shape[1]
    down_half = down_cols // 2
    own_down = take(down_weight, cfg_id * down_half, down_half, 1)
    down_parts = [(down_weight, seq_id * down_cols)]
    for dy in range(1, high):
        part = send_y(own_down, dy)
        other = swap_core(part)
        col = (y_from(dy) * wide + x_id) * down_cols
        down_parts.append((part, col + cfg_id * down_half))
        down_parts.append((other, col + (1 - cfg_id) * down_half))

    query_rows = queries[0, 0]
    row_count = query_rows.shape[0]
    query_heads = query_rows.reshape(row_count, -1, 128)
    text_kv = text_cache[0, 0]
    image_kv = image_cache[0, 0]
    angles = rope_angles(fresh_pos[:, 0, :])
    fresh_keys = rotate(fresh_kv[0, 0, 0].astype(jnp.float32), angles).astype(jnp.bfloat16)
    fresh_pair = jnp.stack([fresh_keys, fresh_kv[0, 0, 1]], axis=0)
    fresh_count = fresh_pair.shape[1]
    for dy in range(high):
        for dx in range(wide):
            rows = send_x(send_y(fresh_pair, dy), dx)
            first = (y_from(dy) * wide + x_from(dx)) * fresh_count
            image_kv = image_kv.at[:, take(fresh_slots[0], first, fresh_count, 0), :].set(rows)
    length = lax.dynamic_index_in_dim(image_len, req_id, 0, keepdims=False)
    image_total = image_kv.shape[1]
    text_scores = head_scores(query_heads, text_kv[0])
    text_best = jnp.max(text_scores, axis=-1, keepdims=True)
    live_keys = (jnp.arange(image_total) < length)[None, None, :]
    image_scores = jnp.where(live_keys, head_scores(query_heads, image_kv[0]), -jnp.inf)
    row_max = jnp.maximum(text_best, jnp.max(image_scores, axis=-1, keepdims=True))
    text_probs = jnp.exp(text_scores - row_max)
    image_probs = jnp.exp(image_scores - row_max)
    total = jnp.sum(text_probs, axis=-1) + jnp.sum(image_probs, axis=-1)
    mixed = head_mix(text_probs.astype(jnp.bfloat16), text_kv[1]) + head_mix(
        image_probs.astype(jnp.bfloat16), image_kv[1]
    )
    attended = (
        (mixed / jnp.transpose(total)[:, :, None]).reshape(row_count, -1).astype(jnp.bfloat16)
    )

    attended_all = jnp.zeros((requests, *attended.shape), attended.dtype)
    for dz in range(requests):
        attended_all = put(attended_all, send_z(attended, dz)[None], (req_id - dz) % requests, 0, 0)
    projected = dot(attended_all.reshape(requests * row_count, -1), proj_cols)
    mod_half = lax.dynamic_index_in_dim(modulation, cfg_id, 0, keepdims=False)
    gate_cols = take(mod_half[:, 0, :], req_id * col_count, col_count, 1)
    residual = (
        stream[0].astype(jnp.float32)
        + gate_cols[:, None, :] * projected.reshape(requests, row_count, col_count)
    ).astype(jnp.bfloat16)

    model = requests * col_count
    full_rows = jnp.zeros((wide, requests, row_count, model), residual.dtype)
    for dz in range(requests):
        along_z = send_z(residual, dz)
        col = (req_id - dz) % requests * col_count
        for dx in range(wide):
            full_rows = put(full_rows, send_x(along_z, dx)[None], x_from(dx), 0, 0, col)
    widened = full_rows.astype(jnp.float32)
    average = jnp.mean(widened, axis=-1, keepdims=True)
    centered = widened - average
    spread = jnp.mean(centered * centered, axis=-1, keepdims=True)
    normed = (
        centered * lax.rsqrt(spread + EPSILON) * (1.0 + mod_half[:, 2][:, None, :])
        + mod_half[:, 1][:, None, :]
    )
    row_total = wide * requests * row_count
    normed = normed.astype(jnp.bfloat16).reshape(row_total, model)
    activated = jax.nn.gelu(dot(normed, up_cols), approximate=True).astype(jnp.bfloat16)
    act_all = jnp.zeros((row_total, hidden), activated.dtype)
    for dx in range(wide):
        act_all = put(act_all, send_x(activated, dx), 0, x_from(dx) * hidden_x)

    own_rows = lax.dynamic_index_in_dim(full_rows, req_id, 1, keepdims=False)
    own_rows = own_rows.reshape(wide * row_count, model)
    gate_two = lax.dynamic_index_in_dim(mod_half[:, 3, :], req_id, 0, keepdims=False)
    velocity = jnp.zeros((wide * row_count, final_weight.shape[1]), jnp.float32)
    for weight, col in down_parts:
        size = weight.shape[1]
        part = dot(act_all, weight).reshape(wide, requests, row_count, size)
        total_part = 0.0
        for dz in range(requests):
            block = lax.dynamic_index_in_dim(part, (req_id + dz) % requests, 1, keepdims=False)
            total_part += send_z(block.astype(jnp.bfloat16), dz).astype(jnp.float32)
        total_part = total_part.reshape(wide * row_count, size)
        block_out = (
            take(own_rows, col, size, 1).astype(jnp.float32)
            + take(gate_two, col, size, 0)[None, :] * total_part
        ).astype(jnp.bfloat16)
        velocity += dot(block_out, take(final_weight, col, size, 0))

    channels = velocity.shape[1]
    velocity = velocity.reshape(wide, row_count // 2, 2, channels)
    cfg_count, seq_count = lax.axis_size("cfg"), lax.axis_size("seq")
    halves = []
    for dc in range(2):
        share = 0.0
        for dx in range(wide):
            block = lax.dynamic_index_in_dim(velocity, (x_id + dx) % wide, 0, keepdims=False)
            block = lax.dynamic_index_in_dim(block, cfg_id ^ dc, 1, keepdims=False)
            if dc or dx:
                route = [
                    (
                        (c * high + y) * wide + x,
                        ((c ^ dc) * high + y) * wide + (x + dx) % wide,
                    )
                    for c in range(cfg_count)
                    for y in range(high)
                    for x in range(wide)
                ]
                block = lax.ppermute(block, ("cfg", "seq"), route)
            share += block
        halves.append(share)
    cond_part = jnp.where(cfg_id == 0, halves[0], halves[1])
    uncond_part = jnp.where(cfg_id == 0, halves[1], halves[0])
    guided = uncond_part + GUIDANCE * (cond_part - uncond_part)
    level_now = noise_level(step_index[0])
    level_next = noise_level(step_index[0] + 1)
    token_ids = (
        seq_id * row_count
        + 2 * jnp.arange(row_count // 2, dtype=jnp.int32)[:, None]
        + cfg_id
        + jnp.zeros((1, channels), jnp.int32)
    )
    valid = token_ids < length
    current = latent[0]
    latent_next = jnp.where(valid, current + (level_next - level_now) * guided, current)
    denoised = jnp.where(valid, current - level_now * guided, current)
    return (latent_next[None], denoised[None])


def solution(mesh):
    in_specs = (
        P("cfg", "req", "seq", None),
        P("cfg", "req", None, None, None),
        P("cfg", "req", None, None, None),
        P("cfg", "req", None, "seq", None),
        P("req", None),
        P(None, "req", "seq"),
        P(),
        P("cfg", None, "seq", "req"),
        P(),
        P("seq", "req"),
        P("seq", "req"),
        P("req", "seq"),
        P(),
        P("req", "seq", "cfg"),
        P(),
    )
    out_specs = (P("req", "seq", "cfg"), P("req", "seq", "cfg"))
    return jax.shard_map(
        per_device, mesh=mesh, in_specs=in_specs, out_specs=out_specs, check_vma=False
    )
```

```python
import functools
import math

import jax
import jax.numpy as jnp
import numpy as np
from jax import lax
from jax.experimental import pallas as pl
from jax.experimental.pallas import tpu as pltpu
from jax.sharding import PartitionSpec as P

STEPS = 28
GUIDANCE = 3.0
SHIFT = 3.0
SCALE = 1.0 / math.sqrt(128.0)
EPSILON = 1e-06
HEAD = 128
BF16 = jnp.bfloat16
F32 = jnp.float32
VMEM_LIMIT = 48 * 1024 * 1024


def noise_level(index):
    fraction = 1.0 - index.astype(jnp.float32) / STEPS
    return SHIFT * fraction / (SHIFT * fraction + 1.0 - fraction)


def lane_frequencies():
    rows = np.zeros((3, HEAD), np.float32)
    lane = 0
    for component, axis_span in ((0, 16), (1, 56), (2, 56)):
        pair_ids = np.arange(axis_span // 2, dtype=np.float32)
        frequency = np.exp(-(2.0 * pair_ids / axis_span) * np.float32(math.log(10000.0)))
        rows[component, lane : lane + axis_span] = np.repeat(frequency, 2)
        lane += axis_span
    return rows


def seq_grid(count):
    columns = 2 ** ((count.bit_length() - 1) // 2)
    return count // columns, columns


def send_x(block, step):
    if step == 0:
        return block
    high, wide = seq_grid(lax.axis_size("seq"))
    route = [(y * wide + x, y * wide + (x + step) % wide) for y in range(high) for x in range(wide)]
    return lax.ppermute(block, "seq", route)


def send_y(block, step):
    if step == 0:
        return block
    high, wide = seq_grid(lax.axis_size("seq"))
    route = [(y * wide + x, (y + step) % high * wide + x) for y in range(high) for x in range(wide)]
    return lax.ppermute(block, "seq", route)


def send_seq(block, dy, dx):
    if dy == 0 and dx == 0:
        return block
    high, wide = seq_grid(lax.axis_size("seq"))
    route = [
        (y * wide + x, (y + dy) % high * wide + (x + dx) % wide)
        for y in range(high)
        for x in range(wide)
    ]
    return lax.ppermute(block, "seq", route)


def send_z(block, step):
    if step == 0:
        return block
    count = lax.axis_size("req")
    return lax.ppermute(block, "req", [(r, (r + step) % count) for r in range(count)])


def swap_core(block):
    return lax.ppermute(block, "cfg", [(0, 1), (1, 0)])


def take(array, start, size, axis):
    return lax.dynamic_slice_in_dim(array, start, size, axis)


def dot(left, right):
    return jnp.dot(left, right, preferred_element_type=jnp.float32)


def whole_spec():
    return pl.BlockSpec(memory_space=pltpu.VMEM)


def smem_spec():
    return pl.BlockSpec(memory_space=pltpu.SMEM)


def params():
    return pltpu.CompilerParams(vmem_limit_bytes=VMEM_LIMIT)


def rotate_kernel(kv_ref, pos_ref, freq_ref, out_ref):
    rows, width = kv_ref.shape[1:]
    pos = pos_ref[...].astype(F32)
    angles = (
        pos[:, 0:1] * freq_ref[0:1, :]
        + pos[:, 1:2] * freq_ref[1:2, :]
        + pos[:, 2:3] * freq_ref[2:3, :]
    )
    cosine, sine = jnp.cos(angles), jnp.sin(angles)
    even = lax.broadcasted_iota(jnp.int32, (rows, HEAD), 1) % 2 == 0
    out_ref[...] = jnp.zeros_like(out_ref)
    for first in range(0, width, HEAD):
        keys = kv_ref[0, :, first : first + HEAD].astype(F32)
        after = pltpu.roll(keys, HEAD - 1, 1)
        before = pltpu.roll(keys, 1, 1)
        rotated = cosine * keys + sine * jnp.where(even, -after, before)
        out_ref[0, 0:rows, first : first + HEAD] = rotated.astype(BF16)
    out_ref[1, 0:rows, :] = kv_ref[1]


def rotate_fresh(fresh, positions, padded):
    width = fresh.shape[2]
    return pl.pallas_call(
        rotate_kernel,
        out_shape=jax.ShapeDtypeStruct((2, padded, width), BF16),
        in_specs=[whole_spec()] * 3,
        out_specs=whole_spec(),
        compiler_params=params(),
    )(fresh, positions, jnp.asarray(lane_frequencies()))


def attention_kernel(pieces, q_ref, text_ref, image_ref, bias_ref, *refs):
    fresh_refs, out_ref, fresh_ref = refs[:pieces], refs[pieces], refs[pieces + 1]
    padded = fresh_refs[0].shape[1]
    for i in range(pieces):
        fresh_ref[:, i * padded : (i + 1) * padded, :] = fresh_refs[i][...]
    slots = image_ref.shape[1]
    image_bias = bias_ref[:, 0:slots]
    fresh_bias = bias_ref[:, slots:]
    over_lanes = (((1,), (1,)), ((), ()))
    for first in range(0, q_ref.shape[1], HEAD):
        head = slice(first, first + HEAD)
        query = q_ref[:, head]

        def scores(keys):
            return lax.dot_general(query, keys, over_lanes, preferred_element_type=F32) * SCALE

        text = scores(text_ref[0, :, head])
        image = scores(image_ref[0, :, head]) + image_bias
        fresh = scores(fresh_ref[0, :, head]) + fresh_bias
        best = jnp.maximum(
            jnp.max(text, axis=1, keepdims=True),
            jnp.maximum(
                jnp.max(image, axis=1, keepdims=True), jnp.max(fresh, axis=1, keepdims=True)
            ),
        )
        text, image, fresh = jnp.exp(text - best), jnp.exp(image - best), jnp.exp(fresh - best)
        total = (
            jnp.sum(text, axis=1, keepdims=True)
            + jnp.sum(image, axis=1, keepdims=True)
            + jnp.sum(fresh, axis=1, keepdims=True)
        )
        mixed = (
            dot(text.astype(BF16), text_ref[1, :, head])
            + dot(image.astype(BF16), image_ref[1, :, head])
            + dot(fresh.astype(BF16), fresh_ref[1, :, head])
        )
        out_ref[0, :, head] = (mixed / total).astype(BF16)


def attention(query, text_kv, image_kv, bias, fresh):
    rows, width = query.shape
    group = 3 * HEAD
    groups = width // group
    pieces = len(fresh)
    text, slots, padded = text_kv.shape[1], image_kv.shape[1], fresh[0].shape[1]
    return pl.pallas_call(
        functools.partial(attention_kernel, pieces),
        grid=(groups,),
        out_shape=jax.ShapeDtypeStruct((groups, rows, group), BF16),
        in_specs=[
            pl.BlockSpec((rows, group), lambda g: (0, g)),
            pl.BlockSpec((2, text, group), lambda g: (0, 0, g)),
            pl.BlockSpec((2, slots, group), lambda g: (0, 0, g)),
            pl.BlockSpec(bias.shape, lambda g: (0, 0)),
        ]
        + [pl.BlockSpec((2, padded, group), lambda g: (0, 0, g))] * pieces,
        out_specs=pl.BlockSpec((1, rows, group), lambda g: (g, 0, 0)),
        scratch_shapes=[pltpu.VMEM((2, padded * pieces, group), BF16)],
        compiler_params=params(),
    )(query, text_kv, image_kv, bias, *fresh)


def residual_kernel(requests, pieces, ids_ref, *refs):
    attended = refs[:requests]
    mine, other = refs[requests : requests + pieces], refs[requests + pieces : requests + 2 * pieces]
    stream_ref, gate_ref, out_ref, rows_ref = refs[requests + 2 * pieces :]
    row_count = attended[0].shape[1]
    for j in range(requests):
        first = pl.multiple_of(ids_ref[j] * row_count, 16)
        rows_ref[:, pl.ds(first, row_count), :] = attended[j][...]
    for half, weights in ((0, mine), (1, other)):
        total = None
        for k in range(pieces):
            term = dot(rows_ref[ids_ref[requests + k]], weights[k][...])
            total = term if total is None else total + term
        width = total.shape[1]
        total = total.reshape(requests, row_count, width)
        out_ref[half] = (
            stream_ref[half].astype(F32) + gate_ref[half][:, None, :] * total
        ).astype(BF16)


def residual_columns(ids, attended, mine, other, stream, gate):
    requests, pieces = len(attended), len(mine)
    segments, row_count, seg = attended[0].shape
    return pl.pallas_call(
        functools.partial(residual_kernel, requests, pieces),
        out_shape=jax.ShapeDtypeStruct(stream.shape, BF16),
        in_specs=[smem_spec()] + [whole_spec()] * (requests + 2 * pieces + 2),
        out_specs=whole_spec(),
        scratch_shapes=[pltpu.VMEM((segments, requests * row_count, seg), BF16)],
        compiler_params=params(),
    )(ids, *attended, *mine, *other, stream, gate)


def up_kernel(wide, requests, pieces, per_piece, ids_ref, *refs):
    count = wide * requests
    blocks = refs[:count]
    mod_ref = refs[count]
    mine = refs[count + 1 : count + 1 + pieces]
    other = refs[count + 1 + pieces : count + 1 + 2 * pieces]
    out_ref, own_ref, rows_ref = refs[count + 1 + 2 * pieces :]
    half, col = pl.program_id(0), pl.program_id(1)
    row_count, seg = blocks[0].shape[2:]
    model = 2 * requests * seg

    @pl.when((half == 0) & (col == 0))
    def _():
        for dx in range(wide):
            mine_x = blocks[dx * requests : (dx + 1) * requests]
            x_at = ids_ref[1 + dx]
            for q in range(requests):
                total = None
                for block in mine_x:
                    for h in range(2):
                        part = jnp.sum(block[h, q].astype(F32), axis=1, keepdims=True)
                        total = part if total is None else total + part
                average = total * (1.0 / model)
                total = None
                for block in mine_x:
                    for h in range(2):
                        centered = block[h, q].astype(F32) - average
                        part = jnp.sum(centered * centered, axis=1, keepdims=True)
                        total = part if total is None else total + part
                inverse = lax.rsqrt(total * (1.0 / model) + EPSILON)
                first = pl.multiple_of((q * wide + x_at) * row_count, 16)
                for dz, block in enumerate(mine_x):
                    place = ids_ref[1 + wide + dz]
                    for h in range(2):
                        centered = block[h, q].astype(F32) - average
                        scale = mod_ref[1, 2 * place + h, q : q + 1, :]
                        shift = mod_ref[0, 2 * place + h, q : q + 1, :]
                        rows_ref[2 * place + h, pl.ds(first, row_count), :] = (
                            centered * inverse * (1.0 + scale) + shift
                        ).astype(BF16)
            own = ids_ref[0]
            first = pl.multiple_of(x_at * row_count, 16)
            for dz, block in enumerate(mine_x):
                place = ids_ref[1 + wide + dz]
                for h in range(2):
                    own_ref[2 * place + h, pl.ds(first, row_count), :] = block[h, own]

    def product(weights):
        total = None
        for k in range(pieces):
            for i in range(per_piece):
                rows = rows_ref[ids_ref[1 + wide + requests + k * per_piece + i]]
                term = dot(rows, weights[k][i * seg : (i + 1) * seg, :])
                total = term if total is None else total + term
        out_ref[0] = jax.nn.gelu(total, approximate=True).astype(BF16)

    pl.when(half == 0)(lambda: product(mine))
    pl.when(half == 1)(lambda: product(other))


def up_products(ids, blocks, mod, mine, other, wide):
    requests, pieces = len(blocks) // wide, len(mine)
    row_count, seg = blocks[0].shape[2:]
    depth, width = mine[0].shape
    per_piece = depth // seg
    rows = requests * wide * row_count
    step = 256 if width % 256 == 0 else width
    cols = width // step
    return pl.pallas_call(
        functools.partial(up_kernel, wide, requests, pieces, per_piece),
        grid=(2, cols),
        out_shape=(
            jax.ShapeDtypeStruct((2, rows, width), BF16),
            jax.ShapeDtypeStruct((2 * requests, wide * row_count, seg), BF16),
        ),
        in_specs=[smem_spec()]
        + [pl.BlockSpec(block.shape, lambda h, c: (0, 0, 0, 0)) for block in blocks]
        + [pl.BlockSpec(mod.shape, lambda h, c: (0, 0, 0, 0))]
        + [pl.BlockSpec((depth, step), lambda h, c: (0, c * (1 - h) + h * (cols - 1)))] * pieces
        + [pl.BlockSpec((depth, step), lambda h, c: (0, c * h))] * pieces,
        out_specs=(
            pl.BlockSpec((1, rows, step), lambda h, c: (h, 0, c)),
            pl.BlockSpec((2 * requests, wide * row_count, seg), lambda h, c: (0, 0, 0)),
        ),
        scratch_shapes=[pltpu.VMEM((2 * requests, rows, seg), BF16)],
        compiler_params=params(),
    )(ids, *blocks, mod, *mine, *other)


def down_kernel(requests, acts, weights, has_start, last, ids_ref, *refs):
    act_refs, refs = refs[:acts], refs[acts:]
    weight_refs, refs = refs[:weights], refs[weights:]
    if has_start:
        start_ref, refs = refs[0], refs[1:]
    out_refs = refs[: requests if last else 1]
    total_ref = refs[-1]
    rows, depth = act_refs[0].shape[1:]

    def product(weight_ref):
        total = start_ref[...] if has_start else None
        for k in range(acts):
            for h in range(2):
                first = pl.multiple_of(ids_ref[1 + 2 * k + h] * depth, 16)
                term = dot(act_refs[k][h], weight_ref[pl.ds(first, depth), :])
                total = term if total is None else total + term
        if not last:
            out_refs[0][...] = total
            return
        total_ref[...] = total
        share = rows // requests
        for dz in range(requests):
            first = pl.multiple_of(lax.rem(ids_ref[0] + dz, requests) * share, 16)
            out_refs[dz][...] = total_ref[pl.ds(first, share), :].astype(BF16)

    if weights == 1:
        product(weight_refs[0])
    else:
        for w in range(weights):
            pl.when(pl.program_id(0) == w)(functools.partial(product, weight_refs[w]))


def down_products(ids, acts, weights, start, last, requests, step):
    rows, depth = acts[0].shape[1:]
    hidden, width = weights[0].shape
    if len(weights) > 1:
        steps, step = len(weights), width
    else:
        steps = width // step
    many = len(weights) > 1
    weight_map = (lambda c: (0, 0)) if many else (lambda c: (0, c))
    specs = [smem_spec()]
    specs += [pl.BlockSpec(act.shape, lambda c: (0, 0, 0)) for act in acts]
    specs += [pl.BlockSpec((hidden, step), weight_map)] * len(weights)
    operands = [ids, *acts, *weights]
    if start is not None:
        specs.append(pl.BlockSpec((None, rows, step), lambda c: (c, 0, 0)))
        operands.append(start)
    if last:
        outs = tuple(
            jax.ShapeDtypeStruct((steps, rows // requests, step), BF16) for _ in range(requests)
        )
        out_specs = tuple(
            pl.BlockSpec((None, rows // requests, step), lambda c: (c, 0, 0))
            for _ in range(requests)
        )
    else:
        outs = (jax.ShapeDtypeStruct((steps, rows, step), F32),)
        out_specs = (pl.BlockSpec((None, rows, step), lambda c: (c, 0, 0)),)
    return pl.pallas_call(
        functools.partial(
            down_kernel, requests, len(acts), len(weights), start is not None, last
        ),
        grid=(steps,),
        out_shape=outs,
        in_specs=specs,
        out_specs=out_specs,
        scratch_shapes=[pltpu.VMEM((rows, step), F32)],
        compiler_params=params(),
    )(*operands)


def per_device(
    queries,
    text_cache,
    image_cache,
    fresh_kv,
    fresh_slots,
    fresh_pos,
    image_len,
    stream,
    modulation,
    out_weight,
    up_weight,
    down_weight,
    final_weight,
    latent,
    step_index,
):
    cfg_id = lax.axis_index("cfg")
    req_id = lax.axis_index("req")
    seq_id = lax.axis_index("seq")
    requests = lax.axis_size("req")
    high, wide = seq_grid(lax.axis_size("seq"))
    y_id, x_id = seq_id // wide, seq_id % wide
    around = [(dy, dx) for dy in range(high) for dx in range(wide)]

    def x_from(step):
        return (x_id - step) % wide

    def y_from(step):
        return (y_id - step) % high

    def seq_from(dy, dx):
        return y_from(dy) * wide + x_from(dx)

    def ids(*values):
        return jnp.stack([jnp.asarray(value, jnp.int32) for value in values])

    fresh_count = fresh_kv.shape[3]
    padded = -(-fresh_count // 16) * 16
    fresh_pair = rotate_fresh(fresh_kv[0, 0], fresh_pos[:, 0, :].T, padded)
    fresh = [send_seq(fresh_pair, dy, dx) for dy, dx in around]

    out_rows, col_count = out_weight.shape
    seg = col_count // 2
    out_mine = [take(out_weight, cfg_id * seg, seg, 1)]
    out_other = [take(out_weight, (1 - cfg_id) * seg, seg, 1)]
    out_y = [send_y(out_mine[0], dy) for dy in range(high)]
    out_mine = [send_x(out_y[dy], dx) for dy, dx in around]
    swapped = swap_core(jnp.concatenate(out_mine[1:], axis=0))
    out_other += [
        lax.slice_in_dim(swapped, k * out_rows, (k + 1) * out_rows, axis=0)
        for k in range(len(around) - 1)
    ]

    up_rows, hidden = up_weight.shape
    hidden_x = hidden // wide
    hidden_half = hidden_x // 2
    up_along_x = []
    for dx in range(wide):
        first = (x_id + dx) % wide * hidden_x + cfg_id * hidden_half
        up_along_x.append(send_x(take(up_weight, first, hidden_half, 1), dx))
    own_other = take(up_weight, x_id * hidden_x + (1 - cfg_id) * hidden_half, hidden_half, 1)
    up_mine = [send_y(up_along_x[dx], dy) for dy, dx in around]
    up_other = [own_other] + [swap_core(part) for part in up_mine[1:]]

    down_cols = down_weight.shape[1]
    down_half = down_cols // 2
    own_down = take(down_weight, cfg_id * down_half, down_half, 1)
    own_down, _ = lax.optimization_barrier((own_down, up_mine[-1]))
    down_mine = [send_y(own_down, dy) for dy in range(1, high)]
    down_other = [swap_core(part) for part in down_mine]

    length = lax.dynamic_index_in_dim(image_len, req_id, 0, keepdims=False)
    image_kv = image_cache[0, 0]
    image_total = image_kv.shape[1]
    slot_ids = fresh_slots[0]
    key_ids = jnp.arange(image_total, dtype=jnp.int32)
    replaced = jnp.any(slot_ids[:, None] == key_ids[None, :], axis=0)
    kept = (key_ids < length) & ~replaced
    piece_slots = [
        jnp.pad(
            take(slot_ids, seq_from(dy, dx) * fresh_count, fresh_count, 0),
            (0, padded - fresh_count),
            constant_values=image_total,
        )
        for dy, dx in around
    ]
    live = jnp.concatenate([kept, jnp.concatenate(piece_slots) < length])
    bias = jnp.where(live, 0.0, -jnp.inf).astype(F32)[None, :]
    attended = attention(queries[0, 0], text_cache[0, 0], image_kv, bias, fresh)
    row_count = queries.shape[2]
    if attended.shape[2] != out_rows:
        attended = jnp.transpose(attended, (1, 0, 2)).reshape(row_count, -1, out_rows)
        attended = jnp.transpose(attended, (1, 0, 2))
    attended_all = [send_z(attended, dz) for dz in range(requests)]

    mod_half = lax.dynamic_index_in_dim(modulation, cfg_id, 0, keepdims=False)

    def halves_first(array, axis):
        shape = array.shape[:axis] + (-1, 2, seg) + array.shape[axis + 1 :]
        split = array.reshape(shape)
        return jnp.where(cfg_id == 0, split, jnp.flip(split, axis + 1))

    stream_halves = jnp.moveaxis(halves_first(stream[0], 2)[:, :, 0], 2, 0)
    gate_cols = take(mod_half[:, 0, :], req_id * col_count, col_count, 1)
    gate_halves = jnp.moveaxis(halves_first(gate_cols, 1)[:, 0], 1, 0)
    residual = residual_columns(
        ids(*[(req_id - dz) % requests for dz in range(requests)], *[seq_from(*d) for d in around]),
        attended_all,
        out_mine,
        out_other,
        stream_halves,
        gate_halves,
    )

    along_z = [send_z(residual, dz) for dz in range(requests)]
    blocks = [send_x(block, dx) for dx in range(wide) for block in along_z]
    mod_norm = jnp.stack([mod_half[:, 1], mod_half[:, 2]])
    mod_norm = jnp.moveaxis(halves_first(mod_norm, 2), 1, 3)
    mod_norm = mod_norm.reshape(2, 2 * requests, requests, seg)
    per_piece = up_rows // seg
    places = []
    for dy, dx in around:
        for i in range(per_piece):
            column = seq_from(dy, dx) * per_piece + i
            places.append(column // 2 * 2 + (column % 2 ^ cfg_id))
    act_own, own_rows = up_products(
        ids(
            req_id,
            *[x_from(dx) for dx in range(wide)],
            *[(req_id - dz) % requests for dz in range(requests)],
            *places,
        ),
        blocks,
        mod_norm,
        up_mine,
        up_other,
        wide,
    )

    acts = [send_x(act_own, dx) for dx in range(wide)]

    def act_places(first, last):
        values = [2 * x_from(dx) + (h ^ cfg_id) for dx in range(first, last) for h in range(2)]
        return ids(req_id, *values)

    own_weights = [down_weight]
    if down_half % 128:
        own_weights = [lax.slice_in_dim(down_weight, h * down_half, (h + 1) * down_half, axis=1) for h in range(2)]
    begun = down_products(
        act_places(0, 1), acts[:1], own_weights, None, False, requests, down_half
    )[0]
    own_share = down_products(
        act_places(1, wide), acts[1:], own_weights, begun, True, requests, down_half
    )
    far_share = down_products(
        act_places(0, wide), acts, down_mine + down_other, None, True, requests, down_half
    )
    model = requests * col_count
    natural = own_rows.reshape(requests, 2, wide * row_count, seg)
    natural = jnp.where(cfg_id == 0, natural, jnp.flip(natural, 1))
    natural = jnp.moveaxis(natural.reshape(2 * requests, wide * row_count, seg), 0, 1)
    natural = natural.reshape(wide * row_count, model).astype(F32)
    gate_two = lax.dynamic_index_in_dim(mod_half[:, 3, :], req_id, 0, keepdims=False)

    def finished(share, columns):
        total = share[0].astype(F32)
        for dz in range(1, requests):
            total += send_z(share[dz], dz).astype(F32)
        result = 0.0
        for k, col in enumerate(columns):
            block_out = (
                take(natural, col, down_half, 1)
                + take(gate_two, col, down_half, 0)[None, :] * total[k]
            ).astype(BF16)
            result += dot(block_out, take(final_weight, col, down_half, 0))
        return result

    far_cols = [seq_from(dy, 0) * down_cols + cfg_id * down_half for dy in range(1, high)]
    far_cols += [seq_from(dy, 0) * down_cols + (1 - cfg_id) * down_half for dy in range(1, high)]
    velocity = finished(own_share, [seq_id * down_cols + h * down_half for h in range(2)])
    velocity += finished(far_share, far_cols)

    channels = velocity.shape[1]
    velocity = velocity.reshape(wide, row_count // 2, 2, channels)
    cfg_count = lax.axis_size("cfg")
    halves = []
    for dc in range(2):
        share = 0.0
        for dx in range(wide):
            block = lax.dynamic_index_in_dim(velocity, (x_id + dx) % wide, 0, keepdims=False)
            block = lax.dynamic_index_in_dim(block, cfg_id ^ dc, 1, keepdims=False)
            if dc or dx:
                route = [
                    (
                        (c * high + y) * wide + x,
                        ((c ^ dc) * high + y) * wide + (x + dx) % wide,
                    )
                    for c in range(cfg_count)
                    for y in range(high)
                    for x in range(wide)
                ]
                block = lax.ppermute(block, ("cfg", "seq"), route)
            share += block
        halves.append(share)
    cond_part = jnp.where(cfg_id == 0, halves[0], halves[1])
    uncond_part = jnp.where(cfg_id == 0, halves[1], halves[0])
    guided = uncond_part + GUIDANCE * (cond_part - uncond_part)
    level_now = noise_level(step_index[0])
    level_next = noise_level(step_index[0] + 1)
    token_ids = (
        seq_id * row_count
        + 2 * jnp.arange(row_count // 2, dtype=jnp.int32)[:, None]
        + cfg_id
        + jnp.zeros((1, channels), jnp.int32)
    )
    valid = token_ids < length
    current = latent[0]
    latent_next = jnp.where(valid, current + (level_next - level_now) * guided, current)
    denoised = jnp.where(valid, current - level_now * guided, current)
    return (latent_next[None], denoised[None])


def solution(mesh):
    in_specs = (
        P("cfg", "req", "seq", None),
        P("cfg", "req", None, None, None),
        P("cfg", "req", None, None, None),
        P("cfg", "req", None, "seq", None),
        P("req", None),
        P(None, "req", "seq"),
        P(),
        P("cfg", None, "seq", "req"),
        P(),
        P("seq", "req"),
        P("seq", "req"),
        P("req", "seq"),
        P(),
        P("req", "seq", "cfg"),
        P(),
    )
    out_specs = (P("req", "seq", "cfg"), P("req", "seq", "cfg"))
    return jax.shard_map(
        per_device, mesh=mesh, in_specs=in_specs, out_specs=out_specs, check_vma=False
    )
```

```python
import functools
import math

import jax
import jax.numpy as jnp
import numpy as np
from jax import lax
from jax.experimental import pallas as pl
from jax.experimental.pallas import tpu as pltpu
from jax.sharding import PartitionSpec as P

STEPS = 28
GUIDANCE = 3.0
SHIFT = 3.0
SCALE = 1.0 / math.sqrt(128.0)
EPSILON = 1e-06
HEAD = 128
BF16 = jnp.bfloat16
F32 = jnp.float32
MIB = 1024 * 1024


def noise_level(index):
    fraction = 1.0 - index.astype(jnp.float32) / STEPS
    return SHIFT * fraction / (SHIFT * fraction + 1.0 - fraction)


def lane_frequencies():
    rows = np.zeros((3, HEAD), np.float32)
    lane = 0
    for component, axis_span in ((0, 16), (1, 56), (2, 56)):
        pair_ids = np.arange(axis_span // 2, dtype=np.float32)
        frequency = np.exp(-(2.0 * pair_ids / axis_span) * np.float32(math.log(10000.0)))
        rows[component, lane : lane + axis_span] = np.repeat(frequency, 2)
        lane += axis_span
    return rows


def seq_grid(count):
    columns = 2 ** ((count.bit_length() - 1) // 2)
    return count // columns, columns


def send_x(block, step):
    if step == 0:
        return block
    high, wide = seq_grid(lax.axis_size("seq"))
    route = [(y * wide + x, y * wide + (x + step) % wide) for y in range(high) for x in range(wide)]
    return lax.ppermute(block, "seq", route)


def send_y(block, step):
    if step == 0:
        return block
    high, wide = seq_grid(lax.axis_size("seq"))
    route = [(y * wide + x, (y + step) % high * wide + x) for y in range(high) for x in range(wide)]
    return lax.ppermute(block, "seq", route)


def send_seq(block, dy, dx):
    if dy == 0 and dx == 0:
        return block
    high, wide = seq_grid(lax.axis_size("seq"))
    route = [
        (y * wide + x, (y + dy) % high * wide + (x + dx) % wide)
        for y in range(high)
        for x in range(wide)
    ]
    return lax.ppermute(block, "seq", route)


def send_z(block, step):
    if step == 0:
        return block
    count = lax.axis_size("req")
    return lax.ppermute(block, "req", [(r, (r + step) % count) for r in range(count)])


def swap_core(block):
    return lax.ppermute(block, "cfg", [(0, 1), (1, 0)])


def take(array, start, size, axis):
    return lax.dynamic_slice_in_dim(array, start, size, axis)


def dot(left, right):
    return jnp.dot(left, right, preferred_element_type=jnp.float32)


def whole_spec():
    return pl.BlockSpec(memory_space=pltpu.VMEM)


def smem_spec():
    return pl.BlockSpec(memory_space=pltpu.SMEM)


def params(mib):
    return pltpu.CompilerParams(vmem_limit_bytes=mib * MIB)


def rotate_kernel(kv_ref, pos_ref, freq_ref, out_ref):
    rows, width = kv_ref.shape[1:]
    pos = pos_ref[...].astype(F32)
    angles = (
        pos[:, 0:1] * freq_ref[0:1, :]
        + pos[:, 1:2] * freq_ref[1:2, :]
        + pos[:, 2:3] * freq_ref[2:3, :]
    )
    cosine, sine = jnp.cos(angles), jnp.sin(angles)
    even = lax.broadcasted_iota(jnp.int32, (rows, HEAD), 1) % 2 == 0
    out_ref[...] = jnp.zeros_like(out_ref)
    for first in range(0, width, HEAD):
        keys = kv_ref[0, :, first : first + HEAD].astype(F32)
        after = pltpu.roll(keys, HEAD - 1, 1)
        before = pltpu.roll(keys, 1, 1)
        rotated = cosine * keys + sine * jnp.where(even, -after, before)
        out_ref[0, 0:rows, first : first + HEAD] = rotated.astype(BF16)
    out_ref[1, 0:rows, :] = kv_ref[1]


def rotate_fresh(fresh, positions, padded):
    width = fresh.shape[2]
    return pl.pallas_call(
        rotate_kernel,
        out_shape=jax.ShapeDtypeStruct((2, padded, width), BF16),
        in_specs=[whole_spec()] * 3,
        out_specs=whole_spec(),
        compiler_params=params(4),
    )(fresh, positions, jnp.asarray(lane_frequencies()))


def attention_kernel(q_ref, text_ref, image_ref, bias_ref, gathered_ref, out_ref, fresh_ref):
    pieces, _, padded, _ = gathered_ref.shape
    for i in range(pieces):
        fresh_ref[:, i * padded : (i + 1) * padded, :] = gathered_ref[i]
    slots = image_ref.shape[1]
    image_bias = bias_ref[:, 0:slots]
    fresh_bias = bias_ref[:, slots:]
    over_lanes = (((1,), (1,)), ((), ()))
    for first in range(0, q_ref.shape[1], HEAD):
        head = slice(first, first + HEAD)
        query = q_ref[:, head]

        def scores(keys):
            return lax.dot_general(query, keys, over_lanes, preferred_element_type=F32) * SCALE

        text = scores(text_ref[0, :, head])
        image = scores(image_ref[0, :, head]) + image_bias
        fresh = scores(fresh_ref[0, :, head]) + fresh_bias
        best = jnp.maximum(
            jnp.max(text, axis=1, keepdims=True),
            jnp.maximum(
                jnp.max(image, axis=1, keepdims=True), jnp.max(fresh, axis=1, keepdims=True)
            ),
        )
        text, image, fresh = jnp.exp(text - best), jnp.exp(image - best), jnp.exp(fresh - best)
        total = (
            jnp.sum(text, axis=1, keepdims=True)
            + jnp.sum(image, axis=1, keepdims=True)
            + jnp.sum(fresh, axis=1, keepdims=True)
        )
        mixed = (
            dot(text.astype(BF16), text_ref[1, :, head])
            + dot(image.astype(BF16), image_ref[1, :, head])
            + dot(fresh.astype(BF16), fresh_ref[1, :, head])
        )
        out_ref[0, :, head] = (mixed / total).astype(BF16)


def attention(query, text_kv, image_kv, bias, fresh):
    rows, width = query.shape
    group = 3 * HEAD
    groups = width // group
    text, slots = text_kv.shape[1], image_kv.shape[1]
    pieces, _, padded, _ = fresh.shape
    return pl.pallas_call(
        attention_kernel,
        grid=(groups,),
        out_shape=jax.ShapeDtypeStruct((groups, rows, group), BF16),
        in_specs=[
            pl.BlockSpec((rows, group), lambda g: (0, g)),
            pl.BlockSpec((2, text, group), lambda g: (0, 0, g)),
            pl.BlockSpec((2, slots, group), lambda g: (0, 0, g)),
            pl.BlockSpec(bias.shape, lambda g: (0, 0)),
            pl.BlockSpec((pieces, 2, padded, group), lambda g: (0, 0, 0, g)),
        ],
        out_specs=pl.BlockSpec((1, rows, group), lambda g: (g, 0, 0)),
        scratch_shapes=[pltpu.VMEM((2, padded * pieces, group), BF16)],
        compiler_params=params(10),
    )(query, text_kv, image_kv, bias, fresh)


def residual_kernel(requests, pieces, ids_ref, *refs):
    attended = refs[:requests]
    mine, other = refs[requests : requests + pieces], refs[requests + pieces : requests + 2 * pieces]
    stream_ref, gate_ref, out_ref, rows_ref = refs[requests + 2 * pieces :]
    row_count = attended[0].shape[1]
    for j in range(requests):
        first = pl.multiple_of(ids_ref[j] * row_count, 16)
        rows_ref[:, pl.ds(first, row_count), :] = attended[j][...]
    for half, weights in ((0, mine), (1, other)):
        total = None
        for k in range(pieces):
            term = dot(rows_ref[ids_ref[requests + k]], weights[k][...])
            total = term if total is None else total + term
        width = total.shape[1]
        total = total.reshape(requests, row_count, width)
        out_ref[half] = (
            stream_ref[half].astype(F32) + gate_ref[half][:, None, :] * total
        ).astype(BF16)


def residual_columns(ids, attended, mine, other, stream, gate):
    requests, pieces = len(attended), len(mine)
    segments, row_count, seg = attended[0].shape
    return pl.pallas_call(
        functools.partial(residual_kernel, requests, pieces),
        out_shape=jax.ShapeDtypeStruct(stream.shape, BF16),
        in_specs=[smem_spec()] + [whole_spec()] * (requests + 2 * pieces + 2),
        out_specs=whole_spec(),
        scratch_shapes=[pltpu.VMEM((segments, requests * row_count, seg), BF16)],
        compiler_params=params(14),
    )(ids, *attended, *mine, *other, stream, gate)


def up_kernel(wide, requests, pieces, per_piece, ids_ref, *refs):
    count = wide * requests
    blocks = refs[:count]
    mod_ref = refs[count]
    mine = refs[count + 1 : count + 1 + pieces]
    other = refs[count + 1 + pieces : count + 1 + 2 * pieces]
    out_ref, own_ref, rows_ref = refs[count + 1 + 2 * pieces :]
    half, col = pl.program_id(0), pl.program_id(1)
    row_count, seg = blocks[0].shape[2:]
    model = 2 * requests * seg
    core_at = 1 + wide + requests

    @pl.when((half == 0) & (col == 0))
    def _():
        for dx in range(wide):
            mine_x = blocks[dx * requests : (dx + 1) * requests]
            x_at = ids_ref[1 + dx]
            for q in range(requests):
                total = None
                for block in mine_x:
                    for h in range(2):
                        part = jnp.sum(block[h, q].astype(F32), axis=1, keepdims=True)
                        total = part if total is None else total + part
                average = total * (1.0 / model)
                total = None
                for block in mine_x:
                    for h in range(2):
                        centered = block[h, q].astype(F32) - average
                        part = jnp.sum(centered * centered, axis=1, keepdims=True)
                        total = part if total is None else total + part
                inverse = lax.rsqrt(total * (1.0 / model) + EPSILON)
                first = pl.multiple_of((q * wide + x_at) * row_count, 16)
                for dz, block in enumerate(mine_x):
                    place = ids_ref[1 + wide + dz]
                    for h in range(2):
                        centered = block[h, q].astype(F32) - average
                        scale = mod_ref[1, 2 * place + h, q : q + 1, :]
                        shift = mod_ref[0, 2 * place + h, q : q + 1, :]
                        column = 2 * place + (h ^ ids_ref[core_at])
                        lanes = pl.ds(0, seg)
                        if per_piece > 1:
                            lanes = pl.ds(pl.multiple_of(column % per_piece * seg, 128), seg)
                        rows_ref[column // per_piece, pl.ds(first, row_count), lanes] = (
                            centered * inverse * (1.0 + scale) + shift
                        ).astype(BF16)
            own = ids_ref[0]
            first = pl.multiple_of(x_at * row_count, 16)
            for dz, block in enumerate(mine_x):
                place = ids_ref[1 + wide + dz]
                for h in range(2):
                    own_ref[2 * place + h, pl.ds(first, row_count), :] = block[h, own]

    def product(weights):
        total = None
        for k in range(pieces):
            term = dot(rows_ref[ids_ref[core_at + 1 + k]], weights[k][...])
            total = term if total is None else total + term
        out_ref[0] = jax.nn.gelu(total, approximate=True).astype(BF16)

    pl.when(half == 0)(lambda: product(mine))
    pl.when(half == 1)(lambda: product(other))


def up_products(ids, blocks, mod, mine, other, wide):
    requests, pieces = len(blocks) // wide, len(mine)
    row_count, seg = blocks[0].shape[2:]
    depth, width = mine[0].shape
    per_piece = depth // seg
    rows = requests * wide * row_count
    step = 256 if width % 256 == 0 else width
    cols = width // step
    return pl.pallas_call(
        functools.partial(up_kernel, wide, requests, pieces, per_piece),
        grid=(2, cols),
        out_shape=(
            jax.ShapeDtypeStruct((2, rows, width), BF16),
            jax.ShapeDtypeStruct((2 * requests, wide * row_count, seg), BF16),
        ),
        in_specs=[smem_spec()]
        + [pl.BlockSpec(block.shape, lambda h, c: (0, 0, 0, 0)) for block in blocks]
        + [pl.BlockSpec(mod.shape, lambda h, c: (0, 0, 0, 0))]
        + [pl.BlockSpec((depth, step), lambda h, c: (0, c * (1 - h) + h * (cols - 1)))] * pieces
        + [pl.BlockSpec((depth, step), lambda h, c: (0, c * h))] * pieces,
        out_specs=(
            pl.BlockSpec((1, rows, step), lambda h, c: (h, 0, c)),
            pl.BlockSpec((2 * requests, wide * row_count, seg), lambda h, c: (0, 0, 0)),
        ),
        scratch_shapes=[pltpu.VMEM((2 * requests // per_piece, rows, depth), BF16)],
        compiler_params=params(28),
    )(ids, *blocks, mod, *mine, *other)


def down_kernel(requests, acts, weights, has_start, last, ids_ref, *refs):
    act_refs, refs = refs[:acts], refs[acts:]
    weight_refs, refs = refs[:weights], refs[weights:]
    if has_start:
        start_ref, refs = refs[0], refs[1:]
    out_refs = refs[: requests if last else 1]
    total_ref, order_ref = refs[-2:] if weights > 1 else (refs[-1], None)
    rows, depth = act_refs[0].shape[1:]

    if weights > 1:

        @pl.when(pl.program_id(0) == 0)
        def _():
            for k in range(acts):
                for h in range(2):
                    order_ref[ids_ref[2 + 2 * k + h]] = act_refs[k][h]

    total = start_ref[...] if has_start else None
    for k in range(2 * acts):
        if weights == 1:
            block = ids_ref[2 + k]
            first = pl.multiple_of(block * depth, 16)
            term = dot(act_refs[k // 2][k % 2], weight_refs[0][pl.ds(first, depth), :])
        else:
            part, row = divmod(k, acts)
            block = (ids_ref[1] ^ part) * acts + row
            term = dot(order_ref[block], weight_refs[part][row * depth : (row + 1) * depth, :])
        total = term if total is None else total + term
    if not last:
        out_refs[0][...] = total
        return
    total_ref[...] = total
    share = rows // requests
    for dz in range(requests):
        first = pl.multiple_of(lax.rem(ids_ref[0] + dz, requests) * share, 16)
        out_refs[dz][...] = total_ref[pl.ds(first, share), :].astype(BF16)


def down_products(ids, acts, weights, start, last, requests):
    rows, depth = acts[0].shape[1:]
    width = weights[0].shape[1]
    step = 256 if width % 256 == 0 else width
    steps = width // step
    specs = [smem_spec()]
    specs += [pl.BlockSpec(act.shape, lambda c: (0, 0, 0)) for act in acts]
    specs += [pl.BlockSpec((weight.shape[0], step), lambda c: (0, c)) for weight in weights]
    operands = [ids, *acts, *weights]
    if start is not None:
        specs.append(pl.BlockSpec((rows, step), lambda c: (0, c)))
        operands.append(start)
    if last:
        share = rows // requests
        outs = tuple(jax.ShapeDtypeStruct((share, width), BF16) for _ in range(requests))
        out_specs = tuple(pl.BlockSpec((share, step), lambda c: (0, c)) for _ in range(requests))
    else:
        outs = (jax.ShapeDtypeStruct((rows, width), F32),)
        out_specs = (pl.BlockSpec((rows, step), lambda c: (0, c)),)
    scratch = [pltpu.VMEM((rows, step), F32)]
    if len(weights) > 1:
        scratch.append(pltpu.VMEM((2 * len(acts), rows, depth), BF16))
    return pl.pallas_call(
        functools.partial(
            down_kernel, requests, len(acts), len(weights), start is not None, last
        ),
        grid=(steps,),
        out_shape=outs,
        in_specs=specs,
        out_specs=out_specs,
        scratch_shapes=scratch,
        compiler_params=params(28),
    )(*operands)


def per_device(
    queries,
    text_cache,
    image_cache,
    fresh_kv,
    fresh_slots,
    fresh_pos,
    image_len,
    stream,
    modulation,
    out_weight,
    up_weight,
    down_weight,
    final_weight,
    latent,
    step_index,
):
    cfg_id = lax.axis_index("cfg")
    req_id = lax.axis_index("req")
    seq_id = lax.axis_index("seq")
    requests = lax.axis_size("req")
    high, wide = seq_grid(lax.axis_size("seq"))
    y_id, x_id = seq_id // wide, seq_id % wide
    around = [(dy, dx) for dy in range(high) for dx in range(wide)]

    def x_from(step):
        return (x_id - step) % wide

    def y_from(step):
        return (y_id - step) % high

    def seq_from(dy, dx):
        return y_from(dy) * wide + x_from(dx)

    def ids(*values):
        return jnp.stack([jnp.asarray(value, jnp.int32) for value in values])

    fresh_count = fresh_kv.shape[3]
    padded = -(-fresh_count // 16) * 16
    fresh_pair = rotate_fresh(fresh_kv[0, 0], fresh_pos[:, 0, :].T, padded)
    fresh = lax.all_gather(fresh_pair, "seq", axis=0, tiled=False)

    out_rows, col_count = out_weight.shape
    seg = col_count // 2
    out_mine = take(out_weight, cfg_id * seg, seg, 1)
    out_other = [take(out_weight, (1 - cfg_id) * seg, seg, 1)]
    out_y = [send_y(out_mine, dy) for dy in range(high)]
    out_x = [send_x(out_mine, dx) for dx in range(wide)]

    up_rows, hidden = up_weight.shape
    hidden_x = hidden // wide
    hidden_half = hidden_x // 2
    up_x = []
    for dx in range(wide):
        first = (x_id + dx) % wide * hidden_x + cfg_id * hidden_half
        up_x.append(send_x(take(up_weight, first, hidden_half, 1), dx))
    up_y = [send_y(up_x[0], dy) for dy in range(high)]
    own_other = take(up_weight, x_id * hidden_x + (1 - cfg_id) * hidden_half, hidden_half, 1)

    out_y, fresh = lax.optimization_barrier((out_y, fresh))
    out_mine = [send_x(out_y[dy], dx) if dy else out_x[dx] for dy, dx in around]

    length = lax.dynamic_index_in_dim(image_len, req_id, 0, keepdims=False)
    image_kv = image_cache[0, 0]
    image_total = image_kv.shape[1]
    slot_ids = fresh_slots[0]
    key_ids = jnp.arange(image_total, dtype=jnp.int32)
    replaced = jnp.any(slot_ids[:, None] == key_ids[None, :], axis=0)
    kept = (key_ids < length) & ~replaced
    piece_slots = jnp.pad(
        slot_ids.reshape(-1, fresh_count),
        ((0, 0), (0, padded - fresh_count)),
        constant_values=image_total,
    )
    live = jnp.concatenate([kept, piece_slots.reshape(-1) < length])
    bias = jnp.where(live, 0.0, -jnp.inf).astype(F32)[None, :]
    attended = attention(queries[0, 0], text_cache[0, 0], image_kv, bias, fresh)
    row_count = queries.shape[2]
    if attended.shape[2] != out_rows:
        attended = jnp.transpose(attended, (1, 0, 2)).reshape(row_count, -1, out_rows)
        attended = jnp.transpose(attended, (1, 0, 2))
    attended_all = [send_z(attended, dz) for dz in range(requests)]
    out_mine, attended = lax.optimization_barrier((out_mine, attended))
    swapped = swap_core(jnp.concatenate(out_mine[1:], axis=0))
    out_other += [
        lax.slice_in_dim(swapped, k * out_rows, (k + 1) * out_rows, axis=0)
        for k in range(len(around) - 1)
    ]

    mod_half = lax.dynamic_index_in_dim(modulation, cfg_id, 0, keepdims=False)

    def halves_first(array, axis):
        shape = array.shape[:axis] + (-1, 2, seg) + array.shape[axis + 1 :]
        split = array.reshape(shape)
        return jnp.where(cfg_id == 0, split, jnp.flip(split, axis + 1))

    stream_halves = jnp.moveaxis(halves_first(stream[0], 2)[:, :, 0], 2, 0)
    gate_cols = take(mod_half[:, 0, :], req_id * col_count, col_count, 1)
    gate_halves = jnp.moveaxis(halves_first(gate_cols, 1)[:, 0], 1, 0)
    residual = residual_columns(
        ids(*[(req_id - dz) % requests for dz in range(requests)], *[seq_from(*d) for d in around]),
        attended_all,
        out_mine,
        out_other,
        stream_halves,
        gate_halves,
    )

    along_z = [send_z(residual, dz) for dz in range(requests)]
    near = [send_x(residual, dx) for dx in range(wide)]

    up_x[1:], _ = lax.optimization_barrier((up_x[1:], residual))
    up_mine = [send_y(up_x[dx], dy) if dx else up_y[dy] for dy, dx in around]

    down_cols = down_weight.shape[1]
    down_half = hidden // 2
    own_down = take(down_weight, cfg_id * down_half, down_half, 0)
    along_z, near, up_mine, own_down = lax.optimization_barrier(
        (along_z, near, up_mine, own_down)
    )
    down_mine = [send_y(own_down, dy) for dy in range(1, high)]
    blocks = [send_x(b, dx) if dz else near[dx] for dx in range(wide) for dz, b in enumerate(along_z)]
    up_other = [own_other] + [swap_core(part) for part in up_mine[1:]]
    mod_norm = jnp.stack([mod_half[:, 1], mod_half[:, 2]])
    mod_norm = jnp.moveaxis(halves_first(mod_norm, 2), 1, 3)
    mod_norm = mod_norm.reshape(2, 2 * requests, requests, seg)
    act_own, own_rows = up_products(
        ids(
            req_id,
            *[x_from(dx) for dx in range(wide)],
            *[(req_id - dz) % requests for dz in range(requests)],
            cfg_id,
            *[seq_from(*d) for d in around],
        ),
        blocks,
        mod_norm,
        up_mine,
        up_other,
        wide,
    )

    acts = [send_x(act_own, dx) for dx in range(wide)]

    def act_places(first, last):
        values = [2 * x_from(dx) + (h ^ cfg_id) for dx in range(first, last) for h in range(2)]
        return ids(req_id, cfg_id, *values)

    begun = down_products(act_places(0, 1), acts[:1], [down_weight], None, False, requests)[0]
    shares = [
        down_products(act_places(1, wide), acts[1:], [down_weight], begun, True, requests)
    ]
    down_mine, _ = lax.optimization_barrier((down_mine, shares[0]))
    down_other = [swap_core(part) for part in down_mine]
    for mine, other in zip(down_mine, down_other):
        shares.append(
            down_products(act_places(0, wide), acts, [mine, other], None, True, requests)
        )
    model = requests * col_count
    natural = own_rows.reshape(requests, 2, wide * row_count, seg)
    natural = jnp.where(cfg_id == 0, natural, jnp.flip(natural, 1))
    natural = jnp.moveaxis(natural.reshape(2 * requests, wide * row_count, seg), 0, 1)
    natural = natural.reshape(wide * row_count, model).astype(F32)
    gate_two = lax.dynamic_index_in_dim(mod_half[:, 3, :], req_id, 0, keepdims=False)

    def finished(share, col):
        total = share[0].astype(F32)
        for dz in range(1, requests):
            total += send_z(share[dz], dz).astype(F32)
        block_out = (
            take(natural, col, down_cols, 1) + take(gate_two, col, down_cols, 0)[None, :] * total
        ).astype(BF16)
        return dot(block_out, take(final_weight, col, down_cols, 0))

    velocity = 0.0
    for dy, share in enumerate(shares):
        velocity += finished(share, seq_from(dy, 0) * down_cols)

    channels = velocity.shape[1]
    velocity = velocity.reshape(wide, row_count // 2, 2, channels)
    cfg_count = lax.axis_size("cfg")
    halves = []
    for dc in range(2):
        share = 0.0
        for dx in range(wide):
            block = lax.dynamic_index_in_dim(velocity, (x_id + dx) % wide, 0, keepdims=False)
            block = lax.dynamic_index_in_dim(block, cfg_id ^ dc, 1, keepdims=False)
            if dc or dx:
                route = [
                    (
                        (c * high + y) * wide + x,
                        ((c ^ dc) * high + y) * wide + (x + dx) % wide,
                    )
                    for c in range(cfg_count)
                    for y in range(high)
                    for x in range(wide)
                ]
                block = lax.ppermute(block, ("cfg", "seq"), route)
            share += block
        halves.append(share)
    cond_part = jnp.where(cfg_id == 0, halves[0], halves[1])
    uncond_part = jnp.where(cfg_id == 0, halves[1], halves[0])
    guided = uncond_part + GUIDANCE * (cond_part - uncond_part)
    level_now = noise_level(step_index[0])
    level_next = noise_level(step_index[0] + 1)
    token_ids = (
        seq_id * row_count
        + 2 * jnp.arange(row_count // 2, dtype=jnp.int32)[:, None]
        + cfg_id
        + jnp.zeros((1, channels), jnp.int32)
    )
    valid = token_ids < length
    current = latent[0]
    latent_next = jnp.where(valid, current + (level_next - level_now) * guided, current)
    denoised = jnp.where(valid, current - level_now * guided, current)
    return (latent_next[None], denoised[None])


def solution(mesh):
    in_specs = (
        P("cfg", "req", "seq", None),
        P("cfg", "req", None, None, None),
        P("cfg", "req", None, None, None),
        P("cfg", "req", None, "seq", None),
        P("req", None),
        P(None, "req", "seq"),
        P(),
        P("cfg", None, "seq", "req"),
        P(),
        P("seq", "req"),
        P("seq", "req"),
        P("req", "seq"),
        P(),
        P("req", "seq", "cfg"),
        P(),
    )
    out_specs = (P("req", "seq", "cfg"), P("req", "seq", "cfg"))
    return jax.shard_map(
        per_device, mesh=mesh, in_specs=in_specs, out_specs=out_specs, check_vma=False
    )
```

```python
import functools
import math

import jax
import jax.numpy as jnp
import numpy as np
from jax import lax
from jax.experimental import pallas as pl
from jax.experimental.pallas import tpu as pltpu
from jax.sharding import PartitionSpec as P

STEPS = 28
GUIDANCE = 3.0
SHIFT = 3.0
SCALE = 1.0 / math.sqrt(128.0)
EPSILON = 1e-06
HEAD = 128
BF16 = jnp.bfloat16
F32 = jnp.float32
MIB = 1024 * 1024


def noise_level(index):
    fraction = 1.0 - index.astype(jnp.float32) / STEPS
    return SHIFT * fraction / (SHIFT * fraction + 1.0 - fraction)


def lane_frequencies():
    rows = np.zeros((3, HEAD), np.float32)
    lane = 0
    for component, axis_span in ((0, 16), (1, 56), (2, 56)):
        pair_ids = np.arange(axis_span // 2, dtype=np.float32)
        frequency = np.exp(-(2.0 * pair_ids / axis_span) * np.float32(math.log(10000.0)))
        rows[component, lane : lane + axis_span] = np.repeat(frequency, 2)
        lane += axis_span
    return rows


def seq_grid(count):
    columns = 2 ** ((count.bit_length() - 1) // 2)
    return count // columns, columns


def send_x(block, step):
    if step == 0:
        return block
    high, wide = seq_grid(lax.axis_size("seq"))
    route = [(y * wide + x, y * wide + (x + step) % wide) for y in range(high) for x in range(wide)]
    return lax.ppermute(block, "seq", route)


def send_y(block, step):
    if step == 0:
        return block
    high, wide = seq_grid(lax.axis_size("seq"))
    route = [(y * wide + x, (y + step) % high * wide + x) for y in range(high) for x in range(wide)]
    return lax.ppermute(block, "seq", route)


def send_seq(block, dy, dx):
    if dy == 0 and dx == 0:
        return block
    high, wide = seq_grid(lax.axis_size("seq"))
    route = [
        (y * wide + x, (y + dy) % high * wide + (x + dx) % wide)
        for y in range(high)
        for x in range(wide)
    ]
    return lax.ppermute(block, "seq", route)


def send_z(block, step):
    if step == 0:
        return block
    count = lax.axis_size("req")
    return lax.ppermute(block, "req", [(r, (r + step) % count) for r in range(count)])


def swap_core(block):
    return lax.ppermute(block, "cfg", [(0, 1), (1, 0)])


def gather_core(block):
    return lax.all_gather(block, "cfg", axis=0, tiled=False)


def take(array, start, size, axis):
    return lax.dynamic_slice_in_dim(array, start, size, axis)


def dot(left, right):
    return jnp.dot(left, right, preferred_element_type=jnp.float32)


def whole_spec():
    return pl.BlockSpec(memory_space=pltpu.VMEM)


def smem_spec():
    return pl.BlockSpec(memory_space=pltpu.SMEM)


def params():
    return pltpu.CompilerParams(vmem_limit_bytes=60 * MIB)


def rotate_kernel(kv_ref, pos_ref, freq_ref, out_ref):
    rows, width = kv_ref.shape[1:]
    row_ids = lax.broadcasted_iota(jnp.int32, (rows, HEAD), 0)
    angles = jnp.zeros((rows, HEAD), F32)
    for row in range(rows):
        line = (
            pos_ref[0, 0, row].astype(F32) * freq_ref[0:1, :]
            + pos_ref[1, 0, row].astype(F32) * freq_ref[1:2, :]
            + pos_ref[2, 0, row].astype(F32) * freq_ref[2:3, :]
        )
        angles = jnp.where(row_ids == row, line, angles)
    cosine, sine = jnp.cos(angles), jnp.sin(angles)
    even = lax.broadcasted_iota(jnp.int32, (rows, HEAD), 1) % 2 == 0
    out_ref[...] = jnp.zeros_like(out_ref)
    for first in range(0, width, HEAD):
        keys = kv_ref[0, :, first : first + HEAD].astype(F32)
        after = pltpu.roll(keys, HEAD - 1, 1)
        before = pltpu.roll(keys, 1, 1)
        rotated = cosine * keys + sine * jnp.where(even, -after, before)
        out_ref[0, 0:rows, first : first + HEAD] = rotated.astype(BF16)
    out_ref[1, 0:rows, :] = kv_ref[1]


def rotate_fresh(fresh, positions, padded):
    width = fresh.shape[2]
    return pl.pallas_call(
        rotate_kernel,
        out_shape=jax.ShapeDtypeStruct((2, padded, width), BF16),
        in_specs=[whole_spec(), smem_spec(), whole_spec()],
        out_specs=whole_spec(),
        compiler_params=params(),
    )(fresh, positions, jnp.asarray(lane_frequencies()))


def attention_kernel(pieces, ids_ref, slots_ref, q_ref, text_ref, image_ref, *refs):
    fresh_refs, (out_ref, fresh_ref) = refs[:pieces], refs[pieces:]
    padded = fresh_refs[0].shape[1]
    for i in range(pieces):
        fresh_ref[:, i * padded : (i + 1) * padded, :] = fresh_refs[i][...]
    slots = image_ref.shape[1]
    count = slots_ref.shape[1] // pieces
    length = ids_ref[0]
    key_ids = lax.broadcasted_iota(jnp.int32, (1, slots), 1)
    fresh_ids = lax.broadcasted_iota(jnp.int32, (1, pieces * padded), 1)
    image_bias = jnp.where(key_ids < length, 0.0, -jnp.inf)
    fresh_bias = jnp.full(fresh_ids.shape, -jnp.inf, F32)
    for i in range(pieces):
        for j in range(count):
            slot = slots_ref[0, ids_ref[1 + i] * count + j]
            image_bias = jnp.where(key_ids == slot, -jnp.inf, image_bias)
            here = (fresh_ids == i * padded + j) & (slot < length)
            fresh_bias = jnp.where(here, 0.0, fresh_bias)
    over_lanes = (((1,), (1,)), ((), ()))
    for first in range(0, q_ref.shape[1], HEAD):
        head = slice(first, first + HEAD)
        query = q_ref[:, head]

        def scores(keys):
            return lax.dot_general(query, keys, over_lanes, preferred_element_type=F32) * SCALE

        text = scores(text_ref[0, :, head])
        image = scores(image_ref[0, :, head]) + image_bias
        fresh = scores(fresh_ref[0, :, head]) + fresh_bias
        best = jnp.maximum(
            jnp.max(text, axis=1, keepdims=True),
            jnp.maximum(
                jnp.max(image, axis=1, keepdims=True), jnp.max(fresh, axis=1, keepdims=True)
            ),
        )
        text, image, fresh = jnp.exp(text - best), jnp.exp(image - best), jnp.exp(fresh - best)
        total = (
            jnp.sum(text, axis=1, keepdims=True)
            + jnp.sum(image, axis=1, keepdims=True)
            + jnp.sum(fresh, axis=1, keepdims=True)
        )
        mixed = (
            dot(text.astype(BF16), text_ref[1, :, head])
            + dot(image.astype(BF16), image_ref[1, :, head])
            + dot(fresh.astype(BF16), fresh_ref[1, :, head])
        )
        out_ref[0, :, head] = (mixed / total).astype(BF16)


def attention(ids, slot_ids, query, text_kv, image_kv, fresh):
    rows, width = query.shape
    group = 3 * HEAD
    groups = width // group
    text, slots = text_kv.shape[1], image_kv.shape[1]
    pieces, padded = len(fresh), fresh[0].shape[1]
    return pl.pallas_call(
        functools.partial(attention_kernel, pieces),
        grid=(groups,),
        out_shape=jax.ShapeDtypeStruct((groups, rows, group), BF16),
        in_specs=[
            smem_spec(),
            smem_spec(),
            pl.BlockSpec((rows, group), lambda g: (0, g)),
            pl.BlockSpec((2, text, group), lambda g: (0, 0, g)),
            pl.BlockSpec((2, slots, group), lambda g: (0, 0, g)),
        ]
        + [pl.BlockSpec((2, padded, group), lambda g: (0, 0, g))] * pieces,
        out_specs=pl.BlockSpec((1, rows, group), lambda g: (g, 0, 0)),
        scratch_shapes=[pltpu.VMEM((2, padded * pieces, group), BF16)],
        compiler_params=params(),
    )(ids, slot_ids, query, text_kv, image_kv, *fresh)


def residual_kernel(requests, pieces, ids_ref, *refs):
    attended, refs = refs[:requests], refs[requests:]
    own_ref, mine, refs = refs[0], refs[1:pieces], refs[pieces:]
    swapped_ref, stream_ref, mod_ref, out_ref, rows_ref = refs
    row_count = attended[0].shape[1]
    depth, width = own_ref.shape
    half_width = width // 2
    cfg, req = ids_ref[0], ids_ref[1]
    for j in range(requests):
        first = pl.multiple_of(ids_ref[2 + j] * row_count, 16)
        rows_ref[:, pl.ds(first, row_count), :] = attended[j][...]
    at = pl.multiple_of(req * width, 128)
    gates = [mod_ref[cfg, q, 0:1, pl.ds(at, width)] for q in range(requests)]

    def columns(core):
        for role, half in ((0, core), (1, 1 - core)):
            lanes = slice(half * half_width, (half + 1) * half_width)
            total = dot(rows_ref[ids_ref[2 + requests]], own_ref[:, lanes])
            for k in range(1, pieces):
                piece = swapped_ref[(k - 1) * depth : k * depth, :] if role else mine[k - 1][...]
                total += dot(rows_ref[ids_ref[2 + requests + k]], piece)
            for q in range(requests):
                out_ref[q, :, lanes] = (
                    stream_ref[0, q, :, lanes].astype(F32)
                    + gates[q][:, lanes] * total[q * row_count : (q + 1) * row_count]
                ).astype(BF16)

    pl.when(cfg == 0)(functools.partial(columns, 0))
    pl.when(cfg == 1)(functools.partial(columns, 1))


def residual_columns(ids, attended, own, mine, swapped, stream, modulation):
    requests, pieces = len(attended), len(mine) + 1
    segments, row_count, seg = attended[0].shape
    return pl.pallas_call(
        functools.partial(residual_kernel, requests, pieces),
        out_shape=jax.ShapeDtypeStruct(stream.shape[1:], BF16),
        in_specs=[smem_spec()] + [whole_spec()] * (requests + pieces + 3),
        out_specs=whole_spec(),
        scratch_shapes=[pltpu.VMEM((segments, requests * row_count, seg), BF16)],
        compiler_params=params(),
    )(ids, *attended, own, *mine, swapped, stream, modulation)


def up_kernel(requests, pieces, ids_ref, *refs):
    blocks, refs = refs[:requests], refs[requests:]
    mod_ref, own_weights, refs = refs[0], refs[1:3], refs[3:]
    weights, (out_ref, own_ref, rows_ref) = refs[: pieces - 1], refs[pieces - 1 :]
    row_count, width = blocks[0].shape[1:]
    depth = rows_ref.shape[2]
    cfg, req = ids_ref[0], ids_ref[1]
    scale_of_mean = 1.0 / (requests * width)

    @pl.when((pl.program_id(0) == 0) & (pl.program_id(1) == 0))
    def _():
        for q in range(requests):
            total = jnp.zeros((row_count, 1), F32)
            for block in blocks:
                total += jnp.sum(block[q].astype(F32), axis=1, keepdims=True)
            average = total * scale_of_mean
            total = jnp.zeros((row_count, 1), F32)
            for block in blocks:
                centered = block[q].astype(F32) - average
                total += jnp.sum(centered * centered, axis=1, keepdims=True)
            inverse = lax.rsqrt(total * scale_of_mean + EPSILON)
            for dz, block in enumerate(blocks):
                place = ids_ref[2 + dz]
                at = pl.ds(pl.multiple_of(place * width, 128), width)
                scale = 1.0 + mod_ref[cfg, q, 2:3, at]
                shift = mod_ref[cfg, q, 1:2, at]
                normed = (block[q].astype(F32) - average) * inverse * scale + shift
                normed = normed.astype(BF16)
                for i in range(width // depth):
                    rows_ref[
                        place * (width // depth) + i, q * row_count : (q + 1) * row_count, :
                    ] = normed[:, i * depth : (i + 1) * depth]
        for dz, block in enumerate(blocks):
            own_ref[ids_ref[2 + dz]] = block[req]

    def product(own_weight):
        total = dot(rows_ref[ids_ref[2 + requests]], own_weight[...])
        for k in range(1, pieces):
            total += dot(rows_ref[ids_ref[2 + requests + k]], weights[k - 1][...])
        out_ref[...] = jax.nn.gelu(total, approximate=True).astype(BF16)

    for h in range(2):
        pl.when(pl.program_id(0) == h)(functools.partial(product, own_weights[h]))


def up_products(ids, blocks, modulation, own_weights, weights):
    requests, pieces = len(blocks), len(weights) + 1
    row_count, slice_width = blocks[0].shape[1:]
    depth, width = own_weights[0].shape
    rows = requests * row_count
    step = 256 if width % 256 == 0 else width
    cols = width // step
    return pl.pallas_call(
        functools.partial(up_kernel, requests, pieces),
        grid=(2, cols),
        out_shape=(
            jax.ShapeDtypeStruct((2, rows, width), BF16),
            jax.ShapeDtypeStruct((requests, row_count, slice_width), BF16),
        ),
        in_specs=[smem_spec()]
        + [pl.BlockSpec(block.shape, lambda h, c: (0, 0, 0)) for block in blocks]
        + [pl.BlockSpec(modulation.shape, lambda h, c: (0, 0, 0, 0))]
        + [pl.BlockSpec((depth, step), lambda h, c: (0, c * (1 - h) + h * (cols - 1)))]
        + [pl.BlockSpec((depth, step), lambda h, c: (0, c * h))]
        + [pl.BlockSpec((None, depth, step), lambda h, c: (h, 0, c))] * (pieces - 1),
        out_specs=(
            pl.BlockSpec((None, rows, step), lambda h, c: (h, 0, c)),
            pl.BlockSpec((requests, row_count, slice_width), lambda h, c: (0, 0, 0)),
        ),
        scratch_shapes=[pltpu.VMEM((requests * slice_width // depth, rows, depth), BF16)],
        compiler_params=params(),
    )(ids, *blocks, modulation, *own_weights, *weights)


def down_kernel(requests, wide, weights, ids_ref, *refs):
    act_refs, refs = refs[: wide * wide], refs[wide * wide :]
    weight_refs, out_refs = refs[:weights], refs[weights : weights + requests]
    total_ref, order_ref = refs[weights + requests :]
    rows, depth = act_refs[0].shape[1:]
    row_count = rows // requests
    cfg, req = ids_ref[0], ids_ref[1]

    @pl.when(pl.program_id(0) == 0)
    def _():
        for k, act in enumerate(act_refs):
            first = pl.multiple_of(ids_ref[2 + 2 * k] * rows, 16)
            for h in range(2):
                order_ref[2 * ids_ref[3 + 2 * k] + h, pl.ds(first, rows), :] = act[h]

    total = None
    share = 2 * wide // weights
    for w in range(weights):
        for i in range(share):
            block = (cfg ^ w) * share + i if weights > 1 else i
            term = dot(order_ref[block], weight_refs[w][i * depth : (i + 1) * depth, :])
            total = term if total is None else total + term
    total_ref[...] = total
    for dz in range(requests):
        place = lax.rem(req + dz, requests)
        for x in range(wide):
            first = pl.multiple_of((x * requests + place) * row_count, 16)
            out_refs[dz][x] = total_ref[pl.ds(first, row_count), :].astype(BF16)


def down_products(ids, acts, weights, requests):
    rows, depth = acts[0].shape[1:]
    wide = math.isqrt(len(acts))
    width = weights[0].shape[1]
    step = 256 if width % 256 == 0 else width
    shape = (wide, rows // requests, width)
    out_block = (wide, rows // requests, step)
    return pl.pallas_call(
        functools.partial(down_kernel, requests, wide, len(weights)),
        grid=(width // step,),
        out_shape=tuple(jax.ShapeDtypeStruct(shape, BF16) for _ in range(requests)),
        in_specs=[smem_spec()]
        + [pl.BlockSpec(act.shape, lambda c: (0, 0, 0)) for act in acts]
        + [pl.BlockSpec((weight.shape[0], step), lambda c: (0, c)) for weight in weights],
        out_specs=tuple(pl.BlockSpec(out_block, lambda c: (0, 0, c)) for _ in range(requests)),
        scratch_shapes=[
            pltpu.VMEM((wide * rows, step), F32),
            pltpu.VMEM((2 * wide, wide * rows, depth), BF16),
        ],
        compiler_params=params(),
    )(ids, *acts, *weights)


def per_device(
    queries,
    text_cache,
    image_cache,
    fresh_kv,
    fresh_slots,
    fresh_pos,
    image_len,
    stream,
    modulation,
    out_weight,
    up_weight,
    down_weight,
    final_weight,
    latent,
    step_index,
):
    cfg_id = lax.axis_index("cfg")
    req_id = lax.axis_index("req")
    seq_id = lax.axis_index("seq")
    requests = lax.axis_size("req")
    high, wide = seq_grid(lax.axis_size("seq"))
    y_id, x_id = seq_id // wide, seq_id % wide
    around = [(dy, dx) for dy in range(high) for dx in range(wide)]

    def x_from(step):
        return (x_id - step) % wide

    def y_from(step):
        return (y_id - step) % high

    def seq_from(dy, dx):
        return y_from(dy) * wide + x_from(dx)

    def ids(*values):
        return jnp.stack([jnp.asarray(value, jnp.int32) for value in values])

    fresh_count = fresh_kv.shape[3]
    padded = -(-fresh_count // 16) * 16
    fresh_pair = rotate_fresh(fresh_kv[0, 0], fresh_pos, padded)
    fresh = [send_seq(fresh_pair, dy, dx) for dy, dx in around]

    out_rows, col_count = out_weight.shape
    seg = col_count // 2
    own_out, _ = lax.optimization_barrier((out_weight, fresh_pair))
    own_out = take(own_out, cfg_id * seg, seg, 1)
    out_y = [send_y(own_out, dy) for dy in range(high)]
    out_x = [send_x(own_out, dx) for dx in range(wide)]

    up_rows, hidden = up_weight.shape
    hidden_x = hidden // wide
    hidden_half = hidden_x // 2
    early_up, _ = lax.optimization_barrier((up_weight, fresh_pair))
    to_x = []
    for dx in range(wide):
        first = (x_id + dx) % wide * hidden_x + cfg_id * hidden_half
        to_x.append(take(early_up, first, hidden_half, 1))
    to_x, out_y, fresh = lax.optimization_barrier((to_x, out_y, fresh))
    up_x = [send_x(part, dx) for dx, part in enumerate(to_x)]
    up_y = [send_y(up_x[0], dy) for dy in range(high)]
    out_mine = [send_x(out_y[dy], dx) if dy else out_x[dx] for dy, dx in around]

    length = lax.dynamic_index_in_dim(image_len, req_id, 0, keepdims=False)
    attended = attention(
        ids(length, *[seq_from(*d) for d in around]),
        fresh_slots,
        queries[0, 0],
        text_cache[0, 0],
        image_cache[0, 0],
        fresh,
    )
    row_count = queries.shape[2]
    if attended.shape[2] != out_rows:
        attended = jnp.transpose(attended, (1, 0, 2)).reshape(row_count, -1, out_rows)
        attended = jnp.transpose(attended, (1, 0, 2))
    attended_all = [send_z(attended, dz) for dz in range(requests)]
    out_mine, attended, late_up = lax.optimization_barrier((out_mine, attended, up_weight))
    swapped = swap_core(jnp.concatenate(out_mine[1:], axis=0))
    own_up = [
        take(late_up, x_id * hidden_x + h * hidden_half, hidden_half, 1) for h in range(2)
    ]

    from_z = [(req_id - dz) % requests for dz in range(requests)]
    residual = residual_columns(
        ids(cfg_id, req_id, *from_z, *[seq_from(*d) for d in around]),
        attended_all,
        out_weight,
        out_mine[1:],
        swapped,
        stream,
        modulation,
    )
    along_z = [send_z(residual, dz) for dz in range(requests)]
    near = [send_x(residual, dx) for dx in range(wide)]

    up_x[1:], _ = lax.optimization_barrier((up_x[1:], residual))
    up_mine = [send_y(up_x[dx], dy) if dx else up_y[dy] for dy, dx in around]

    along_x = [gather_core(part) for part in up_x[1:]]

    down_cols = down_weight.shape[1]
    down_half = hidden // 2
    own_down = take(down_weight, cfg_id * down_half, down_half, 0)
    along_z, near, along_x, up_mine, own_down = lax.optimization_barrier(
        (along_z, near, along_x, up_mine, own_down)
    )
    blocks = [
        [send_x(block, dx) if dz else near[dx] for dz, block in enumerate(along_z)]
        for dx in range(wide)
    ]
    down_mine = [send_y(own_down, dy) for dy in range(1, high)]
    up_all = [
        gather_core(part) if dy else along_x[dx - 1]
        for part, (dy, dx) in zip(up_mine[1:], around[1:])
    ]

    up_ids = ids(cfg_id, req_id, *from_z, *[seq_from(*d) for d in around])
    acts, own_rows, act_ids = [], [], [cfg_id, req_id]
    for dx in range(wide):
        if acts:
            blocks[dx], acts[0] = lax.optimization_barrier((blocks[dx], acts[0]))
        act, own = up_products(up_ids, blocks[dx], modulation, own_up, up_all)
        own_rows.append(own)
        for step in range(wide):
            acts.append(send_x(act, step))
            act_ids += [x_from(dx + step), x_from(step)]

    shares = [down_products(ids(*act_ids), acts, [down_weight], requests)]
    down_mine, _ = lax.optimization_barrier((down_mine, shares[0]))
    for mine in down_mine:
        shares.append(down_products(ids(*act_ids), acts, [mine, swap_core(mine)], requests))

    model = requests * col_count
    natural = jnp.zeros((wide, row_count, model), F32)
    for dx, own in enumerate(own_rows):
        own = jnp.moveaxis(own, 0, 1).reshape(1, row_count, model).astype(F32)
        natural = lax.dynamic_update_slice_in_dim(natural, own, x_from(dx), 0)
    natural = natural.reshape(wide * row_count, model)
    mod_half = lax.dynamic_index_in_dim(modulation, cfg_id, 0, keepdims=False)
    gate_two = lax.dynamic_index_in_dim(mod_half[:, 3, :], req_id, 0, keepdims=False)

    def finished(share, col):
        total = share[0].astype(F32)
        for dz in range(1, requests):
            total += send_z(share[dz], dz).astype(F32)
        total = total.reshape(wide * row_count, down_cols)
        block_out = (
            take(natural, col, down_cols, 1) + take(gate_two, col, down_cols, 0)[None, :] * total
        ).astype(BF16)
        return dot(block_out, take(final_weight, col, down_cols, 0))

    velocity = 0.0
    for dy, share in enumerate(shares):
        velocity += finished(share, seq_from(dy, 0) * down_cols)

    channels = velocity.shape[1]
    velocity = velocity.reshape(wide, row_count // 2, 2, channels)
    cfg_count = lax.axis_size("cfg")
    halves = []
    for dc in range(2):
        share = 0.0
        for dx in range(wide):
            block = lax.dynamic_index_in_dim(velocity, (x_id + dx) % wide, 0, keepdims=False)
            block = lax.dynamic_index_in_dim(block, cfg_id ^ dc, 1, keepdims=False)
            if dc or dx:
                route = [
                    (
                        (c * high + y) * wide + x,
                        ((c ^ dc) * high + y) * wide + (x + dx) % wide,
                    )
                    for c in range(cfg_count)
                    for y in range(high)
                    for x in range(wide)
                ]
                block = lax.ppermute(block, ("cfg", "seq"), route)
            share += block
        halves.append(share)
    cond_part = jnp.where(cfg_id == 0, halves[0], halves[1])
    uncond_part = jnp.where(cfg_id == 0, halves[1], halves[0])
    guided = uncond_part + GUIDANCE * (cond_part - uncond_part)
    level_now = noise_level(step_index[0])
    level_next = noise_level(step_index[0] + 1)
    token_ids = (
        seq_id * row_count
        + 2 * jnp.arange(row_count // 2, dtype=jnp.int32)[:, None]
        + cfg_id
        + jnp.zeros((1, channels), jnp.int32)
    )
    valid = token_ids < length
    current = latent[0]
    latent_next = jnp.where(valid, current + (level_next - level_now) * guided, current)
    denoised = jnp.where(valid, current - level_now * guided, current)
    return (latent_next[None], denoised[None])


def solution(mesh):
    in_specs = (
        P("cfg", "req", "seq", None),
        P("cfg", "req", None, None, None),
        P("cfg", "req", None, None, None),
        P("cfg", "req", None, "seq", None),
        P("req", None),
        P(None, "req", "seq"),
        P(),
        P("cfg", None, "seq", "req"),
        P(),
        P("seq", "req"),
        P("seq", "req"),
        P("req", "seq"),
        P(),
        P("req", "seq", "cfg"),
        P(),
    )
    out_specs = (P("req", "seq", "cfg"), P("req", "seq", "cfg"))
    return jax.shard_map(
        per_device, mesh=mesh, in_specs=in_specs, out_specs=out_specs, check_vma=False
    )
```

```python
import functools
import math

import jax
import jax.numpy as jnp
import numpy as np
from jax import lax
from jax.experimental import pallas as pl
from jax.experimental.pallas import tpu as pltpu
from jax.sharding import PartitionSpec as P

STEPS = 28
GUIDANCE = 3.0
SHIFT = 3.0
SCALE = 1.0 / math.sqrt(128.0)
EPSILON = 1e-06
HEAD = 128
BF16 = jnp.bfloat16
F32 = jnp.float32
MIB = 1024 * 1024


def noise_level(index):
    fraction = 1.0 - index.astype(jnp.float32) / STEPS
    return SHIFT * fraction / (SHIFT * fraction + 1.0 - fraction)


def lane_frequencies():
    rows = np.zeros((3, HEAD), np.float32)
    lane = 0
    for component, axis_span in ((0, 16), (1, 56), (2, 56)):
        pair_ids = np.arange(axis_span // 2, dtype=np.float32)
        frequency = np.exp(-(2.0 * pair_ids / axis_span) * np.float32(math.log(10000.0)))
        rows[component, lane : lane + axis_span] = np.repeat(frequency, 2)
        lane += axis_span
    return rows


def seq_grid(count):
    columns = 2 ** ((count.bit_length() - 1) // 2)
    return count // columns, columns


def send_x(block, step):
    if step == 0:
        return block
    high, wide = seq_grid(lax.axis_size("seq"))
    route = [(y * wide + x, y * wide + (x + step) % wide) for y in range(high) for x in range(wide)]
    return lax.ppermute(block, "seq", route)


def send_y(block, step):
    if step == 0:
        return block
    high, wide = seq_grid(lax.axis_size("seq"))
    route = [(y * wide + x, (y + step) % high * wide + x) for y in range(high) for x in range(wide)]
    return lax.ppermute(block, "seq", route)


def send_seq(block, dy, dx):
    if dy == 0 and dx == 0:
        return block
    high, wide = seq_grid(lax.axis_size("seq"))
    route = [
        (y * wide + x, (y + dy) % high * wide + (x + dx) % wide)
        for y in range(high)
        for x in range(wide)
    ]
    return lax.ppermute(block, "seq", route)


def send_z(block, step):
    if step == 0:
        return block
    count = lax.axis_size("req")
    return lax.ppermute(block, "req", [(r, (r + step) % count) for r in range(count)])


def swap_core(block):
    return lax.ppermute(block, "cfg", [(0, 1), (1, 0)])


def gather_core(block):
    return lax.all_gather(block, "cfg", axis=0, tiled=False)


def take(array, start, size, axis):
    return lax.dynamic_slice_in_dim(array, start, size, axis)


def dot(left, right):
    return jnp.dot(left, right, preferred_element_type=jnp.float32)


def hbm_spec():
    return pl.BlockSpec(memory_space=pl.ANY)


def place_of(step_x, step_y=0):
    high, wide = seq_grid(lax.axis_size("seq"))
    seq = lax.axis_index("seq")
    return lax.rem(seq // wide + high - step_y, high) * wide + x_of(step_x)


def x_of(step):
    wide = seq_grid(lax.axis_size("seq"))[1]
    return lax.rem(lax.axis_index("seq") % wide + 2 * wide - step, wide)


def z_of(step):
    count = lax.axis_size("req")
    return lax.rem(lax.axis_index("req") + count - step, count)


def whole_spec():
    return pl.BlockSpec(memory_space=pltpu.VMEM)


def smem_spec():
    return pl.BlockSpec(memory_space=pltpu.SMEM)


def params():
    return pltpu.CompilerParams(vmem_limit_bytes=60 * MIB)


def rotate_kernel(kv_ref, pos_ref, freq_ref, out_ref):
    rows, width = kv_ref.shape[1:]
    row_ids = lax.broadcasted_iota(jnp.int32, (rows, HEAD), 0)
    angles = jnp.zeros((rows, HEAD), F32)
    for row in range(rows):
        line = (
            pos_ref[0, 0, row].astype(F32) * freq_ref[0:1, :]
            + pos_ref[1, 0, row].astype(F32) * freq_ref[1:2, :]
            + pos_ref[2, 0, row].astype(F32) * freq_ref[2:3, :]
        )
        angles = jnp.where(row_ids == row, line, angles)
    cosine, sine = jnp.cos(angles), jnp.sin(angles)
    even = lax.broadcasted_iota(jnp.int32, (rows, HEAD), 1) % 2 == 0
    out_ref[...] = jnp.zeros_like(out_ref)
    for first in range(0, width, HEAD):
        keys = kv_ref[0, :, first : first + HEAD].astype(F32)
        after = pltpu.roll(keys, HEAD - 1, 1)
        before = pltpu.roll(keys, 1, 1)
        rotated = cosine * keys + sine * jnp.where(even, -after, before)
        out_ref[0, 0:rows, first : first + HEAD] = rotated.astype(BF16)
    out_ref[1, 0:rows, :] = kv_ref[1]


def rotate_fresh(fresh, positions, padded):
    width = fresh.shape[2]
    return pl.pallas_call(
        rotate_kernel,
        out_shape=jax.ShapeDtypeStruct((2, padded, width), BF16),
        in_specs=[whole_spec(), smem_spec(), whole_spec()],
        out_specs=whole_spec(),
        compiler_params=params(),
    )(fresh, positions, jnp.asarray(lane_frequencies()))


def attention_kernel(around, lengths_ref, slots_ref, q_ref, text_ref, image_ref, *refs):
    pieces = len(around)
    fresh_refs, (out_ref, fresh_ref) = refs[:pieces], refs[pieces:]
    padded = fresh_refs[0].shape[1]
    for i in range(pieces):
        fresh_ref[:, i * padded : (i + 1) * padded, :] = fresh_refs[i][...]
    slots = image_ref.shape[1]
    count = slots_ref.shape[1] // pieces
    length = lengths_ref[lax.axis_index("req")]
    key_ids = lax.broadcasted_iota(jnp.int32, (1, slots), 1)
    fresh_ids = lax.broadcasted_iota(jnp.int32, (1, pieces * padded), 1)
    image_bias = jnp.where(key_ids < length, 0.0, -jnp.inf)
    fresh_bias = jnp.full(fresh_ids.shape, -jnp.inf, F32)
    for i, (dy, dx) in enumerate(around):
        first = place_of(dx, dy) * count
        for j in range(count):
            slot = slots_ref[0, first + j]
            image_bias = jnp.where(key_ids == slot, -jnp.inf, image_bias)
            here = (fresh_ids == i * padded + j) & (slot < length)
            fresh_bias = jnp.where(here, 0.0, fresh_bias)
    over_lanes = (((1,), (1,)), ((), ()))
    for first in range(0, q_ref.shape[1], HEAD):
        head = slice(first, first + HEAD)
        query = q_ref[:, head]

        def scores(keys):
            return lax.dot_general(query, keys, over_lanes, preferred_element_type=F32) * SCALE

        text = scores(text_ref[0, :, head])
        image = scores(image_ref[0, :, head]) + image_bias
        fresh = scores(fresh_ref[0, :, head]) + fresh_bias
        best = jnp.maximum(
            jnp.max(text, axis=1, keepdims=True),
            jnp.maximum(
                jnp.max(image, axis=1, keepdims=True), jnp.max(fresh, axis=1, keepdims=True)
            ),
        )
        text, image, fresh = jnp.exp(text - best), jnp.exp(image - best), jnp.exp(fresh - best)
        total = (
            jnp.sum(text, axis=1, keepdims=True)
            + jnp.sum(image, axis=1, keepdims=True)
            + jnp.sum(fresh, axis=1, keepdims=True)
        )
        mixed = (
            dot(text.astype(BF16), text_ref[1, :, head])
            + dot(image.astype(BF16), image_ref[1, :, head])
            + dot(fresh.astype(BF16), fresh_ref[1, :, head])
        )
        out_ref[0, :, head] = (mixed / total).astype(BF16)


def attention(around, lengths, slot_ids, query, text_kv, image_kv, fresh):
    rows, width = query.shape
    group = 3 * HEAD
    groups = width // group
    text, slots = text_kv.shape[1], image_kv.shape[1]
    pieces, padded = len(fresh), fresh[0].shape[1]
    return pl.pallas_call(
        functools.partial(attention_kernel, around),
        grid=(groups,),
        out_shape=jax.ShapeDtypeStruct((groups, rows, group), BF16),
        in_specs=[
            smem_spec(),
            smem_spec(),
            pl.BlockSpec((rows, group), lambda g: (0, g)),
            pl.BlockSpec((2, text, group), lambda g: (0, 0, g)),
            pl.BlockSpec((2, slots, group), lambda g: (0, 0, g)),
        ]
        + [pl.BlockSpec((2, padded, group), lambda g: (0, 0, g))] * pieces,
        out_specs=pl.BlockSpec((1, rows, group), lambda g: (g, 0, 0)),
        scratch_shapes=[pltpu.VMEM((2, padded * pieces, group), BF16)],
        compiler_params=params(),
    )(lengths, slot_ids, query, text_kv, image_kv, *fresh)


def residual_kernel(requests, around, *refs):
    pieces = len(around)
    attended, refs = refs[:requests], refs[requests:]
    own_ref, mine, refs = refs[0], refs[1:pieces], refs[pieces:]
    swapped_ref, stream_ref, mod_ref, out_ref, rows_ref = refs
    row_count = attended[0].shape[1]
    depth, width = own_ref.shape
    half_width = width // 2
    cfg, req = lax.axis_index("cfg"), lax.axis_index("req")
    places = [place_of(dx, dy) for dy, dx in around]
    for j in range(requests):
        first = pl.multiple_of(z_of(j) * row_count, 16)
        rows_ref[:, pl.ds(first, row_count), :] = attended[j][...]
    at = pl.multiple_of(req * width, 128)
    gates = [mod_ref[cfg, q, 0:1, pl.ds(at, width)] for q in range(requests)]

    def columns(core):
        for role, half in ((0, core), (1, 1 - core)):
            lanes = slice(half * half_width, (half + 1) * half_width)
            total = dot(rows_ref[places[0]], own_ref[:, lanes])
            for k in range(1, pieces):
                piece = swapped_ref[(k - 1) * depth : k * depth, :] if role else mine[k - 1][...]
                total += dot(rows_ref[places[k]], piece)
            for q in range(requests):
                out_ref[q, :, lanes] = (
                    stream_ref[0, q, :, lanes].astype(F32)
                    + gates[q][:, lanes] * total[q * row_count : (q + 1) * row_count]
                ).astype(BF16)

    pl.when(cfg == 0)(functools.partial(columns, 0))
    pl.when(cfg == 1)(functools.partial(columns, 1))


def residual_columns(around, attended, own, mine, swapped, stream, modulation):
    requests, pieces = len(attended), len(mine) + 1
    segments, row_count, seg = attended[0].shape
    return pl.pallas_call(
        functools.partial(residual_kernel, requests, around),
        out_shape=jax.ShapeDtypeStruct(stream.shape[1:], BF16),
        in_specs=[whole_spec()] * (requests + pieces + 3),
        out_specs=whole_spec(),
        scratch_shapes=[pltpu.VMEM((segments, requests * row_count, seg), BF16)],
        compiler_params=params(),
    )(*attended, own, *mine, swapped, stream, modulation)


def copies_of(pieces, buffer, sems):
    cfg = lax.axis_index("cfg")
    copies = []
    for k, (kind, parts) in enumerate(pieces):
        for h in range(2):
            source, slot = parts[0].at[h] if kind == "stack" else parts[h], h
            if kind == "core":
                slot = cfg if h == 0 else 1 - cfg
            copies.append(
                (h, pltpu.make_async_copy(source, buffer.at[slot, k], sems.at[slot, k]))
            )
    return [copy for h in range(2) for half, copy in copies if half == h]


def up_kernel(requests, around, kinds, *refs):
    blocks, refs = refs[:requests], refs[requests:]
    mod_ref, refs = refs[0], refs[1:]
    pieces = []
    for kind in kinds:
        count = 1 if kind == "stack" else 2
        pieces.append((kind, refs[:count]))
        refs = refs[count:]
    out_ref, own_ref, rows_ref, buffer, sems = refs
    row_count, width = blocks[0].shape[1:]
    depth, hidden = buffer.shape[2:]
    cfg, req = lax.axis_index("cfg"), lax.axis_index("req")
    scale_of_mean = 1.0 / (requests * width)
    for copy in copies_of(pieces, buffer, sems):
        copy.start()
    for q in range(requests):
        total = jnp.zeros((row_count, 1), F32)
        for block in blocks:
            total += jnp.sum(block[q].astype(F32), axis=1, keepdims=True)
        average = total * scale_of_mean
        total = jnp.zeros((row_count, 1), F32)
        for block in blocks:
            centered = block[q].astype(F32) - average
            total += jnp.sum(centered * centered, axis=1, keepdims=True)
        inverse = lax.rsqrt(total * scale_of_mean + EPSILON)
        for dz, block in enumerate(blocks):
            place = z_of(dz)
            at = pl.ds(pl.multiple_of(place * width, 128), width)
            scale = 1.0 + mod_ref[cfg, q, 2:3, at]
            shift = mod_ref[cfg, q, 1:2, at]
            normed = (block[q].astype(F32) - average) * inverse * scale + shift
            normed = normed.astype(BF16)
            for i in range(width // depth):
                rows_ref[
                    place * (width // depth) + i, q * row_count : (q + 1) * row_count, :
                ] = normed[:, i * depth : (i + 1) * depth]
    for dz, block in enumerate(blocks):
        at = pl.ds(pl.multiple_of(z_of(dz) * width, 128), width)
        own_ref[:, at] = block[req]
    step = 256 if hidden % 256 == 0 else hidden
    for h in range(2):
        for c in range(hidden // step):
            total = None
            for k, (dy, dx) in enumerate(around):
                if c == 0:
                    source = pieces[k][1][0]
                    source = source.at[h] if pieces[k][0] == "stack" else source
                    pltpu.make_async_copy(source, buffer.at[h, k], sems.at[h, k]).wait()
                weight = buffer[h, k, :, c * step : (c + 1) * step]
                term = dot(rows_ref[place_of(dx, dy)], weight)
                total = term if total is None else total + term
            out_ref[h, :, c * step : (c + 1) * step] = jax.nn.gelu(
                total, approximate=True
            ).astype(BF16)


def up_products(around, blocks, modulation, pieces):
    requests = len(blocks)
    row_count, slice_width = blocks[0].shape[1:]
    model = requests * slice_width
    depth, hidden = pieces[0][1][0].shape[-2:]
    rows = requests * row_count
    operands = [part for _, parts in pieces for part in parts]
    return pl.pallas_call(
        functools.partial(up_kernel, requests, around, [kind for kind, _ in pieces]),
        out_shape=(
            jax.ShapeDtypeStruct((2, rows, hidden), BF16),
            jax.ShapeDtypeStruct((row_count, model), BF16),
        ),
        in_specs=[whole_spec()] * (requests + 1) + [hbm_spec()] * len(operands),
        out_specs=(whole_spec(), whole_spec()),
        scratch_shapes=[
            pltpu.VMEM((model // depth, rows, depth), BF16),
            pltpu.VMEM((2, len(pieces), depth, hidden), BF16),
            pltpu.SemaphoreType.DMA((2, len(pieces))),
        ],
        compiler_params=params(),
    )(*blocks, modulation, *operands)


def down_kernel(requests, wide, weights, *refs):
    acts, refs = refs[: wide * wide], refs[wide * wide :]
    weight_refs, out_refs = refs[:weights], refs[weights : weights + requests]
    total_ref, buffer, sems = refs[weights + requests :]
    rows, depth = acts[0].shape[1:]
    row_count = rows // requests
    width = buffer.shape[2]
    cfg = lax.axis_index("cfg")
    share = 2 * wide // weights
    for w, weight in enumerate(weight_refs):
        for i in range(share):
            slot = (cfg if w == 0 else 1 - cfg) * share + i if weights > 1 else i
            source = weight.at[pl.ds(i * depth, depth), :]
            pltpu.make_async_copy(source, buffer.at[slot], sems.at[slot]).start()
    for slot in range(2 * wide):
        source = weight_refs[0].at[pl.ds(0, depth), :]
        pltpu.make_async_copy(source, buffer.at[slot], sems.at[slot]).wait()
    step = 256 if width % 256 == 0 else width
    for c in range(width // step):
        lanes = slice(c * step, (c + 1) * step)
        for e in range(wide):
            total = None
            for dx in range(wide):
                far = (e - dx) % wide
                for h in range(2):
                    weight = buffer[2 * x_of(far) + h, :, lanes]
                    term = dot(acts[dx * wide + far][h], weight)
                    total = term if total is None else total + term
            total_ref[x_of(e)] = total
        for dz in range(requests):
            first = pl.multiple_of(z_of(requests - dz) * row_count, 16)
            for x in range(wide):
                out_refs[dz][x, :, lanes] = total_ref[x, pl.ds(first, row_count), :].astype(BF16)


def down_products(acts, weights, requests):
    rows, depth = acts[0].shape[1:]
    wide = math.isqrt(len(acts))
    width = weights[0].shape[1]
    step = 256 if width % 256 == 0 else width
    shape = (wide, rows // requests, width)
    return pl.pallas_call(
        functools.partial(down_kernel, requests, wide, len(weights)),
        out_shape=tuple(jax.ShapeDtypeStruct(shape, BF16) for _ in range(requests)),
        in_specs=[whole_spec()] * len(acts) + [hbm_spec()] * len(weights),
        out_specs=tuple(whole_spec() for _ in range(requests)),
        scratch_shapes=[
            pltpu.VMEM((wide, rows, step), F32),
            pltpu.VMEM((2 * wide, depth, width), BF16),
            pltpu.SemaphoreType.DMA((2 * wide,)),
        ],
        compiler_params=params(),
    )(*acts, *weights)


def per_device(
    queries,
    text_cache,
    image_cache,
    fresh_kv,
    fresh_slots,
    fresh_pos,
    image_len,
    stream,
    modulation,
    out_weight,
    up_weight,
    down_weight,
    final_weight,
    latent,
    step_index,
):
    cfg_id = lax.axis_index("cfg")
    req_id = lax.axis_index("req")
    seq_id = lax.axis_index("seq")
    requests = lax.axis_size("req")
    high, wide = seq_grid(lax.axis_size("seq"))
    y_id, x_id = seq_id // wide, seq_id % wide
    around = [(dy, dx) for dy in range(high) for dx in range(wide)]

    def x_from(step):
        return (x_id - step) % wide

    def y_from(step):
        return (y_id - step) % high

    def seq_from(dy, dx):
        return y_from(dy) * wide + x_from(dx)

    fresh_count = fresh_kv.shape[3]
    padded = -(-fresh_count // 16) * 16
    fresh_pair = rotate_fresh(fresh_kv[0, 0], fresh_pos, padded)
    fresh = [send_seq(fresh_pair, dy, dx) for dy, dx in around]

    out_rows, col_count = out_weight.shape
    seg = col_count // 2
    own_out, _ = lax.optimization_barrier((out_weight, fresh_pair))
    own_out = take(own_out, cfg_id * seg, seg, 1)
    out_y = [send_y(own_out, dy) for dy in range(high)]
    out_x = [send_x(own_out, dx) for dx in range(wide)]

    up_rows, hidden = up_weight.shape
    hidden_x = hidden // wide
    hidden_half = hidden_x // 2
    early_up, _ = lax.optimization_barrier((up_weight, fresh_pair))
    to_x = []
    for dx in range(wide):
        first = (x_id + dx) % wide * hidden_x + cfg_id * hidden_half
        to_x.append(take(early_up, first, hidden_half, 1))
    to_x, out_y, fresh = lax.optimization_barrier((to_x, out_y, fresh))
    up_x = [send_x(part, dx) for dx, part in enumerate(to_x)]
    up_y = [send_y(up_x[0], dy) for dy in range(high)]
    out_mine = [send_x(out_y[dy], dx) if dy else out_x[dx] for dy, dx in around]

    length = lax.dynamic_index_in_dim(image_len, req_id, 0, keepdims=False)
    attended = attention(
        around,
        image_len,
        fresh_slots,
        queries[0, 0],
        text_cache[0, 0],
        image_cache[0, 0],
        fresh,
    )
    row_count = queries.shape[2]
    if attended.shape[2] != out_rows:
        attended = jnp.transpose(attended, (1, 0, 2)).reshape(row_count, -1, out_rows)
        attended = jnp.transpose(attended, (1, 0, 2))
    attended_all = [send_z(attended, dz) for dz in range(requests)]
    out_mine, attended, late_up = lax.optimization_barrier((out_mine, attended, up_weight))
    swapped = swap_core(jnp.concatenate(out_mine[1:], axis=0))
    own_up = [
        take(late_up, x_id * hidden_x + h * hidden_half, hidden_half, 1) for h in range(2)
    ]

    attended_all, up_y = lax.optimization_barrier((attended_all, up_y))
    along_y = [gather_core(part) for part in up_y[1:]]
    residual = residual_columns(
        around,
        attended_all,
        out_weight,
        out_mine[1:],
        swapped,
        stream,
        modulation,
    )
    along_z = [send_z(residual, dz) for dz in range(requests)]
    near = [send_x(residual, dx) for dx in range(wide)]

    up_x[1:], _ = lax.optimization_barrier((up_x[1:], residual))
    up_mine = [send_y(up_x[dx], dy) if dx else up_y[dy] for dy, dx in around]

    along_x = [gather_core(part) for part in up_x[1:]]

    down_cols = down_weight.shape[1]
    down_half = hidden // 2
    own_down = take(down_weight, cfg_id * down_half, down_half, 0)
    along_z, near, along_x, along_y, up_mine, own_down = lax.optimization_barrier(
        (along_z, near, along_x, along_y, up_mine, own_down)
    )
    blocks = [
        [send_x(block, dx) if dz else near[dx] for dz, block in enumerate(along_z)]
        for dx in range(wide)
    ]
    down_mine = [send_y(own_down, dy) for dy in range(1, high)]
    up_pieces = [("halves", own_up)]
    for part, (dy, dx) in zip(up_mine[1:], around[1:]):
        if dy and dx:
            up_pieces.append(("core", [part, swap_core(part)]))
        else:
            up_pieces.append(("stack", [along_y[dy - 1] if dy else along_x[dx - 1]]))

    acts, own_rows = [], []
    for dx in range(wide):
        if acts:
            blocks[dx], acts[0] = lax.optimization_barrier((blocks[dx], acts[0]))
        act, own = up_products(around, blocks[dx], modulation, up_pieces)
        own_rows.append(own)
        acts += [send_x(act, step) for step in range(wide)]

    shares = [down_products(acts, [down_weight], requests)]
    down_mine, _ = lax.optimization_barrier((down_mine, shares[0]))
    for mine in down_mine:
        shares.append(down_products(acts, [mine, swap_core(mine)], requests))

    model = requests * col_count
    natural = jnp.zeros((wide, row_count, model), F32)
    for dx, own in enumerate(own_rows):
        natural = lax.dynamic_update_slice_in_dim(natural, own[None].astype(F32), x_from(dx), 0)
    natural = natural.reshape(wide * row_count, model)
    mod_half = lax.dynamic_index_in_dim(modulation, cfg_id, 0, keepdims=False)
    gate_two = lax.dynamic_index_in_dim(mod_half[:, 3, :], req_id, 0, keepdims=False)

    def finished(share, col):
        total = share[0].astype(F32)
        for dz in range(1, requests):
            total += send_z(share[dz], dz).astype(F32)
        total = total.reshape(wide * row_count, down_cols)
        block_out = (
            take(natural, col, down_cols, 1) + take(gate_two, col, down_cols, 0)[None, :] * total
        ).astype(BF16)
        return dot(block_out, take(final_weight, col, down_cols, 0))

    velocity = 0.0
    for dy, share in enumerate(shares):
        velocity += finished(share, seq_from(dy, 0) * down_cols)

    channels = velocity.shape[1]
    velocity = velocity.reshape(wide, row_count // 2, 2, channels)
    cfg_count = lax.axis_size("cfg")
    halves = []
    for dc in range(2):
        share = 0.0
        for dx in range(wide):
            block = lax.dynamic_index_in_dim(velocity, (x_id + dx) % wide, 0, keepdims=False)
            block = lax.dynamic_index_in_dim(block, cfg_id ^ dc, 1, keepdims=False)
            if dc or dx:
                route = [
                    (
                        (c * high + y) * wide + x,
                        ((c ^ dc) * high + y) * wide + (x + dx) % wide,
                    )
                    for c in range(cfg_count)
                    for y in range(high)
                    for x in range(wide)
                ]
                block = lax.ppermute(block, ("cfg", "seq"), route)
            share += block
        halves.append(share)
    cond_part = jnp.where(cfg_id == 0, halves[0], halves[1])
    uncond_part = jnp.where(cfg_id == 0, halves[1], halves[0])
    guided = uncond_part + GUIDANCE * (cond_part - uncond_part)
    level_now = noise_level(step_index[0])
    level_next = noise_level(step_index[0] + 1)
    token_ids = (
        seq_id * row_count
        + 2 * jnp.arange(row_count // 2, dtype=jnp.int32)[:, None]
        + cfg_id
        + jnp.zeros((1, channels), jnp.int32)
    )
    valid = token_ids < length
    current = latent[0]
    latent_next = jnp.where(valid, current + (level_next - level_now) * guided, current)
    denoised = jnp.where(valid, current - level_now * guided, current)
    return (latent_next[None], denoised[None])


def solution(mesh):
    in_specs = (
        P("cfg", "req", "seq", None),
        P("cfg", "req", None, None, None),
        P("cfg", "req", None, None, None),
        P("cfg", "req", None, "seq", None),
        P("req", None),
        P(None, "req", "seq"),
        P(),
        P("cfg", None, "seq", "req"),
        P(),
        P("seq", "req"),
        P("seq", "req"),
        P("req", "seq"),
        P(),
        P("req", "seq", "cfg"),
        P(),
    )
    out_specs = (P("req", "seq", "cfg"), P("req", "seq", "cfg"))
    return jax.shard_map(
        per_device, mesh=mesh, in_specs=in_specs, out_specs=out_specs, check_vma=False
    )
```

```python
import functools
import math

import jax
import jax.numpy as jnp
import numpy as np
from jax import lax
from jax.experimental import pallas as pl
from jax.experimental.pallas import tpu as pltpu
from jax.sharding import PartitionSpec as P

STEPS = 28
GUIDANCE = 3.0
SHIFT = 3.0
SCALE = 1.0 / math.sqrt(128.0)
EPSILON = 1e-06
HEAD = 128
BF16 = jnp.bfloat16
F32 = jnp.float32
MIB = 1024 * 1024


def noise_level(index):
    fraction = 1.0 - index.astype(jnp.float32) / STEPS
    return SHIFT * fraction / (SHIFT * fraction + 1.0 - fraction)


def lane_frequencies():
    rows = np.zeros((3, HEAD), np.float32)
    lane = 0
    for component, axis_span in ((0, 16), (1, 56), (2, 56)):
        pair_ids = np.arange(axis_span // 2, dtype=np.float32)
        frequency = np.exp(-(2.0 * pair_ids / axis_span) * np.float32(math.log(10000.0)))
        rows[component, lane : lane + axis_span] = np.repeat(frequency, 2)
        lane += axis_span
    return rows


def seq_grid(count):
    columns = 2 ** ((count.bit_length() - 1) // 2)
    return count // columns, columns


def send_x(block, step):
    if step == 0:
        return block
    high, wide = seq_grid(lax.axis_size("seq"))
    route = [(y * wide + x, y * wide + (x + step) % wide) for y in range(high) for x in range(wide)]
    return lax.ppermute(block, "seq", route)


def send_y(block, step):
    if step == 0:
        return block
    high, wide = seq_grid(lax.axis_size("seq"))
    route = [(y * wide + x, (y + step) % high * wide + x) for y in range(high) for x in range(wide)]
    return lax.ppermute(block, "seq", route)


def send_seq(block, dy, dx):
    if dy == 0 and dx == 0:
        return block
    high, wide = seq_grid(lax.axis_size("seq"))
    route = [
        (y * wide + x, (y + dy) % high * wide + (x + dx) % wide)
        for y in range(high)
        for x in range(wide)
    ]
    return lax.ppermute(block, "seq", route)


def send_z(block, step):
    if step == 0:
        return block
    count = lax.axis_size("req")
    return lax.ppermute(block, "req", [(r, (r + step) % count) for r in range(count)])


def swap_core(block):
    return lax.ppermute(block, "cfg", [(0, 1), (1, 0)])


def take(array, start, size, axis):
    return lax.dynamic_slice_in_dim(array, start, size, axis)


def dot(left, right):
    return jnp.dot(left, right, preferred_element_type=jnp.float32)


def hbm_spec():
    return pl.BlockSpec(memory_space=pl.ANY)


def place_of(step_x, step_y=0):
    high, wide = seq_grid(lax.axis_size("seq"))
    seq = lax.axis_index("seq")
    return lax.rem(seq // wide + high - step_y, high) * wide + x_of(step_x)


def x_of(step):
    wide = seq_grid(lax.axis_size("seq"))[1]
    return lax.rem(lax.axis_index("seq") % wide + 2 * wide - step, wide)


def z_of(step):
    count = lax.axis_size("req")
    return lax.rem(lax.axis_index("req") + count - step, count)


def whole_spec():
    return pl.BlockSpec(memory_space=pltpu.VMEM)


def smem_spec():
    return pl.BlockSpec(memory_space=pltpu.SMEM)


def cost(flops, moved):
    return pl.CostEstimate(flops=int(flops), bytes_accessed=int(moved), transcendentals=0)


def params():
    return pltpu.CompilerParams(vmem_limit_bytes=60 * MIB)


def rotate_kernel(kv_ref, pos_ref, freq_ref, out_ref):
    rows, width = kv_ref.shape[1:]
    row_ids = lax.broadcasted_iota(jnp.int32, (rows, HEAD), 0)
    angles = jnp.zeros((rows, HEAD), F32)
    for row in range(rows):
        line = (
            pos_ref[0, 0, row].astype(F32) * freq_ref[0:1, :]
            + pos_ref[1, 0, row].astype(F32) * freq_ref[1:2, :]
            + pos_ref[2, 0, row].astype(F32) * freq_ref[2:3, :]
        )
        angles = jnp.where(row_ids == row, line, angles)
    cosine, sine = jnp.cos(angles), jnp.sin(angles)
    even = lax.broadcasted_iota(jnp.int32, (rows, HEAD), 1) % 2 == 0
    out_ref[...] = jnp.zeros_like(out_ref)
    for first in range(0, width, HEAD):
        keys = kv_ref[0, :, first : first + HEAD].astype(F32)
        after = pltpu.roll(keys, HEAD - 1, 1)
        before = pltpu.roll(keys, 1, 1)
        rotated = cosine * keys + sine * jnp.where(even, -after, before)
        out_ref[0, 0:rows, first : first + HEAD] = rotated.astype(BF16)
    out_ref[1, 0:rows, :] = kv_ref[1]


def rotate_fresh(fresh, positions, padded):
    width = fresh.shape[2]
    return pl.pallas_call(
        rotate_kernel,
        out_shape=jax.ShapeDtypeStruct((2, padded, width), BF16),
        in_specs=[whole_spec(), smem_spec(), whole_spec()],
        out_specs=whole_spec(),
        compiler_params=params(),
        cost_estimate=cost(10**6, fresh.size * 4),
    )(fresh, positions, jnp.asarray(lane_frequencies()))


def attention_kernel(around, lengths_ref, slots_ref, q_ref, text_ref, image_ref, *refs):
    pieces = len(around)
    fresh_refs, (out_ref, fresh_ref) = refs[:pieces], refs[pieces:]
    padded = fresh_refs[0].shape[1]
    for i in range(pieces):
        fresh_ref[:, i * padded : (i + 1) * padded, :] = fresh_refs[i][...]
    slots = image_ref.shape[1]
    count = slots_ref.shape[1] // pieces
    length = lengths_ref[lax.axis_index("req")]
    key_ids = lax.broadcasted_iota(jnp.int32, (1, slots), 1)
    fresh_ids = lax.broadcasted_iota(jnp.int32, (1, pieces * padded), 1)
    image_bias = jnp.where(key_ids < length, 0.0, -jnp.inf)
    fresh_bias = jnp.full(fresh_ids.shape, -jnp.inf, F32)
    for i, (dy, dx) in enumerate(around):
        first = place_of(dx, dy) * count
        for j in range(count):
            slot = slots_ref[0, first + j]
            image_bias = jnp.where(key_ids == slot, -jnp.inf, image_bias)
            here = (fresh_ids == i * padded + j) & (slot < length)
            fresh_bias = jnp.where(here, 0.0, fresh_bias)
    over_lanes = (((1,), (1,)), ((), ()))
    for first in range(0, q_ref.shape[1], HEAD):
        head = slice(first, first + HEAD)
        query = q_ref[:, head]

        def scores(keys):
            return lax.dot_general(query, keys, over_lanes, preferred_element_type=F32) * SCALE

        text = scores(text_ref[0, :, head])
        image = scores(image_ref[0, :, head]) + image_bias
        fresh = scores(fresh_ref[0, :, head]) + fresh_bias
        best = jnp.maximum(
            jnp.max(text, axis=1, keepdims=True),
            jnp.maximum(
                jnp.max(image, axis=1, keepdims=True), jnp.max(fresh, axis=1, keepdims=True)
            ),
        )
        text, image, fresh = jnp.exp(text - best), jnp.exp(image - best), jnp.exp(fresh - best)
        total = (
            jnp.sum(text, axis=1, keepdims=True)
            + jnp.sum(image, axis=1, keepdims=True)
            + jnp.sum(fresh, axis=1, keepdims=True)
        )
        mixed = (
            dot(text.astype(BF16), text_ref[1, :, head])
            + dot(image.astype(BF16), image_ref[1, :, head])
            + dot(fresh.astype(BF16), fresh_ref[1, :, head])
        )
        out_ref[0, :, head] = (mixed / total).astype(BF16)


def attention(around, lengths, slot_ids, query, text_kv, image_kv, fresh):
    rows, width = query.shape
    group = 3 * HEAD
    groups = width // group
    text, slots = text_kv.shape[1], image_kv.shape[1]
    pieces, padded = len(fresh), fresh[0].shape[1]
    return pl.pallas_call(
        functools.partial(attention_kernel, around),
        grid=(groups,),
        out_shape=jax.ShapeDtypeStruct((groups, rows, group), BF16),
        in_specs=[
            smem_spec(),
            smem_spec(),
            pl.BlockSpec((rows, group), lambda g: (0, g)),
            pl.BlockSpec((2, text, group), lambda g: (0, 0, g)),
            pl.BlockSpec((2, slots, group), lambda g: (0, 0, g)),
        ]
        + [pl.BlockSpec((2, padded, group), lambda g: (0, 0, g))] * pieces,
        out_specs=pl.BlockSpec((1, rows, group), lambda g: (g, 0, 0)),
        scratch_shapes=[pltpu.VMEM((2, padded * pieces, group), BF16)],
        compiler_params=params(),
        cost_estimate=cost(4 * query.size * (text + slots), 2 * (text_kv.size + image_kv.size)),
    )(lengths, slot_ids, query, text_kv, image_kv, *fresh)


def residual_kernel(requests, around, *refs):
    pieces = len(around)
    attended, refs = refs[:requests], refs[requests:]
    own_ref, mine, refs = refs[0], refs[1:pieces], refs[pieces:]
    swapped_ref, stream_ref, mod_ref, out_ref, rows_ref = refs
    row_count = attended[0].shape[1]
    depth, width = own_ref.shape
    half_width = width // 2
    cfg, req = lax.axis_index("cfg"), lax.axis_index("req")
    places = [place_of(dx, dy) for dy, dx in around]
    for j in range(requests):
        first = pl.multiple_of(z_of(j) * row_count, 16)
        rows_ref[:, pl.ds(first, row_count), :] = attended[j][...]
    at = pl.multiple_of(req * width, 128)
    gates = [mod_ref[cfg, q, 0:1, pl.ds(at, width)] for q in range(requests)]

    def columns(core):
        for role, half in ((0, core), (1, 1 - core)):
            lanes = slice(half * half_width, (half + 1) * half_width)
            total = dot(rows_ref[places[0]], own_ref[:, lanes])
            for k in range(1, pieces):
                piece = swapped_ref[(k - 1) * depth : k * depth, :] if role else mine[k - 1][...]
                total += dot(rows_ref[places[k]], piece)
            for q in range(requests):
                out_ref[q, :, lanes] = (
                    stream_ref[0, q, :, lanes].astype(F32)
                    + gates[q][:, lanes] * total[q * row_count : (q + 1) * row_count]
                ).astype(BF16)

    pl.when(cfg == 0)(functools.partial(columns, 0))
    pl.when(cfg == 1)(functools.partial(columns, 1))


def residual_columns(around, attended, own, mine, swapped, stream, modulation):
    requests, pieces = len(attended), len(mine) + 1
    segments, row_count, seg = attended[0].shape
    return pl.pallas_call(
        functools.partial(residual_kernel, requests, around),
        out_shape=jax.ShapeDtypeStruct(stream.shape[1:], BF16),
        in_specs=[whole_spec()] * (requests + pieces + 3),
        out_specs=whole_spec(),
        scratch_shapes=[pltpu.VMEM((segments, requests * row_count, seg), BF16)],
        compiler_params=params(),
        cost_estimate=cost(2 * stream.size * own.shape[0] * pieces, 8 * stream.size),
    )(*attended, own, *mine, swapped, stream, modulation)


def copies_of(pieces, buffer, sems):
    cfg = lax.axis_index("cfg")
    copies = []
    for k, (kind, parts) in enumerate(pieces):
        for h in range(2):
            slot = h
            if kind == "core":
                slot = cfg if h == 0 else 1 - cfg
            copies.append(
                (h, pltpu.make_async_copy(parts[h], buffer.at[slot, k], sems.at[slot, k]))
            )
    return [copy for h in range(2) for half, copy in copies if half == h]


def up_kernel(requests, around, kinds, *refs):
    blocks, refs = refs[:requests], refs[requests:]
    mod_ref, refs = refs[0], refs[1:]
    pieces = []
    for kind in kinds:
        pieces.append((kind, refs[:2]))
        refs = refs[2:]
    out_refs, (own_ref, rows_ref, buffer, sems) = refs[:2], refs[2:]
    row_count, width = blocks[0].shape[1:]
    depth, hidden = buffer.shape[2:]
    cfg, req = lax.axis_index("cfg"), lax.axis_index("req")
    scale_of_mean = 1.0 / (requests * width)
    for copy in copies_of(pieces, buffer, sems):
        copy.start()
    for q in range(requests):
        total = jnp.zeros((row_count, 1), F32)
        for block in blocks:
            total += jnp.sum(block[q].astype(F32), axis=1, keepdims=True)
        average = total * scale_of_mean
        total = jnp.zeros((row_count, 1), F32)
        for block in blocks:
            centered = block[q].astype(F32) - average
            total += jnp.sum(centered * centered, axis=1, keepdims=True)
        inverse = lax.rsqrt(total * scale_of_mean + EPSILON)
        for dz, block in enumerate(blocks):
            place = z_of(dz)
            at = pl.ds(pl.multiple_of(place * width, 128), width)
            scale = 1.0 + mod_ref[cfg, q, 2:3, at]
            shift = mod_ref[cfg, q, 1:2, at]
            normed = (block[q].astype(F32) - average) * inverse * scale + shift
            normed = normed.astype(BF16)
            for i in range(width // depth):
                rows_ref[
                    place * (width // depth) + i, q * row_count : (q + 1) * row_count, :
                ] = normed[:, i * depth : (i + 1) * depth]
    for dz, block in enumerate(blocks):
        at = pl.ds(pl.multiple_of(z_of(dz) * width, 128), width)
        own_ref[:, at] = block[req]
    step = 256 if hidden % 256 == 0 else hidden
    for h in range(2):
        for c in range(hidden // step):
            total = None
            for k, (dy, dx) in enumerate(around):
                if c == 0:
                    source = pieces[k][1][0]
                    pltpu.make_async_copy(source, buffer.at[h, k], sems.at[h, k]).wait()
                weight = buffer[h, k, :, c * step : (c + 1) * step]
                term = dot(rows_ref[place_of(dx, dy)], weight)
                total = term if total is None else total + term
            out_refs[h][:, c * step : (c + 1) * step] = jax.nn.gelu(
                total, approximate=True
            ).astype(BF16)


def up_products(around, blocks, modulation, pieces):
    requests = len(blocks)
    row_count, slice_width = blocks[0].shape[1:]
    model = requests * slice_width
    depth, hidden = pieces[0][1][0].shape[-2:]
    rows = requests * row_count
    operands = [part for _, parts in pieces for part in parts]
    return pl.pallas_call(
        functools.partial(up_kernel, requests, around, [kind for kind, _ in pieces]),
        out_shape=(
            jax.ShapeDtypeStruct((rows, hidden), BF16),
            jax.ShapeDtypeStruct((rows, hidden), BF16),
            jax.ShapeDtypeStruct((row_count, model), BF16),
        ),
        in_specs=[whole_spec()] * (requests + 1) + [hbm_spec()] * len(operands),
        out_specs=(whole_spec(),) * 3,
        scratch_shapes=[
            pltpu.VMEM((model // depth, rows, depth), BF16),
            pltpu.VMEM((2, len(pieces), depth, hidden), BF16),
            pltpu.SemaphoreType.DMA((2, len(pieces))),
        ],
        compiler_params=params(),
        cost_estimate=cost(4 * rows * model * hidden, 4 * model * hidden),
    )(*blocks, modulation, *operands)


def begin_kernel(wide, *refs):
    acts, (weight_ref, out_ref, buffer, sems) = refs[: 2 * wide], refs[2 * wide :]
    rows, depth = acts[0].shape
    width = weight_ref.shape[1]
    copies = []
    for h in range(2):
        first = pl.multiple_of((2 * x_of(0) + h) * depth, 16)
        source = weight_ref.at[pl.ds(first, depth), :]
        copies.append(pltpu.make_async_copy(source, buffer.at[h], sems.at[h]))
        copies[h].start()
    for h in range(2):
        copies[h].wait()
    step = 256 if width % 256 == 0 else width
    for c in range(width // step):
        lanes = slice(c * step, (c + 1) * step)
        total = None
        for h in range(2):
            left = jnp.concatenate([act[...] for act in acts[h::2]], axis=0)
            term = dot(left, buffer[h, :, lanes])
            total = term if total is None else total + term
        for e in range(wide):
            out_ref[e, :, lanes] = total[e * rows : (e + 1) * rows]


def begin_down(acts, weight):
    wide, (rows, depth), width = len(acts), acts[0][0].shape, weight.shape[1]
    return pl.pallas_call(
        functools.partial(begin_kernel, wide),
        out_shape=jax.ShapeDtypeStruct((wide, rows, width), F32),
        in_specs=[whole_spec()] * (2 * wide) + [hbm_spec()],
        out_specs=whole_spec(),
        scratch_shapes=[
            pltpu.VMEM((2, depth, width), BF16),
            pltpu.SemaphoreType.DMA((2,)),
        ],
        compiler_params=params(),
        cost_estimate=cost(4 * wide * rows * depth * width, 4 * depth * width),
    )(*[half for act in acts for half in act], weight)


def end_kernel(requests, block, steps, weights, *refs):
    acts, refs = refs[: 2 * len(steps)], refs[2 * len(steps) :]
    weight_refs, refs = refs[:weights], refs[weights:]
    begun_refs, refs = refs[:weights], refs[weights:]
    out_refs, (scratch_ref, buffer, sems) = refs[:requests], refs[requests:]
    rows, depth = acts[0].shape
    width = weight_refs[0].shape[1]
    copies = []
    for w, weight_ref in enumerate(weight_refs):
        for k, far in enumerate(steps):
            for h in range(2):
                first = pl.multiple_of((2 * x_of(far) + h) * depth, 16)
                source = weight_ref.at[pl.ds(first, depth), :]
                target = buffer.at[w, k, h]
                copies.append(pltpu.make_async_copy(source, target, sems.at[w, k, h]))
                copies[-1].start()
    step = 256 if width % 256 == 0 else width
    for w in range(weights):
        for copy in copies[w * 2 * len(steps) : (w + 1) * 2 * len(steps)]:
            copy.wait()
        for c in range(width // step):
            lanes = slice(c * step, (c + 1) * step)
            total = begun_refs[w][block, :, lanes]
            for k in range(len(steps)):
                for h in range(2):
                    total += dot(acts[2 * k + h][...], buffer[w, k, h, :, lanes])
            scratch_ref[...] = total
            at = slice(w * width + c * step, w * width + (c + 1) * step)
            row_count = rows // requests
            for dz in range(requests):
                first = pl.multiple_of(z_of(requests - dz) * row_count, 16)
                out_refs[dz][:, at] = scratch_ref[pl.ds(first, row_count), :].astype(BF16)


def end_down(block, acts, steps, weights, begun, requests):
    (rows, depth), width = acts[0][0].shape, weights[0].shape[1]
    count = len(weights)
    step = 256 if width % 256 == 0 else width
    shape = (rows // requests, width * count)
    return pl.pallas_call(
        functools.partial(end_kernel, requests, block, steps, count),
        out_shape=tuple(jax.ShapeDtypeStruct(shape, BF16) for _ in range(requests)),
        in_specs=[whole_spec()] * (2 * len(acts))
        + [hbm_spec()] * count
        + [whole_spec()] * count,
        out_specs=tuple(whole_spec() for _ in range(requests)),
        scratch_shapes=[
            pltpu.VMEM((rows, step), F32),
            pltpu.VMEM((count, len(steps), 2, depth, width), BF16),
            pltpu.SemaphoreType.DMA((count, len(steps), 2)),
        ],
        compiler_params=params(),
        cost_estimate=cost(4 * count * rows * depth * width, 4 * count * depth * width),
    )(*[half for act in acts for half in act], *weights, *begun)


def join_kernel(parts, *refs):
    part_refs, out_ref, sems = refs[:parts], refs[parts], refs[parts + 1]
    cfg = lax.axis_index("cfg")
    half = out_ref.shape[0] // 2
    copies = []
    for k in range(parts):
        first = (cfg if k < parts // 2 else 1 - cfg) * half
        if k % (parts // 2):
            first += sum(ref.shape[0] for ref in part_refs[: k % (parts // 2)])
        rows = part_refs[k].shape[0]
        target = out_ref.at[pl.ds(pl.multiple_of(first, 16), rows), :]
        copies.append(pltpu.make_async_copy(part_refs[k], target, sems.at[k]))
        copies[k].start()
    for copy in copies:
        copy.wait()


def join_halves(mine, other):
    parts = [*mine, *other]
    rows = sum(part.shape[0] for part in parts)
    return pl.pallas_call(
        functools.partial(join_kernel, len(parts)),
        out_shape=jax.ShapeDtypeStruct((rows, mine[0].shape[1]), BF16),
        in_specs=[hbm_spec()] * len(parts),
        out_specs=hbm_spec(),
        scratch_shapes=[pltpu.SemaphoreType.DMA((len(parts),))],
        compiler_params=params(),
        cost_estimate=cost(0, 4 * rows * mine[0].shape[1]),
    )(*parts)


def per_device(
    queries,
    text_cache,
    image_cache,
    fresh_kv,
    fresh_slots,
    fresh_pos,
    image_len,
    stream,
    modulation,
    out_weight,
    up_weight,
    down_weight,
    final_weight,
    latent,
    step_index,
):
    cfg_id = lax.axis_index("cfg")
    req_id = lax.axis_index("req")
    seq_id = lax.axis_index("seq")
    requests = lax.axis_size("req")
    high, wide = seq_grid(lax.axis_size("seq"))
    y_id, x_id = seq_id // wide, seq_id % wide
    around = [(dy, dx) for dy in range(high) for dx in range(wide)]

    def x_from(step):
        return (x_id - step) % wide

    def y_from(step):
        return (y_id - step) % high

    def seq_from(dy, dx):
        return y_from(dy) * wide + x_from(dx)

    fresh_count = fresh_kv.shape[3]
    padded = -(-fresh_count // 16) * 16
    fresh_pair = rotate_fresh(fresh_kv[0, 0], fresh_pos, padded)
    fresh = [send_seq(fresh_pair, dy, dx) for dy, dx in around]

    out_rows, col_count = out_weight.shape
    seg = col_count // 2
    own_out, _ = lax.optimization_barrier((out_weight, fresh_pair))
    own_out = take(own_out, cfg_id * seg, seg, 1)
    out_y = [send_y(own_out, dy) for dy in range(high)]
    out_x = [send_x(own_out, dx) for dx in range(wide)]

    up_rows, hidden = up_weight.shape
    hidden_x = hidden // wide
    hidden_half = hidden_x // 2
    early_up, _ = lax.optimization_barrier((up_weight, fresh_pair))
    to_x = []
    for dx in range(wide):
        first = (x_id + dx) % wide * hidden_x + cfg_id * hidden_half
        to_x.append(take(early_up, first, hidden_half, 1))
    down_cols = down_weight.shape[1]
    down_half = hidden // 2
    down_early = down_half // 4
    early_down, _ = lax.optimization_barrier((down_weight, fresh_pair))
    early_down = take(early_down, cfg_id * down_half, down_early, 0)
    early_down, to_x, out_y, fresh = lax.optimization_barrier((early_down, to_x, out_y, fresh))
    down_first = [send_y(early_down, dy) for dy in range(1, high)]
    up_x = [send_x(part, dx) for dx, part in enumerate(to_x)]
    up_y = [send_y(up_x[0], dy) for dy in range(high)]
    out_mine = [send_x(out_y[dy], dx) if dy else out_x[dx] for dy, dx in around]

    length = lax.dynamic_index_in_dim(image_len, req_id, 0, keepdims=False)
    attended = attention(
        around,
        image_len,
        fresh_slots,
        queries[0, 0],
        text_cache[0, 0],
        image_cache[0, 0],
        fresh,
    )
    row_count = queries.shape[2]
    if attended.shape[2] != out_rows:
        attended = jnp.transpose(attended, (1, 0, 2)).reshape(row_count, -1, out_rows)
        attended = jnp.transpose(attended, (1, 0, 2))
    out_mine, attended, late_up = lax.optimization_barrier((out_mine, attended, up_weight))
    fetched = jnp.concatenate(out_mine[1:], axis=0)
    fetched, up_x[1:] = lax.optimization_barrier((fetched, up_x[1:]))
    swapped = swap_core(fetched)
    attended_all = [send_z(attended, dz) for dz in range(requests)]
    own_up = [
        take(late_up, x_id * hidden_x + h * hidden_half, hidden_half, 1) for h in range(2)
    ]

    attended_all, up_y, down_first = lax.optimization_barrier((attended_all, up_y, down_first))
    other_y = [swap_core(part) for part in up_y[1:]]
    residual = residual_columns(
        around,
        attended_all,
        out_weight,
        out_mine[1:],
        swapped,
        stream,
        modulation,
    )
    along_z = [send_z(residual, dz) for dz in range(requests)]

    up_x[1:], other_y, _ = lax.optimization_barrier((up_x[1:], other_y, residual))
    other_x = [swap_core(part) for part in up_x[1:]]
    up_mine = [send_y(up_x[dx], dy) if dx else up_y[dy] for dy, dx in around]

    ahead = [dz for dz in (1, requests - 1) if dz != requests // 2]
    along_z[0] = residual
    forward = {(dz, dx): send_x(along_z[dz], dx) for dz in [*ahead, 0] for dx in range(1, wide)}

    own_down = take(down_weight, cfg_id * down_half + down_early, down_half - down_early, 0)
    along_z, forward, other_x, up_mine, own_down = lax.optimization_barrier(
        (along_z, forward, other_x, up_mine, own_down)
    )
    for dx in range(1, wide):
        for dz in range(requests):
            if (dz, dx) not in forward:
                forward[dz, dx] = send_x(along_z[dz], dx)
    along_z, forward = lax.optimization_barrier((along_z, forward))
    blocks = [along_z]
    blocks += [[forward[dz, dx] for dz in range(requests)] for dx in range(1, wide)]
    down_mine = [send_y(own_down, dy) for dy in range(1, high)]
    up_pieces = [("halves", own_up)]
    for part, (dy, dx) in zip(up_mine[1:], around[1:]):
        if dy and dx:
            up_pieces.append(("core", [part, swap_core(part)]))
        else:
            up_pieces.append(("core", [part, other_y[dy - 1] if dy else other_x[dx - 1]]))

    acts, own_rows = [], []
    for dx in range(wide):
        if acts:
            blocks[dx], acts[-1] = lax.optimization_barrier((blocks[dx], acts[-1]))
        *act, own = up_products(around, blocks[dx], modulation, up_pieces)
        own_rows.append(own.astype(F32))
        acts += [[send_x(half, step) for half in act] for step in range(wide)]

    own_acts = acts[::wide]
    steps = list(range(1, wide))

    def parts_of(e):
        return [acts[(e - step) % wide * wide + step] for step in steps]

    def sent(share):
        return [send_z(part, dz) for dz, part in enumerate(share)]

    begun = [begin_down(own_acts, down_weight)]
    shares = [[] for _ in range(wide)]
    for e in steps:
        shares[e].append(
            sent(end_down(e, parts_of(e), steps, [down_weight], begun, requests))
        )
    down_mine, down_first, acts[-1][0] = lax.optimization_barrier(
        (down_mine, down_first, acts[-1][0])
    )
    far = [
        join_halves([early, late], [swap_core(early), swap_core(late)])
        for early, late in zip(down_first, down_mine)
    ]
    begun_far = [begin_down(own_acts, weight) for weight in far]
    for e in steps:
        share = end_down(e, parts_of(e), steps, far, begun_far, requests)
        last, share, shares[e][0] = lax.optimization_barrier((parts_of(0), share, shares[e][0]))
        shares[e].append(sent(share))
    weights = [down_weight, *far]
    shares[0].append(sent(end_down(0, last, steps, weights, begun + begun_far, requests)))

    mod_half = lax.dynamic_index_in_dim(modulation, cfg_id, 0, keepdims=False)
    gate_two = lax.dynamic_index_in_dim(mod_half[:, 3, :], req_id, 0, keepdims=False)

    def summed(parts):
        total = parts[0].astype(F32)
        for part in parts[1:]:
            total += part.astype(F32)
        return total

    def finished(total, rows, dy):
        col = seq_from(dy, 0) * down_cols
        block_out = (
            take(rows, col, down_cols, 1) + take(gate_two, col, down_cols, 0)[None, :] * total
        ).astype(BF16)
        return dot(block_out, take(final_weight, col, down_cols, 0))

    velocity = []
    for e in range(wide):
        total = jnp.concatenate([summed(parts) for parts in shares[e]], axis=1)
        velocity.append(0.0)
        for dy in range(high):
            part = lax.slice_in_dim(total, dy * down_cols, (dy + 1) * down_cols, axis=1)
            velocity[e] += finished(part, own_rows[e], dy)

    channels = final_weight.shape[1]
    cfg_count = lax.axis_size("cfg")
    halves = []
    for dc in range(2):
        share = 0.0
        for e in range(wide):
            block = velocity[e].reshape(row_count // 2, 2, channels)
            block = lax.dynamic_index_in_dim(block, cfg_id ^ dc, 1, keepdims=False)
            if dc or e:
                route = [
                    ((c * high + y) * wide + x, ((c ^ dc) * high + y) * wide + (x - e) % wide)
                    for c in range(cfg_count)
                    for y in range(high)
                    for x in range(wide)
                ]
                block = lax.ppermute(block, ("cfg", "seq"), route)
            share += block
        halves.append(share)
    cond_part = jnp.where(cfg_id == 0, halves[0], halves[1])
    uncond_part = jnp.where(cfg_id == 0, halves[1], halves[0])
    guided = uncond_part + GUIDANCE * (cond_part - uncond_part)
    level_now = noise_level(step_index[0])
    level_next = noise_level(step_index[0] + 1)
    token_ids = (
        seq_id * row_count
        + 2 * jnp.arange(row_count // 2, dtype=jnp.int32)[:, None]
        + cfg_id
        + jnp.zeros((1, channels), jnp.int32)
    )
    valid = token_ids < length
    current = latent[0]
    latent_next = jnp.where(valid, current + (level_next - level_now) * guided, current)
    denoised = jnp.where(valid, current - level_now * guided, current)
    return (latent_next[None], denoised[None])


def solution(mesh):
    in_specs = (
        P("cfg", "req", "seq", None),
        P("cfg", "req", None, None, None),
        P("cfg", "req", None, None, None),
        P("cfg", "req", None, "seq", None),
        P("req", None),
        P(None, "req", "seq"),
        P(),
        P("cfg", None, "seq", "req"),
        P(),
        P("seq", "req"),
        P("seq", "req"),
        P("req", "seq"),
        P(),
        P("req", "seq", "cfg"),
        P(),
    )
    out_specs = (P("req", "seq", "cfg"), P("req", "seq", "cfg"))
    return jax.shard_map(
        per_device, mesh=mesh, in_specs=in_specs, out_specs=out_specs, check_vma=False
    )
```

```python
import functools
import math

import jax
import jax.numpy as jnp
import numpy as np
from jax import lax
from jax.experimental import pallas as pl
from jax.experimental.pallas import tpu as pltpu
from jax.sharding import PartitionSpec as P

STEPS = 28
GUIDANCE = 3.0
SHIFT = 3.0
SCALE = 1.0 / math.sqrt(128.0)
EPSILON = 1e-06
HEAD = 128
BF16 = jnp.bfloat16
F32 = jnp.float32
MIB = 1024 * 1024


def noise_level(index):
    fraction = 1.0 - index.astype(jnp.float32) / STEPS
    return SHIFT * fraction / (SHIFT * fraction + 1.0 - fraction)


def lane_frequencies():
    rows = np.zeros((3, HEAD), np.float32)
    lane = 0
    for component, axis_span in ((0, 16), (1, 56), (2, 56)):
        pair_ids = np.arange(axis_span // 2, dtype=np.float32)
        frequency = np.exp(-(2.0 * pair_ids / axis_span) * np.float32(math.log(10000.0)))
        rows[component, lane : lane + axis_span] = np.repeat(frequency, 2)
        lane += axis_span
    return rows


def seq_grid(count):
    columns = 2 ** ((count.bit_length() - 1) // 2)
    return count // columns, columns


def send_x(block, step):
    if step == 0:
        return block
    high, wide = seq_grid(lax.axis_size("seq"))
    route = [(y * wide + x, y * wide + (x + step) % wide) for y in range(high) for x in range(wide)]
    return lax.ppermute(block, "seq", route)


def send_y(block, step):
    if step == 0:
        return block
    high, wide = seq_grid(lax.axis_size("seq"))
    route = [(y * wide + x, (y + step) % high * wide + x) for y in range(high) for x in range(wide)]
    return lax.ppermute(block, "seq", route)


def send_seq(block, dy, dx):
    if dy == 0 and dx == 0:
        return block
    high, wide = seq_grid(lax.axis_size("seq"))
    route = [
        (y * wide + x, (y + dy) % high * wide + (x + dx) % wide)
        for y in range(high)
        for x in range(wide)
    ]
    return lax.ppermute(block, "seq", route)


def send_z(block, step):
    if step == 0:
        return block
    count = lax.axis_size("req")
    return lax.ppermute(block, "req", [(r, (r + step) % count) for r in range(count)])


def swap_core(block):
    return lax.ppermute(block, "cfg", [(0, 1), (1, 0)])


def take(array, start, size, axis):
    return lax.dynamic_slice_in_dim(array, start, size, axis)


def dot(left, right):
    return jnp.dot(left, right, preferred_element_type=jnp.float32)


def hbm_spec():
    return pl.BlockSpec(memory_space=pl.ANY)


def place_of(step_x, step_y=0):
    high, wide = seq_grid(lax.axis_size("seq"))
    seq = lax.axis_index("seq")
    return lax.rem(seq // wide + high - step_y, high) * wide + x_of(step_x)


def x_of(step):
    wide = seq_grid(lax.axis_size("seq"))[1]
    return lax.rem(lax.axis_index("seq") % wide + 2 * wide - step, wide)


def z_of(step):
    count = lax.axis_size("req")
    return lax.rem(lax.axis_index("req") + count - step, count)


def whole_spec():
    return pl.BlockSpec(memory_space=pltpu.VMEM)


def smem_spec():
    return pl.BlockSpec(memory_space=pltpu.SMEM)


def cost(flops, moved):
    return pl.CostEstimate(flops=int(flops), bytes_accessed=int(moved), transcendentals=0)


def params():
    return pltpu.CompilerParams(vmem_limit_bytes=60 * MIB)


def rotate_kernel(kv_ref, pos_ref, freq_ref, out_ref):
    rows, width = kv_ref.shape[1:]
    row_ids = lax.broadcasted_iota(jnp.int32, (rows, HEAD), 0)
    angles = jnp.zeros((rows, HEAD), F32)
    for row in range(rows):
        line = (
            pos_ref[0, 0, row].astype(F32) * freq_ref[0:1, :]
            + pos_ref[1, 0, row].astype(F32) * freq_ref[1:2, :]
            + pos_ref[2, 0, row].astype(F32) * freq_ref[2:3, :]
        )
        angles = jnp.where(row_ids == row, line, angles)
    cosine, sine = jnp.cos(angles), jnp.sin(angles)
    even = lax.broadcasted_iota(jnp.int32, (rows, HEAD), 1) % 2 == 0
    out_ref[...] = jnp.zeros_like(out_ref)
    for first in range(0, width, HEAD):
        keys = kv_ref[0, :, first : first + HEAD].astype(F32)
        after = pltpu.roll(keys, HEAD - 1, 1)
        before = pltpu.roll(keys, 1, 1)
        rotated = cosine * keys + sine * jnp.where(even, -after, before)
        out_ref[0, 0:rows, first : first + HEAD] = rotated.astype(BF16)
    out_ref[1, 0:rows, :] = kv_ref[1]


def rotate_fresh(fresh, positions, padded):
    width = fresh.shape[2]
    return pl.pallas_call(
        rotate_kernel,
        out_shape=jax.ShapeDtypeStruct((2, padded, width), BF16),
        in_specs=[whole_spec(), smem_spec(), whole_spec()],
        out_specs=whole_spec(),
        compiler_params=params(),
        cost_estimate=cost(10**6, fresh.size * 4),
    )(fresh, positions, jnp.asarray(lane_frequencies()))


def attention_kernel(around, lengths_ref, slots_ref, q_ref, text_ref, image_ref, *refs):
    pieces = len(around)
    fresh_refs, (out_ref, fresh_ref) = refs[:pieces], refs[pieces:]
    padded = fresh_refs[0].shape[1]
    for i in range(pieces):
        fresh_ref[:, i * padded : (i + 1) * padded, :] = fresh_refs[i][...]
    slots = image_ref.shape[1]
    count = slots_ref.shape[1] // pieces
    length = lengths_ref[lax.axis_index("req")]
    key_ids = lax.broadcasted_iota(jnp.int32, (1, slots), 1)
    fresh_ids = lax.broadcasted_iota(jnp.int32, (1, pieces * padded), 1)
    image_bias = jnp.where(key_ids < length, 0.0, -jnp.inf)
    fresh_bias = jnp.full(fresh_ids.shape, -jnp.inf, F32)
    for i, (dy, dx) in enumerate(around):
        first = place_of(dx, dy) * count
        for j in range(count):
            slot = slots_ref[0, first + j]
            image_bias = jnp.where(key_ids == slot, -jnp.inf, image_bias)
            here = (fresh_ids == i * padded + j) & (slot < length)
            fresh_bias = jnp.where(here, 0.0, fresh_bias)
    over_lanes = (((1,), (1,)), ((), ()))
    for first in range(0, q_ref.shape[1], HEAD):
        head = slice(first, first + HEAD)
        query = q_ref[:, head]

        def scores(keys):
            return lax.dot_general(query, keys, over_lanes, preferred_element_type=F32) * SCALE

        text = scores(text_ref[0, :, head])
        image = scores(image_ref[0, :, head]) + image_bias
        fresh = scores(fresh_ref[0, :, head]) + fresh_bias
        best = jnp.maximum(
            jnp.max(text, axis=1, keepdims=True),
            jnp.maximum(
                jnp.max(image, axis=1, keepdims=True), jnp.max(fresh, axis=1, keepdims=True)
            ),
        )
        text, image, fresh = jnp.exp(text - best), jnp.exp(image - best), jnp.exp(fresh - best)
        total = (
            jnp.sum(text, axis=1, keepdims=True)
            + jnp.sum(image, axis=1, keepdims=True)
            + jnp.sum(fresh, axis=1, keepdims=True)
        )
        mixed = (
            dot(text.astype(BF16), text_ref[1, :, head])
            + dot(image.astype(BF16), image_ref[1, :, head])
            + dot(fresh.astype(BF16), fresh_ref[1, :, head])
        )
        out_ref[0, :, head] = (mixed / total).astype(BF16)


def attention(around, lengths, slot_ids, query, text_kv, image_kv, fresh):
    rows, width = query.shape
    group = 3 * HEAD
    groups = width // group
    text, slots = text_kv.shape[1], image_kv.shape[1]
    pieces, padded = len(fresh), fresh[0].shape[1]
    return pl.pallas_call(
        functools.partial(attention_kernel, around),
        grid=(groups,),
        out_shape=jax.ShapeDtypeStruct((groups, rows, group), BF16),
        in_specs=[
            smem_spec(),
            smem_spec(),
            pl.BlockSpec((rows, group), lambda g: (0, g)),
            pl.BlockSpec((2, text, group), lambda g: (0, 0, g)),
            pl.BlockSpec((2, slots, group), lambda g: (0, 0, g)),
        ]
        + [pl.BlockSpec((2, padded, group), lambda g: (0, 0, g))] * pieces,
        out_specs=pl.BlockSpec((1, rows, group), lambda g: (g, 0, 0)),
        scratch_shapes=[pltpu.VMEM((2, padded * pieces, group), BF16)],
        compiler_params=params(),
        cost_estimate=cost(4 * query.size * (text + slots), 2 * (text_kv.size + image_kv.size)),
    )(lengths, slot_ids, query, text_kv, image_kv, *fresh)


def residual_kernel(requests, around, *refs):
    pieces = len(around)
    attended, refs = refs[:requests], refs[requests:]
    own_ref, mine, refs = refs[0], refs[1:pieces], refs[pieces:]
    swapped_ref, stream_ref, mod_ref, out_ref, rows_ref = refs
    row_count = attended[0].shape[1]
    depth, width = own_ref.shape
    half_width = width // 2
    cfg, req = lax.axis_index("cfg"), lax.axis_index("req")
    places = [place_of(dx, dy) for dy, dx in around]
    for j in range(requests):
        first = pl.multiple_of(z_of(j) * row_count, 16)
        rows_ref[:, pl.ds(first, row_count), :] = attended[j][...]
    at = pl.multiple_of(req * width, 128)
    gates = [mod_ref[cfg, q, 0:1, pl.ds(at, width)] for q in range(requests)]

    def columns(core):
        for role, half in ((0, core), (1, 1 - core)):
            lanes = slice(half * half_width, (half + 1) * half_width)
            total = dot(rows_ref[places[0]], own_ref[:, lanes])
            for k in range(1, pieces):
                piece = swapped_ref[(k - 1) * depth : k * depth, :] if role else mine[k - 1][...]
                total += dot(rows_ref[places[k]], piece)
            for q in range(requests):
                out_ref[q, :, lanes] = (
                    stream_ref[0, q, :, lanes].astype(F32)
                    + gates[q][:, lanes] * total[q * row_count : (q + 1) * row_count]
                ).astype(BF16)

    pl.when(cfg == 0)(functools.partial(columns, 0))
    pl.when(cfg == 1)(functools.partial(columns, 1))


def residual_columns(around, attended, own, mine, swapped, stream, modulation):
    requests, pieces = len(attended), len(mine) + 1
    segments, row_count, seg = attended[0].shape
    return pl.pallas_call(
        functools.partial(residual_kernel, requests, around),
        out_shape=jax.ShapeDtypeStruct(stream.shape[1:], BF16),
        in_specs=[whole_spec()] * (requests + pieces + 3),
        out_specs=whole_spec(),
        scratch_shapes=[pltpu.VMEM((segments, requests * row_count, seg), BF16)],
        compiler_params=params(),
        cost_estimate=cost(2 * stream.size * own.shape[0] * pieces, 8 * stream.size),
    )(*attended, own, *mine, swapped, stream, modulation)


def copies_of(pieces, buffer, sems):
    cfg = lax.axis_index("cfg")
    copies = []
    for k, (kind, parts) in enumerate(pieces):
        for h in range(2):
            slot = h
            if kind == "core":
                slot = cfg if h == 0 else 1 - cfg
            copies.append(
                (h, pltpu.make_async_copy(parts[h], buffer.at[slot, k], sems.at[slot, k]))
            )
    return [copy for h in range(2) for half, copy in copies if half == h]


def up_kernel(requests, around, kinds, *refs):
    blocks, refs = refs[:requests], refs[requests:]
    mod_ref, refs = refs[0], refs[1:]
    pieces = []
    for kind in kinds:
        pieces.append((kind, refs[:2]))
        refs = refs[2:]
    out_refs, (own_ref, rows_ref, buffer, sems) = refs[:2], refs[2:]
    row_count, width = blocks[0].shape[1:]
    depth, hidden = buffer.shape[2:]
    cfg, req = lax.axis_index("cfg"), lax.axis_index("req")
    scale_of_mean = 1.0 / (requests * width)
    for copy in copies_of(pieces, buffer, sems):
        copy.start()
    for q in range(requests):
        total = jnp.zeros((row_count, 1), F32)
        for block in blocks:
            total += jnp.sum(block[q].astype(F32), axis=1, keepdims=True)
        average = total * scale_of_mean
        total = jnp.zeros((row_count, 1), F32)
        for block in blocks:
            centered = block[q].astype(F32) - average
            total += jnp.sum(centered * centered, axis=1, keepdims=True)
        inverse = lax.rsqrt(total * scale_of_mean + EPSILON)
        for dz, block in enumerate(blocks):
            place = z_of(dz)
            at = pl.ds(pl.multiple_of(place * width, 128), width)
            scale = 1.0 + mod_ref[cfg, q, 2:3, at]
            shift = mod_ref[cfg, q, 1:2, at]
            normed = (block[q].astype(F32) - average) * inverse * scale + shift
            normed = normed.astype(BF16)
            for i in range(width // depth):
                rows_ref[
                    place * (width // depth) + i, q * row_count : (q + 1) * row_count, :
                ] = normed[:, i * depth : (i + 1) * depth]
    for dz, block in enumerate(blocks):
        at = pl.ds(pl.multiple_of(z_of(dz) * width, 128), width)
        own_ref[:, at] = block[req]
    step = 256 if hidden % 256 == 0 else hidden
    for h in range(2):
        for c in range(hidden // step):
            total = None
            for k, (dy, dx) in enumerate(around):
                if c == 0:
                    source = pieces[k][1][0]
                    pltpu.make_async_copy(source, buffer.at[h, k], sems.at[h, k]).wait()
                weight = buffer[h, k, :, c * step : (c + 1) * step]
                term = dot(rows_ref[place_of(dx, dy)], weight)
                total = term if total is None else total + term
            out_refs[h][:, c * step : (c + 1) * step] = jax.nn.gelu(
                total, approximate=True
            ).astype(BF16)


def up_products(around, blocks, modulation, pieces):
    requests = len(blocks)
    row_count, slice_width = blocks[0].shape[1:]
    model = requests * slice_width
    depth, hidden = pieces[0][1][0].shape[-2:]
    rows = requests * row_count
    operands = [part for _, parts in pieces for part in parts]
    return pl.pallas_call(
        functools.partial(up_kernel, requests, around, [kind for kind, _ in pieces]),
        out_shape=(
            jax.ShapeDtypeStruct((rows, hidden), BF16),
            jax.ShapeDtypeStruct((rows, hidden), BF16),
            jax.ShapeDtypeStruct((row_count, model), BF16),
        ),
        in_specs=[whole_spec()] * (requests + 1) + [hbm_spec()] * len(operands),
        out_specs=(whole_spec(),) * 3,
        scratch_shapes=[
            pltpu.VMEM((model // depth, rows, depth), BF16),
            pltpu.VMEM((2, len(pieces), depth, hidden), BF16),
            pltpu.SemaphoreType.DMA((2, len(pieces))),
        ],
        compiler_params=params(),
        cost_estimate=cost(4 * rows * model * hidden, 4 * model * hidden),
    )(*blocks, modulation, *operands)


def begin_kernel(wide, *refs):
    acts, (weight_ref, out_ref, buffer, sems) = refs[: 2 * wide], refs[2 * wide :]
    rows, depth = acts[0].shape
    width = weight_ref.shape[1]
    copies = []
    for h in range(2):
        first = pl.multiple_of((2 * x_of(0) + h) * depth, 16)
        source = weight_ref.at[pl.ds(first, depth), :]
        copies.append(pltpu.make_async_copy(source, buffer.at[h], sems.at[h]))
        copies[h].start()
    for h in range(2):
        copies[h].wait()
    step = 256 if width % 256 == 0 else width
    for c in range(width // step):
        lanes = slice(c * step, (c + 1) * step)
        total = None
        for h in range(2):
            left = jnp.concatenate([act[...] for act in acts[h::2]], axis=0)
            term = dot(left, buffer[h, :, lanes])
            total = term if total is None else total + term
        for e in range(wide):
            out_ref[e, :, lanes] = total[e * rows : (e + 1) * rows]


def begin_down(acts, weight):
    wide, (rows, depth), width = len(acts), acts[0][0].shape, weight.shape[1]
    return pl.pallas_call(
        functools.partial(begin_kernel, wide),
        out_shape=jax.ShapeDtypeStruct((wide, rows, width), F32),
        in_specs=[whole_spec()] * (2 * wide) + [hbm_spec()],
        out_specs=whole_spec(),
        scratch_shapes=[
            pltpu.VMEM((2, depth, width), BF16),
            pltpu.SemaphoreType.DMA((2,)),
        ],
        compiler_params=params(),
        cost_estimate=cost(4 * wide * rows * depth * width, 4 * depth * width),
    )(*[half for act in acts for half in act], weight)


def end_kernel(requests, block, steps, weights, *refs):
    acts, refs = refs[: 2 * len(steps)], refs[2 * len(steps) :]
    weight_refs, refs = refs[:weights], refs[weights:]
    begun_refs, refs = refs[:weights], refs[weights:]
    out_refs, (scratch_ref, buffer, sems) = refs[:requests], refs[requests:]
    rows, depth = acts[0].shape
    width = weight_refs[0].shape[1]
    copies = []
    for w, weight_ref in enumerate(weight_refs):
        for k, far in enumerate(steps):
            for h in range(2):
                first = pl.multiple_of((2 * x_of(far) + h) * depth, 16)
                source = weight_ref.at[pl.ds(first, depth), :]
                target = buffer.at[w, k, h]
                copies.append(pltpu.make_async_copy(source, target, sems.at[w, k, h]))
                copies[-1].start()
    step = 256 if width % 256 == 0 else width
    for w in range(weights):
        for copy in copies[w * 2 * len(steps) : (w + 1) * 2 * len(steps)]:
            copy.wait()
        for c in range(width // step):
            lanes = slice(c * step, (c + 1) * step)
            total = begun_refs[w][block, :, lanes]
            for k in range(len(steps)):
                for h in range(2):
                    total += dot(acts[2 * k + h][...], buffer[w, k, h, :, lanes])
            scratch_ref[...] = total
            at = slice(w * width + c * step, w * width + (c + 1) * step)
            row_count = rows // requests
            for dz in range(requests):
                first = pl.multiple_of(z_of(requests - dz) * row_count, 16)
                out_refs[dz][:, at] = scratch_ref[pl.ds(first, row_count), :].astype(BF16)


def end_down(block, acts, steps, weights, begun, requests):
    (rows, depth), width = acts[0][0].shape, weights[0].shape[1]
    count = len(weights)
    step = 256 if width % 256 == 0 else width
    shape = (rows // requests, width * count)
    return pl.pallas_call(
        functools.partial(end_kernel, requests, block, steps, count),
        out_shape=tuple(jax.ShapeDtypeStruct(shape, BF16) for _ in range(requests)),
        in_specs=[whole_spec()] * (2 * len(acts))
        + [hbm_spec()] * count
        + [whole_spec()] * count,
        out_specs=tuple(whole_spec() for _ in range(requests)),
        scratch_shapes=[
            pltpu.VMEM((rows, step), F32),
            pltpu.VMEM((count, len(steps), 2, depth, width), BF16),
            pltpu.SemaphoreType.DMA((count, len(steps), 2)),
        ],
        compiler_params=params(),
        cost_estimate=cost(4 * count * rows * depth * width, 4 * count * depth * width),
    )(*[half for act in acts for half in act], *weights, *begun)


def far_kernel(requests, wide, *refs):
    acts, refs = refs[: 2 * wide * wide], refs[2 * wide * wide :]
    weight_refs, out_refs = refs[:2], refs[2 : 2 + requests]
    scratch_ref, buffer, sems = refs[2 + requests :]
    rows, depth = acts[0].shape
    row_count = rows // requests
    width = buffer.shape[2]
    cfg = lax.axis_index("cfg")
    for w, weight in enumerate(weight_refs):
        for i in range(wide):
            slot = (cfg if w == 0 else 1 - cfg) * wide + i
            source = weight.at[pl.ds(i * depth, depth), :]
            pltpu.make_async_copy(source, buffer.at[slot], sems.at[slot]).start()
    step = 256 if width % 256 == 0 else width
    for c in range(width // step):
        lanes = slice(c * step, (c + 1) * step)
        total = None
        for far in range(wide):
            for h in range(2):
                slot = 2 * x_of(far) + h
                if c == 0:
                    source = weight_refs[0].at[pl.ds(0, depth), :]
                    pltpu.make_async_copy(source, buffer.at[slot], sems.at[slot]).wait()
                left = jnp.concatenate(
                    [acts[2 * ((e - far) % wide * wide + far) + h][...] for e in range(wide)],
                    axis=0,
                )
                term = dot(left, buffer[slot, :, lanes])
                total = term if total is None else total + term
        scratch_ref[...] = total
        for dz, out_ref in enumerate(out_refs):
            for e in range(wide):
                first = e * rows + z_of(requests - dz) * row_count
                first = pl.multiple_of(first, 16)
                out_ref[e, :, lanes] = scratch_ref[pl.ds(first, row_count), :].astype(BF16)


def far_down(acts, mine, other, requests):
    rows, depth = acts[0][0].shape
    wide = math.isqrt(len(acts))
    width = mine.shape[1]
    step = 256 if width % 256 == 0 else width
    shape = (wide, rows // requests, width)
    return pl.pallas_call(
        functools.partial(far_kernel, requests, wide),
        out_shape=tuple(jax.ShapeDtypeStruct(shape, BF16) for _ in range(requests)),
        in_specs=[whole_spec()] * (2 * len(acts)) + [hbm_spec()] * 2,
        out_specs=tuple(whole_spec() for _ in range(requests)),
        scratch_shapes=[
            pltpu.VMEM((wide * rows, step), F32),
            pltpu.VMEM((2 * wide, depth, width), BF16),
            pltpu.SemaphoreType.DMA((2 * wide,)),
        ],
        compiler_params=params(),
        cost_estimate=cost(4 * len(acts) * rows * depth * width, 4 * wide * depth * width),
    )(*[half for act in acts for half in act], mine, other)


def per_device(
    queries,
    text_cache,
    image_cache,
    fresh_kv,
    fresh_slots,
    fresh_pos,
    image_len,
    stream,
    modulation,
    out_weight,
    up_weight,
    down_weight,
    final_weight,
    latent,
    step_index,
):
    cfg_id = lax.axis_index("cfg")
    req_id = lax.axis_index("req")
    seq_id = lax.axis_index("seq")
    requests = lax.axis_size("req")
    high, wide = seq_grid(lax.axis_size("seq"))
    y_id, x_id = seq_id // wide, seq_id % wide
    around = [(dy, dx) for dy in range(high) for dx in range(wide)]

    def x_from(step):
        return (x_id - step) % wide

    def y_from(step):
        return (y_id - step) % high

    def seq_from(dy, dx):
        return y_from(dy) * wide + x_from(dx)

    fresh_count = fresh_kv.shape[3]
    padded = -(-fresh_count // 16) * 16
    fresh_pair = rotate_fresh(fresh_kv[0, 0], fresh_pos, padded)
    fresh = [send_seq(fresh_pair, dy, dx) for dy, dx in around]

    out_rows, col_count = out_weight.shape
    seg = col_count // 2
    own_out, _ = lax.optimization_barrier((out_weight, fresh_pair))
    own_out = take(own_out, cfg_id * seg, seg, 1)
    out_y = [send_y(own_out, dy) for dy in range(high)]
    out_x = [send_x(own_out, dx) for dx in range(wide)]

    up_rows, hidden = up_weight.shape
    hidden_x = hidden // wide
    hidden_half = hidden_x // 2
    early_up, _ = lax.optimization_barrier((up_weight, fresh_pair))
    to_x = []
    for dx in range(wide):
        first = (x_id + dx) % wide * hidden_x + cfg_id * hidden_half
        to_x.append(take(early_up, first, hidden_half, 1))
    to_x, out_x, out_y, fresh = lax.optimization_barrier((to_x, out_x, out_y, fresh))
    up_x = [send_x(part, dx) for dx, part in enumerate(to_x)]
    up_y = [send_y(up_x[0], dy) for dy in range(high)]
    out_mine = [send_x(out_y[dy], dx) if dy else out_x[dx] for dy, dx in around]

    length = lax.dynamic_index_in_dim(image_len, req_id, 0, keepdims=False)
    attended = attention(
        around,
        image_len,
        fresh_slots,
        queries[0, 0],
        text_cache[0, 0],
        image_cache[0, 0],
        fresh,
    )
    row_count = queries.shape[2]
    if attended.shape[2] != out_rows:
        attended = jnp.transpose(attended, (1, 0, 2)).reshape(row_count, -1, out_rows)
        attended = jnp.transpose(attended, (1, 0, 2))
    attended_all = [send_z(attended, dz) for dz in range(requests)]
    out_mine, _, late_up = lax.optimization_barrier((out_mine, attended, up_weight))
    fetched = jnp.concatenate(out_mine[1:], axis=0)
    swapped = swap_core(fetched)
    own_up = [
        take(late_up, x_id * hidden_x + h * hidden_half, hidden_half, 1) for h in range(2)
    ]

    attended_all, swapped, up_x, up_y = lax.optimization_barrier(
        (attended_all, swapped, up_x, up_y)
    )
    other_y = [swap_core(part) for part in up_y[1:]]
    residual = residual_columns(
        around,
        attended_all,
        out_weight,
        out_mine[1:],
        swapped,
        stream,
        modulation,
    )
    along_z = [send_z(residual, dz) for dz in range(requests)]

    up_x[1:], other_y, _ = lax.optimization_barrier((up_x[1:], other_y, residual))
    other_x = [swap_core(part) for part in up_x[1:]]
    up_mine = [send_y(up_x[dx], dy) if dx else up_y[dy] for dy, dx in around]

    along_z[0] = residual
    forward = {(dz, dx): send_x(along_z[dz], dx) for dz in range(2) for dx in range(1, wide)}

    down_cols = down_weight.shape[1]
    down_half = hidden // 2
    own_down = take(down_weight, cfg_id * down_half, down_half, 0)
    along_z, forward, other_x, up_mine, own_down = lax.optimization_barrier(
        (along_z, forward, other_x, up_mine, own_down)
    )
    for dx in range(1, wide):
        for dz in range(requests):
            if (dz, dx) not in forward:
                forward[dz, dx] = send_x(along_z[dz], dx)
    blocks = [along_z]
    blocks += [[forward[dz, dx] for dz in range(requests)] for dx in range(1, wide)]
    down_mine = [send_y(own_down, dy) for dy in range(1, high)]
    up_pieces = [("halves", own_up)]
    for part, (dy, dx) in zip(up_mine[1:], around[1:]):
        if dy and dx:
            up_pieces.append(("core", [part, swap_core(part)]))
        else:
            up_pieces.append(("core", [part, other_y[dy - 1] if dy else other_x[dx - 1]]))

    acts, own_rows = [], []
    for dx in range(wide):
        if acts:
            blocks[dx], acts[-1] = lax.optimization_barrier((blocks[dx], acts[-1]))
        *act, own = up_products(around, blocks[dx], modulation, up_pieces)
        own_rows.append(own.astype(F32))
        acts += [[send_x(half, step) for half in act] for step in range(wide)]

    own_acts = acts[::wide]
    steps = list(range(1, wide))

    def parts_of(e):
        return [acts[(e - step) % wide * wide + step] for step in steps]

    def sent(share):
        return [send_z(part, dz) for dz, part in enumerate(share)]

    begun = [begin_down(own_acts, down_weight)]
    shares = [None] * wide
    last = parts_of(0)
    for e in steps:
        shares[e] = sent(end_down(e, parts_of(e), steps, [down_weight], begun, requests))
        last[-1][1], shares[e] = lax.optimization_barrier((last[-1][1], shares[e]))
    shares[0] = sent(end_down(0, last, steps, [down_weight], begun, requests))
    down_mine, acts[-1][0] = lax.optimization_barrier((down_mine, acts[-1][0]))
    far_shares = [sent(far_down(acts, mine, swap_core(mine), requests)) for mine in down_mine]

    mod_half = lax.dynamic_index_in_dim(modulation, cfg_id, 0, keepdims=False)
    gate_two = lax.dynamic_index_in_dim(mod_half[:, 3, :], req_id, 0, keepdims=False)

    def summed(parts):
        total = parts[0].astype(F32)
        for part in parts[1:]:
            total += part.astype(F32)
        return total

    def finished(total, rows, dy):
        col = seq_from(dy, 0) * down_cols
        block_out = (
            take(rows, col, down_cols, 1) + take(gate_two, col, down_cols, 0)[None, :] * total
        ).astype(BF16)
        return dot(block_out, take(final_weight, col, down_cols, 0))

    velocity = [finished(summed(shares[e]), own_rows[e], 0) for e in range(wide)]
    for dy, share in enumerate(far_shares, 1):
        total = summed(share)
        for e in range(wide):
            velocity[e] += finished(total[e], own_rows[e], dy)

    channels = final_weight.shape[1]
    cfg_count = lax.axis_size("cfg")
    halves = []
    for dc in range(2):
        share = 0.0
        for e in range(wide):
            block = velocity[e].reshape(row_count // 2, 2, channels)
            block = lax.dynamic_index_in_dim(block, cfg_id ^ dc, 1, keepdims=False)
            if dc or e:
                route = [
                    ((c * high + y) * wide + x, ((c ^ dc) * high + y) * wide + (x - e) % wide)
                    for c in range(cfg_count)
                    for y in range(high)
                    for x in range(wide)
                ]
                block = lax.ppermute(block, ("cfg", "seq"), route)
            share += block
        halves.append(share)
    cond_part = jnp.where(cfg_id == 0, halves[0], halves[1])
    uncond_part = jnp.where(cfg_id == 0, halves[1], halves[0])
    guided = uncond_part + GUIDANCE * (cond_part - uncond_part)
    level_now = noise_level(step_index[0])
    level_next = noise_level(step_index[0] + 1)
    token_ids = (
        seq_id * row_count
        + 2 * jnp.arange(row_count // 2, dtype=jnp.int32)[:, None]
        + cfg_id
        + jnp.zeros((1, channels), jnp.int32)
    )
    valid = token_ids < length
    current = latent[0]
    latent_next = jnp.where(valid, current + (level_next - level_now) * guided, current)
    denoised = jnp.where(valid, current - level_now * guided, current)
    return (latent_next[None], denoised[None])


def solution(mesh):
    in_specs = (
        P("cfg", "req", "seq", None),
        P("cfg", "req", None, None, None),
        P("cfg", "req", None, None, None),
        P("cfg", "req", None, "seq", None),
        P("req", None),
        P(None, "req", "seq"),
        P(),
        P("cfg", None, "seq", "req"),
        P(),
        P("seq", "req"),
        P("seq", "req"),
        P("req", "seq"),
        P(),
        P("req", "seq", "cfg"),
        P(),
    )
    out_specs = (P("req", "seq", "cfg"), P("req", "seq", "cfg"))
    return jax.shard_map(
        per_device, mesh=mesh, in_specs=in_specs, out_specs=out_specs, check_vma=False
    )
```

```python
import functools
import math

import jax
import jax.numpy as jnp
import numpy as np
from jax import lax
from jax.experimental import pallas as pl
from jax.experimental.pallas import tpu as pltpu
from jax.sharding import PartitionSpec as P

STEPS = 28
GUIDANCE = 3.0
SHIFT = 3.0
SCALE = 1.0 / math.sqrt(128.0)
EPSILON = 1e-06
HEAD = 128
BF16 = jnp.bfloat16
F32 = jnp.float32
MIB = 1024 * 1024


def noise_level(index):
    fraction = 1.0 - index.astype(jnp.float32) / STEPS
    return SHIFT * fraction / (SHIFT * fraction + 1.0 - fraction)


def lane_frequencies():
    rows = np.zeros((3, HEAD), np.float32)
    lane = 0
    for component, axis_span in ((0, 16), (1, 56), (2, 56)):
        pair_ids = np.arange(axis_span // 2, dtype=np.float32)
        frequency = np.exp(-(2.0 * pair_ids / axis_span) * np.float32(math.log(10000.0)))
        rows[component, lane : lane + axis_span] = np.repeat(frequency, 2)
        lane += axis_span
    return rows


def seq_grid(count):
    columns = 2 ** ((count.bit_length() - 1) // 2)
    return count // columns, columns


def send_x(block, step):
    if step == 0:
        return block
    high, wide = seq_grid(lax.axis_size("seq"))
    route = [(y * wide + x, y * wide + (x + step) % wide) for y in range(high) for x in range(wide)]
    return lax.ppermute(block, "seq", route)


def send_y(block, step):
    if step == 0:
        return block
    high, wide = seq_grid(lax.axis_size("seq"))
    route = [(y * wide + x, (y + step) % high * wide + x) for y in range(high) for x in range(wide)]
    return lax.ppermute(block, "seq", route)


def send_seq(block, dy, dx):
    if dy == 0 and dx == 0:
        return block
    high, wide = seq_grid(lax.axis_size("seq"))
    route = [
        (y * wide + x, (y + dy) % high * wide + (x + dx) % wide)
        for y in range(high)
        for x in range(wide)
    ]
    return lax.ppermute(block, "seq", route)


def send_z(block, step):
    if step == 0:
        return block
    count = lax.axis_size("req")
    return lax.ppermute(block, "req", [(r, (r + step) % count) for r in range(count)])


def swap_core(block):
    return lax.ppermute(block, "cfg", [(0, 1), (1, 0)])


def take(array, start, size, axis):
    return lax.dynamic_slice_in_dim(array, start, size, axis)


def dot(left, right):
    return jnp.dot(left, right, preferred_element_type=jnp.float32)


def hbm_spec():
    return pl.BlockSpec(memory_space=pl.ANY)


def place_of(step_x, step_y=0):
    high, wide = seq_grid(lax.axis_size("seq"))
    seq = lax.axis_index("seq")
    return lax.rem(seq // wide + high - step_y, high) * wide + x_of(step_x)


def x_of(step):
    wide = seq_grid(lax.axis_size("seq"))[1]
    return lax.rem(lax.axis_index("seq") % wide + 2 * wide - step, wide)


def z_of(step):
    count = lax.axis_size("req")
    return lax.rem(lax.axis_index("req") + count - step, count)


def whole_spec():
    return pl.BlockSpec(memory_space=pltpu.VMEM)


def smem_spec():
    return pl.BlockSpec(memory_space=pltpu.SMEM)


def cost(flops, moved):
    return pl.CostEstimate(flops=int(flops), bytes_accessed=int(moved), transcendentals=0)


def params():
    return pltpu.CompilerParams(vmem_limit_bytes=60 * MIB)


def rotate_kernel(kv_ref, pos_ref, freq_ref, out_ref):
    rows, width = kv_ref.shape[1:]
    row_ids = lax.broadcasted_iota(jnp.int32, (rows, HEAD), 0)
    angles = jnp.zeros((rows, HEAD), F32)
    for row in range(rows):
        line = (
            pos_ref[0, 0, row].astype(F32) * freq_ref[0:1, :]
            + pos_ref[1, 0, row].astype(F32) * freq_ref[1:2, :]
            + pos_ref[2, 0, row].astype(F32) * freq_ref[2:3, :]
        )
        angles = jnp.where(row_ids == row, line, angles)
    cosine, sine = jnp.cos(angles), jnp.sin(angles)
    even = lax.broadcasted_iota(jnp.int32, (rows, HEAD), 1) % 2 == 0
    out_ref[...] = jnp.zeros_like(out_ref)
    for first in range(0, width, HEAD):
        keys = kv_ref[0, :, first : first + HEAD].astype(F32)
        after = pltpu.roll(keys, HEAD - 1, 1)
        before = pltpu.roll(keys, 1, 1)
        rotated = cosine * keys + sine * jnp.where(even, -after, before)
        out_ref[0, 0:rows, first : first + HEAD] = rotated.astype(BF16)
    out_ref[1, 0:rows, :] = kv_ref[1]


def rotate_fresh(fresh, positions, padded):
    width = fresh.shape[2]
    return pl.pallas_call(
        rotate_kernel,
        out_shape=jax.ShapeDtypeStruct((2, padded, width), BF16),
        in_specs=[whole_spec(), smem_spec(), whole_spec()],
        out_specs=whole_spec(),
        compiler_params=params(),
    )(fresh, positions, jnp.asarray(lane_frequencies()))


def attention_kernel(around, lengths_ref, slots_ref, q_ref, text_ref, image_ref, *refs):
    pieces = len(around)
    fresh_refs, (out_ref, fresh_ref) = refs[:pieces], refs[pieces:]
    padded = fresh_refs[0].shape[1]
    for i in range(pieces):
        fresh_ref[:, i * padded : (i + 1) * padded, :] = fresh_refs[i][...]
    slots = image_ref.shape[1]
    count = slots_ref.shape[1] // pieces
    length = lengths_ref[lax.axis_index("req")]
    key_ids = lax.broadcasted_iota(jnp.int32, (1, slots), 1)
    fresh_ids = lax.broadcasted_iota(jnp.int32, (1, pieces * padded), 1)
    image_bias = jnp.where(key_ids < length, 0.0, -jnp.inf)
    fresh_bias = jnp.full(fresh_ids.shape, -jnp.inf, F32)
    for i, (dy, dx) in enumerate(around):
        first = place_of(dx, dy) * count
        for j in range(count):
            slot = slots_ref[0, first + j]
            image_bias = jnp.where(key_ids == slot, -jnp.inf, image_bias)
            here = (fresh_ids == i * padded + j) & (slot < length)
            fresh_bias = jnp.where(here, 0.0, fresh_bias)
    over_lanes = (((1,), (1,)), ((), ()))
    for first in range(0, q_ref.shape[1], HEAD):
        head = slice(first, first + HEAD)
        query = q_ref[:, head]

        def scores(keys):
            return lax.dot_general(query, keys, over_lanes, preferred_element_type=F32) * SCALE

        text = scores(text_ref[0, :, head])
        image = scores(image_ref[0, :, head]) + image_bias
        fresh = scores(fresh_ref[0, :, head]) + fresh_bias
        best = jnp.maximum(
            jnp.max(text, axis=1, keepdims=True),
            jnp.maximum(
                jnp.max(image, axis=1, keepdims=True), jnp.max(fresh, axis=1, keepdims=True)
            ),
        )
        text, image, fresh = jnp.exp(text - best), jnp.exp(image - best), jnp.exp(fresh - best)
        total = (
            jnp.sum(text, axis=1, keepdims=True)
            + jnp.sum(image, axis=1, keepdims=True)
            + jnp.sum(fresh, axis=1, keepdims=True)
        )
        mixed = (
            dot(text.astype(BF16), text_ref[1, :, head])
            + dot(image.astype(BF16), image_ref[1, :, head])
            + dot(fresh.astype(BF16), fresh_ref[1, :, head])
        )
        out_ref[0, :, head] = (mixed / total).astype(BF16)


def attention(around, lengths, slot_ids, query, text_kv, image_kv, fresh):
    rows, width = query.shape
    group = 3 * HEAD
    groups = width // group
    text, slots = text_kv.shape[1], image_kv.shape[1]
    pieces, padded = len(fresh), fresh[0].shape[1]
    return pl.pallas_call(
        functools.partial(attention_kernel, around),
        grid=(groups,),
        out_shape=jax.ShapeDtypeStruct((groups, rows, group), BF16),
        in_specs=[
            smem_spec(),
            smem_spec(),
            pl.BlockSpec((rows, group), lambda g: (0, g)),
            pl.BlockSpec((2, text, group), lambda g: (0, 0, g)),
            pl.BlockSpec((2, slots, group), lambda g: (0, 0, g)),
        ]
        + [pl.BlockSpec((2, padded, group), lambda g: (0, 0, g))] * pieces,
        out_specs=pl.BlockSpec((1, rows, group), lambda g: (g, 0, 0)),
        scratch_shapes=[pltpu.VMEM((2, padded * pieces, group), BF16)],
        compiler_params=params(),
    )(lengths, slot_ids, query, text_kv, image_kv, *fresh)


def residual_kernel(requests, around, *refs):
    pieces = len(around)
    attended, refs = refs[:requests], refs[requests:]
    own_ref, mine, refs = refs[0], refs[1:pieces], refs[pieces:]
    swapped_ref, stream_ref, mod_ref, out_ref, rows_ref = refs
    row_count = attended[0].shape[1]
    depth, width = own_ref.shape
    half_width = width // 2
    cfg, req = lax.axis_index("cfg"), lax.axis_index("req")
    places = [place_of(dx, dy) for dy, dx in around]
    for j in range(requests):
        first = pl.multiple_of(z_of(j) * row_count, 16)
        rows_ref[:, pl.ds(first, row_count), :] = attended[j][...]
    at = pl.multiple_of(req * width, 128)
    gates = [mod_ref[cfg, q, 0:1, pl.ds(at, width)] for q in range(requests)]

    def columns(core):
        for role, half in ((0, core), (1, 1 - core)):
            lanes = slice(half * half_width, (half + 1) * half_width)
            total = dot(rows_ref[places[0]], own_ref[:, lanes])
            for k in range(1, pieces):
                piece = swapped_ref[(k - 1) * depth : k * depth, :] if role else mine[k - 1][...]
                total += dot(rows_ref[places[k]], piece)
            for q in range(requests):
                out_ref[q, :, lanes] = (
                    stream_ref[0, q, :, lanes].astype(F32)
                    + gates[q][:, lanes] * total[q * row_count : (q + 1) * row_count]
                ).astype(BF16)

    pl.when(cfg == 0)(functools.partial(columns, 0))
    pl.when(cfg == 1)(functools.partial(columns, 1))


def residual_columns(around, attended, own, mine, swapped, stream, modulation):
    requests, pieces = len(attended), len(mine) + 1
    segments, row_count, seg = attended[0].shape
    return pl.pallas_call(
        functools.partial(residual_kernel, requests, around),
        out_shape=jax.ShapeDtypeStruct(stream.shape[1:], BF16),
        in_specs=[whole_spec()] * (requests + pieces + 3),
        out_specs=whole_spec(),
        scratch_shapes=[pltpu.VMEM((segments, requests * row_count, seg), BF16)],
        compiler_params=params(),
    )(*attended, own, *mine, swapped, stream, modulation)


def copies_of(pieces, buffer, sems):
    cfg = lax.axis_index("cfg")
    copies = []
    for k, (kind, parts) in enumerate(pieces):
        for h in range(2):
            slot = h
            if kind == "core":
                slot = cfg if h == 0 else 1 - cfg
            copies.append(
                (h, pltpu.make_async_copy(parts[h], buffer.at[slot, k], sems.at[slot, k]))
            )
    return [copy for h in range(2) for half, copy in copies if half == h]


def up_kernel(requests, around, kinds, *refs):
    blocks, refs = refs[:requests], refs[requests:]
    mod_ref, refs = refs[0], refs[1:]
    pieces = []
    for kind in kinds:
        pieces.append((kind, refs[:2]))
        refs = refs[2:]
    out_ref, own_ref, rows_ref, buffer, sems = refs
    row_count, width = blocks[0].shape[1:]
    depth, hidden = buffer.shape[2:]
    cfg, req = lax.axis_index("cfg"), lax.axis_index("req")
    scale_of_mean = 1.0 / (requests * width)
    for copy in copies_of(pieces, buffer, sems):
        copy.start()
    for q in range(requests):
        total = jnp.zeros((row_count, 1), F32)
        for block in blocks:
            total += jnp.sum(block[q].astype(F32), axis=1, keepdims=True)
        average = total * scale_of_mean
        total = jnp.zeros((row_count, 1), F32)
        for block in blocks:
            centered = block[q].astype(F32) - average
            total += jnp.sum(centered * centered, axis=1, keepdims=True)
        inverse = lax.rsqrt(total * scale_of_mean + EPSILON)
        for dz, block in enumerate(blocks):
            place = z_of(dz)
            at = pl.ds(pl.multiple_of(place * width, 128), width)
            scale = 1.0 + mod_ref[cfg, q, 2:3, at]
            shift = mod_ref[cfg, q, 1:2, at]
            normed = (block[q].astype(F32) - average) * inverse * scale + shift
            normed = normed.astype(BF16)
            for i in range(width // depth):
                rows_ref[
                    place * (width // depth) + i, q * row_count : (q + 1) * row_count, :
                ] = normed[:, i * depth : (i + 1) * depth]
    for dz, block in enumerate(blocks):
        at = pl.ds(pl.multiple_of(z_of(dz) * width, 128), width)
        own_ref[:, at] = block[req]
    step = 256 if hidden % 256 == 0 else hidden
    for h in range(2):
        for c in range(hidden // step):
            total = None
            for k, (dy, dx) in enumerate(around):
                if c == 0:
                    source = pieces[k][1][0]
                    pltpu.make_async_copy(source, buffer.at[h, k], sems.at[h, k]).wait()
                weight = buffer[h, k, :, c * step : (c + 1) * step]
                term = dot(rows_ref[place_of(dx, dy)], weight)
                total = term if total is None else total + term
            out_ref[h, :, c * step : (c + 1) * step] = jax.nn.gelu(
                total, approximate=True
            ).astype(BF16)


def up_products(around, blocks, modulation, pieces):
    requests = len(blocks)
    row_count, slice_width = blocks[0].shape[1:]
    model = requests * slice_width
    depth, hidden = pieces[0][1][0].shape[-2:]
    rows = requests * row_count
    operands = [part for _, parts in pieces for part in parts]
    return pl.pallas_call(
        functools.partial(up_kernel, requests, around, [kind for kind, _ in pieces]),
        out_shape=(
            jax.ShapeDtypeStruct((2, rows, hidden), BF16),
            jax.ShapeDtypeStruct((row_count, model), BF16),
        ),
        in_specs=[whole_spec()] * (requests + 1) + [hbm_spec()] * len(operands),
        out_specs=(whole_spec(), whole_spec()),
        scratch_shapes=[
            pltpu.VMEM((model // depth, rows, depth), BF16),
            pltpu.VMEM((2, len(pieces), depth, hidden), BF16),
            pltpu.SemaphoreType.DMA((2, len(pieces))),
        ],
        compiler_params=params(),
        cost_estimate=cost(8 * rows * model * hidden, 8 * model * hidden),
    )(*blocks, modulation, *operands)


def down_kernel(requests, wide, blocks, weights, *refs):
    acts, refs = refs[: wide * len(blocks)], refs[wide * len(blocks) :]
    weight_refs, refs = refs[:weights], refs[weights:]
    out_refs, (scratch_ref, buffer, sems) = refs[:requests], refs[requests:]
    rows, depth = acts[0].shape[1:]
    row_count = rows // requests
    width = buffer.shape[2]
    share = 2 * wide // weights
    for w, weight in enumerate(weight_refs):
        for i in range(share):
            slot = i
            if weights > 1:
                cfg = lax.axis_index("cfg")
                slot = (cfg if w == 0 else 1 - cfg) * share + i
            source = weight.at[pl.ds(i * depth, depth), :]
            pltpu.make_async_copy(source, buffer.at[slot], sems.at[slot]).start()
    step = 256 if width % 256 == 0 else width
    for c in range(width // step):
        lanes = slice(c * step, (c + 1) * step)
        total = None
        for far in range(wide):
            for h in range(2):
                slot = 2 * x_of(far) + h
                if c == 0:
                    source = weight_refs[0].at[pl.ds(0, depth), :]
                    pltpu.make_async_copy(source, buffer.at[slot], sems.at[slot]).wait()
                left = [acts[b * wide + far][h] for b in range(len(blocks))]
                left = jnp.concatenate(left, axis=0) if len(left) > 1 else left[0]
                term = dot(left, buffer[slot, :, lanes])
                total = term if total is None else total + term
        scratch_ref[...] = total
        for dz, out_ref in enumerate(out_refs):
            for b in range(len(blocks)):
                first = pl.multiple_of(b * rows + z_of(requests - dz) * row_count, 16)
                out_ref[b, :, lanes] = scratch_ref[pl.ds(first, row_count), :].astype(BF16)


def down_products(blocks, acts, weights, requests):
    rows, depth = acts[0].shape[1:]
    wide = math.isqrt(len(acts))
    width = weights[0].shape[1]
    step = 256 if width % 256 == 0 else width
    shape = (len(blocks), rows // requests, width)
    used = [acts[(e - far) % wide * wide + far] for e in blocks for far in range(wide)]
    return pl.pallas_call(
        functools.partial(down_kernel, requests, wide, blocks, len(weights)),
        out_shape=tuple(jax.ShapeDtypeStruct(shape, BF16) for _ in range(requests)),
        in_specs=[whole_spec()] * len(used) + [hbm_spec()] * len(weights),
        out_specs=tuple(whole_spec() for _ in range(requests)),
        scratch_shapes=[
            pltpu.VMEM((len(blocks) * rows, step), F32),
            pltpu.VMEM((2 * wide, depth, width), BF16),
            pltpu.SemaphoreType.DMA((2 * wide,)),
        ],
        compiler_params=params(),
        cost_estimate=cost(4 * len(used) * rows * depth * width, 4 * wide * depth * width),
    )(*used, *weights)


def per_device(
    queries,
    text_cache,
    image_cache,
    fresh_kv,
    fresh_slots,
    fresh_pos,
    image_len,
    stream,
    modulation,
    out_weight,
    up_weight,
    down_weight,
    final_weight,
    latent,
    step_index,
):
    cfg_id = lax.axis_index("cfg")
    req_id = lax.axis_index("req")
    seq_id = lax.axis_index("seq")
    requests = lax.axis_size("req")
    high, wide = seq_grid(lax.axis_size("seq"))
    y_id, x_id = seq_id // wide, seq_id % wide
    around = [(dy, dx) for dy in range(high) for dx in range(wide)]

    def x_from(step):
        return (x_id - step) % wide

    def y_from(step):
        return (y_id - step) % high

    def seq_from(dy, dx):
        return y_from(dy) * wide + x_from(dx)

    fresh_count = fresh_kv.shape[3]
    padded = -(-fresh_count // 16) * 16
    fresh_pair = rotate_fresh(fresh_kv[0, 0], fresh_pos, padded)
    fresh = [send_seq(fresh_pair, dy, dx) for dy, dx in around]

    out_rows, col_count = out_weight.shape
    seg = col_count // 2
    own_out, _ = lax.optimization_barrier((out_weight, fresh_pair))
    own_out = take(own_out, cfg_id * seg, seg, 1)
    out_y = [send_y(own_out, dy) for dy in range(high)]
    out_x = [send_x(own_out, dx) for dx in range(wide)]

    up_rows, hidden = up_weight.shape
    hidden_x = hidden // wide
    hidden_half = hidden_x // 2
    early_up, _ = lax.optimization_barrier((up_weight, fresh_pair))
    to_x = []
    for dx in range(wide):
        first = (x_id + dx) % wide * hidden_x + cfg_id * hidden_half
        to_x.append(take(early_up, first, hidden_half, 1))
    to_x, out_x, out_y, fresh = lax.optimization_barrier((to_x, out_x, out_y, fresh))
    up_x = [send_x(part, dx) for dx, part in enumerate(to_x)]
    up_y = [send_y(up_x[0], dy) for dy in range(high)]
    out_mine = [send_y(out_x[dx], dy) if dx else out_y[dy] for dy, dx in around]

    length = lax.dynamic_index_in_dim(image_len, req_id, 0, keepdims=False)
    attended = attention(
        around,
        image_len,
        fresh_slots,
        queries[0, 0],
        text_cache[0, 0],
        image_cache[0, 0],
        fresh,
    )
    row_count = queries.shape[2]
    if attended.shape[2] != out_rows:
        attended = jnp.transpose(attended, (1, 0, 2)).reshape(row_count, -1, out_rows)
        attended = jnp.transpose(attended, (1, 0, 2))
    attended_all = [send_z(attended, dz) for dz in range(requests)]
    out_mine, attended, late_up = lax.optimization_barrier((out_mine, attended, up_weight))
    swapped = swap_core(jnp.concatenate(out_mine[1:], axis=0))
    own_up = [
        take(late_up, x_id * hidden_x + h * hidden_half, hidden_half, 1) for h in range(2)
    ]

    attended_all, swapped, up_x, up_y = lax.optimization_barrier(
        (attended_all, swapped, up_x, up_y)
    )
    other_y = [swap_core(part) for part in up_y[1:]]
    residual = residual_columns(
        around,
        attended_all,
        out_weight,
        out_mine[1:],
        swapped,
        stream,
        modulation,
    )
    along_z = [send_z(residual, dz) for dz in range(requests)]
    near = [send_x(residual, dx) for dx in range(wide)]

    up_x[1:], other_y, _ = lax.optimization_barrier((up_x[1:], other_y, residual))
    up_mine = [send_y(up_x[dx], dy) if dx else up_y[dy] for dy, dx in around]

    other_x = [swap_core(part) for part in up_x[1:]]

    down_cols = down_weight.shape[1]
    down_half = hidden // 2
    own_down = take(down_weight, cfg_id * down_half, down_half, 0)
    along_z, near, other_x, up_mine, own_down = lax.optimization_barrier(
        (along_z, near, other_x, up_mine, own_down)
    )
    blocks = [
        [send_x(block, dx) if dz else near[dx] for dz, block in enumerate(along_z)]
        for dx in range(wide)
    ]
    down_mine = [send_y(own_down, dy) for dy in range(1, high)]
    up_pieces = [("halves", own_up)]
    for part, (dy, dx) in zip(up_mine[1:], around[1:]):
        if dy and dx:
            other = swap_core(part)
        else:
            other = other_y[dy - 1] if dy else other_x[dx - 1]
        up_pieces.append(("core", [part, other]))

    acts, own_rows = [], []
    for dx in range(wide):
        if acts:
            blocks[dx], acts[0] = lax.optimization_barrier((blocks[dx], acts[0]))
        act, own = up_products(around, blocks[dx], modulation, up_pieces)
        own_rows.append(own.astype(F32))
        acts += [send_x(act, step) for step in range(wide)]

    def sent(share):
        return [send_z(part, dz) for dz, part in enumerate(share)]

    own_shares = [None] * wide
    for e in [*range(1, wide), 0]:
        share = down_products([e], acts, [down_weight], requests)
        own_shares[e] = sent(share)
        if e == 1:
            acts[-1], own_shares[e] = lax.optimization_barrier((acts[-1], own_shares[e]))
    down_mine, acts[-1] = lax.optimization_barrier((down_mine, acts[-1]))
    everything = list(range(wide))
    far_shares = [
        sent(down_products(everything, acts, [mine, swap_core(mine)], requests))
        for mine in down_mine
    ]

    mod_half = lax.dynamic_index_in_dim(modulation, cfg_id, 0, keepdims=False)
    gate_two = lax.dynamic_index_in_dim(mod_half[:, 3, :], req_id, 0, keepdims=False)

    def summed(parts):
        total = parts[0].astype(F32)
        for part in parts[1:]:
            total += part.astype(F32)
        return total

    def finished(total, rows, dy):
        col = seq_from(dy, 0) * down_cols
        block_out = (
            take(rows, col, down_cols, 1) + take(gate_two, col, down_cols, 0)[None, :] * total
        ).astype(BF16)
        return dot(block_out, take(final_weight, col, down_cols, 0))

    velocity = [finished(summed(own_shares[e])[0], own_rows[e], 0) for e in range(wide)]
    for dy, share in enumerate(far_shares, 1):
        total = summed(share)
        for e in range(wide):
            velocity[e] += finished(total[e], own_rows[e], dy)

    channels = final_weight.shape[1]
    cfg_count = lax.axis_size("cfg")
    halves = []
    for dc in range(2):
        share = 0.0
        for e in range(wide):
            block = velocity[e].reshape(row_count // 2, 2, channels)
            block = lax.dynamic_index_in_dim(block, cfg_id ^ dc, 1, keepdims=False)
            if dc or e:
                route = [
                    ((c * high + y) * wide + x, ((c ^ dc) * high + y) * wide + (x - e) % wide)
                    for c in range(cfg_count)
                    for y in range(high)
                    for x in range(wide)
                ]
                block = lax.ppermute(block, ("cfg", "seq"), route)
            share += block
        halves.append(share)
    cond_part = jnp.where(cfg_id == 0, halves[0], halves[1])
    uncond_part = jnp.where(cfg_id == 0, halves[1], halves[0])
    guided = uncond_part + GUIDANCE * (cond_part - uncond_part)
    level_now = noise_level(step_index[0])
    level_next = noise_level(step_index[0] + 1)
    token_ids = (
        seq_id * row_count
        + 2 * jnp.arange(row_count // 2, dtype=jnp.int32)[:, None]
        + cfg_id
        + jnp.zeros((1, channels), jnp.int32)
    )
    valid = token_ids < length
    current = latent[0]
    latent_next = jnp.where(valid, current + (level_next - level_now) * guided, current)
    denoised = jnp.where(valid, current - level_now * guided, current)
    return (latent_next[None], denoised[None])


def solution(mesh):
    in_specs = (
        P("cfg", "req", "seq", None),
        P("cfg", "req", None, None, None),
        P("cfg", "req", None, None, None),
        P("cfg", "req", None, "seq", None),
        P("req", None),
        P(None, "req", "seq"),
        P(),
        P("cfg", None, "seq", "req"),
        P(),
        P("seq", "req"),
        P("seq", "req"),
        P("req", "seq"),
        P(),
        P("req", "seq", "cfg"),
        P(),
    )
    out_specs = (P("req", "seq", "cfg"), P("req", "seq", "cfg"))
    return jax.shard_map(
        per_device, mesh=mesh, in_specs=in_specs, out_specs=out_specs, check_vma=False
    )
```

```python
import functools
import math

import jax
import jax.numpy as jnp
import numpy as np
from jax import lax
from jax.experimental import pallas as pl
from jax.experimental.pallas import tpu as pltpu
from jax.sharding import PartitionSpec as P

STEPS = 28
GUIDANCE = 3.0
SHIFT = 3.0
SCALE = 1.0 / math.sqrt(128.0)
EPSILON = 1e-06
HEAD = 128
BF16 = jnp.bfloat16
F32 = jnp.float32
MIB = 1024 * 1024


def noise_level(index):
    fraction = 1.0 - index.astype(jnp.float32) / STEPS
    return SHIFT * fraction / (SHIFT * fraction + 1.0 - fraction)


def lane_frequencies():
    rows = np.zeros((3, HEAD), np.float32)
    lane = 0
    for component, axis_span in ((0, 16), (1, 56), (2, 56)):
        pair_ids = np.arange(axis_span // 2, dtype=np.float32)
        frequency = np.exp(-(2.0 * pair_ids / axis_span) * np.float32(math.log(10000.0)))
        rows[component, lane : lane + axis_span] = np.repeat(frequency, 2)
        lane += axis_span
    return rows


def seq_grid(count):
    columns = 2 ** ((count.bit_length() - 1) // 2)
    return count // columns, columns


def send_x(block, step):
    if step == 0:
        return block
    high, wide = seq_grid(lax.axis_size("seq"))
    route = [(y * wide + x, y * wide + (x + step) % wide) for y in range(high) for x in range(wide)]
    return lax.ppermute(block, "seq", route)


def send_y(block, step):
    if step == 0:
        return block
    high, wide = seq_grid(lax.axis_size("seq"))
    route = [(y * wide + x, (y + step) % high * wide + x) for y in range(high) for x in range(wide)]
    return lax.ppermute(block, "seq", route)


def send_seq(block, dy, dx):
    if dy == 0 and dx == 0:
        return block
    high, wide = seq_grid(lax.axis_size("seq"))
    route = [
        (y * wide + x, (y + dy) % high * wide + (x + dx) % wide)
        for y in range(high)
        for x in range(wide)
    ]
    return lax.ppermute(block, "seq", route)


def send_z(block, step):
    if step == 0:
        return block
    count = lax.axis_size("req")
    return lax.ppermute(block, "req", [(r, (r + step) % count) for r in range(count)])


def swap_core(block):
    return lax.ppermute(block, "cfg", [(0, 1), (1, 0)])


def take(array, start, size, axis):
    return lax.dynamic_slice_in_dim(array, start, size, axis)


def dot(left, right):
    return jnp.dot(left, right, preferred_element_type=jnp.float32)


def hbm_spec():
    return pl.BlockSpec(memory_space=pl.ANY)


def place_of(step_x, step_y=0):
    high, wide = seq_grid(lax.axis_size("seq"))
    seq = lax.axis_index("seq")
    return lax.rem(seq // wide + high - step_y, high) * wide + x_of(step_x)


def x_of(step):
    wide = seq_grid(lax.axis_size("seq"))[1]
    return lax.rem(lax.axis_index("seq") % wide + 2 * wide - step, wide)


def z_of(step):
    count = lax.axis_size("req")
    return lax.rem(lax.axis_index("req") + count - step, count)


def whole_spec():
    return pl.BlockSpec(memory_space=pltpu.VMEM)


def smem_spec():
    return pl.BlockSpec(memory_space=pltpu.SMEM)


def cost(flops, moved):
    return pl.CostEstimate(flops=int(flops), bytes_accessed=int(moved), transcendentals=0)


def params():
    return pltpu.CompilerParams(vmem_limit_bytes=60 * MIB)


def rotate_kernel(kv_ref, pos_ref, freq_ref, out_ref):
    rows, width = kv_ref.shape[1:]
    row_ids = lax.broadcasted_iota(jnp.int32, (rows, HEAD), 0)
    angles = jnp.zeros((rows, HEAD), F32)
    for row in range(rows):
        line = (
            pos_ref[0, 0, row].astype(F32) * freq_ref[0:1, :]
            + pos_ref[1, 0, row].astype(F32) * freq_ref[1:2, :]
            + pos_ref[2, 0, row].astype(F32) * freq_ref[2:3, :]
        )
        angles = jnp.where(row_ids == row, line, angles)
    cosine, sine = jnp.cos(angles), jnp.sin(angles)
    even = lax.broadcasted_iota(jnp.int32, (rows, HEAD), 1) % 2 == 0
    out_ref[...] = jnp.zeros_like(out_ref)
    for first in range(0, width, HEAD):
        keys = kv_ref[0, :, first : first + HEAD].astype(F32)
        after = pltpu.roll(keys, HEAD - 1, 1)
        before = pltpu.roll(keys, 1, 1)
        rotated = cosine * keys + sine * jnp.where(even, -after, before)
        out_ref[0, 0:rows, first : first + HEAD] = rotated.astype(BF16)
    out_ref[1, 0:rows, :] = kv_ref[1]


def rotate_fresh(fresh, positions, padded):
    width = fresh.shape[2]
    return pl.pallas_call(
        rotate_kernel,
        out_shape=jax.ShapeDtypeStruct((2, padded, width), BF16),
        in_specs=[whole_spec(), smem_spec(), whole_spec()],
        out_specs=whole_spec(),
        compiler_params=params(),
    )(fresh, positions, jnp.asarray(lane_frequencies()))


def attention_kernel(around, lengths_ref, slots_ref, q_ref, text_ref, image_ref, *refs):
    pieces = len(around)
    fresh_refs, (out_ref, fresh_ref) = refs[:pieces], refs[pieces:]
    padded = fresh_refs[0].shape[1]
    for i in range(pieces):
        fresh_ref[:, i * padded : (i + 1) * padded, :] = fresh_refs[i][...]
    slots = image_ref.shape[1]
    count = slots_ref.shape[1] // pieces
    length = lengths_ref[lax.axis_index("req")]
    key_ids = lax.broadcasted_iota(jnp.int32, (1, slots), 1)
    fresh_ids = lax.broadcasted_iota(jnp.int32, (1, pieces * padded), 1)
    image_bias = jnp.where(key_ids < length, 0.0, -jnp.inf)
    fresh_bias = jnp.full(fresh_ids.shape, -jnp.inf, F32)
    for i, (dy, dx) in enumerate(around):
        first = place_of(dx, dy) * count
        for j in range(count):
            slot = slots_ref[0, first + j]
            image_bias = jnp.where(key_ids == slot, -jnp.inf, image_bias)
            here = (fresh_ids == i * padded + j) & (slot < length)
            fresh_bias = jnp.where(here, 0.0, fresh_bias)
    over_lanes = (((1,), (1,)), ((), ()))
    for first in range(0, q_ref.shape[1], HEAD):
        head = slice(first, first + HEAD)
        query = q_ref[:, head]

        def scores(keys):
            return lax.dot_general(query, keys, over_lanes, preferred_element_type=F32) * SCALE

        text = scores(text_ref[0, :, head])
        image = scores(image_ref[0, :, head]) + image_bias
        fresh = scores(fresh_ref[0, :, head]) + fresh_bias
        best = jnp.maximum(
            jnp.max(text, axis=1, keepdims=True),
            jnp.maximum(
                jnp.max(image, axis=1, keepdims=True), jnp.max(fresh, axis=1, keepdims=True)
            ),
        )
        text, image, fresh = jnp.exp(text - best), jnp.exp(image - best), jnp.exp(fresh - best)
        total = (
            jnp.sum(text, axis=1, keepdims=True)
            + jnp.sum(image, axis=1, keepdims=True)
            + jnp.sum(fresh, axis=1, keepdims=True)
        )
        mixed = (
            dot(text.astype(BF16), text_ref[1, :, head])
            + dot(image.astype(BF16), image_ref[1, :, head])
            + dot(fresh.astype(BF16), fresh_ref[1, :, head])
        )
        out_ref[0, :, head] = (mixed / total).astype(BF16)


def attention(around, lengths, slot_ids, query, text_kv, image_kv, fresh):
    rows, width = query.shape
    group = 3 * HEAD
    groups = width // group
    text, slots = text_kv.shape[1], image_kv.shape[1]
    pieces, padded = len(fresh), fresh[0].shape[1]
    return pl.pallas_call(
        functools.partial(attention_kernel, around),
        grid=(groups,),
        out_shape=jax.ShapeDtypeStruct((groups, rows, group), BF16),
        in_specs=[
            smem_spec(),
            smem_spec(),
            pl.BlockSpec((rows, group), lambda g: (0, g)),
            pl.BlockSpec((2, text, group), lambda g: (0, 0, g)),
            pl.BlockSpec((2, slots, group), lambda g: (0, 0, g)),
        ]
        + [pl.BlockSpec((2, padded, group), lambda g: (0, 0, g))] * pieces,
        out_specs=pl.BlockSpec((1, rows, group), lambda g: (g, 0, 0)),
        scratch_shapes=[pltpu.VMEM((2, padded * pieces, group), BF16)],
        compiler_params=params(),
    )(lengths, slot_ids, query, text_kv, image_kv, *fresh)


def residual_kernel(requests, around, *refs):
    pieces = len(around)
    attended, refs = refs[:requests], refs[requests:]
    own_ref, mine, refs = refs[0], refs[1:pieces], refs[pieces:]
    swapped_ref, stream_ref, mod_ref, out_ref, rows_ref = refs
    row_count = attended[0].shape[1]
    depth, width = own_ref.shape
    half_width = width // 2
    cfg, req = lax.axis_index("cfg"), lax.axis_index("req")
    places = [place_of(dx, dy) for dy, dx in around]
    for j in range(requests):
        first = pl.multiple_of(z_of(j) * row_count, 16)
        rows_ref[:, pl.ds(first, row_count), :] = attended[j][...]
    at = pl.multiple_of(req * width, 128)
    gates = [mod_ref[cfg, q, 0:1, pl.ds(at, width)] for q in range(requests)]

    def columns(core):
        for role, half in ((0, core), (1, 1 - core)):
            lanes = slice(half * half_width, (half + 1) * half_width)
            total = dot(rows_ref[places[0]], own_ref[:, lanes])
            for k in range(1, pieces):
                piece = swapped_ref[(k - 1) * depth : k * depth, :] if role else mine[k - 1][...]
                total += dot(rows_ref[places[k]], piece)
            for q in range(requests):
                out_ref[q, :, lanes] = (
                    stream_ref[0, q, :, lanes].astype(F32)
                    + gates[q][:, lanes] * total[q * row_count : (q + 1) * row_count]
                ).astype(BF16)

    pl.when(cfg == 0)(functools.partial(columns, 0))
    pl.when(cfg == 1)(functools.partial(columns, 1))


def residual_columns(around, attended, own, mine, swapped, stream, modulation):
    requests, pieces = len(attended), len(mine) + 1
    segments, row_count, seg = attended[0].shape
    return pl.pallas_call(
        functools.partial(residual_kernel, requests, around),
        out_shape=jax.ShapeDtypeStruct(stream.shape[1:], BF16),
        in_specs=[whole_spec()] * (requests + pieces + 3),
        out_specs=whole_spec(),
        scratch_shapes=[pltpu.VMEM((segments, requests * row_count, seg), BF16)],
        compiler_params=params(),
    )(*attended, own, *mine, swapped, stream, modulation)


def copies_of(pieces, buffer, sems):
    cfg = lax.axis_index("cfg")
    copies = []
    for k, (kind, parts) in enumerate(pieces):
        for h in range(2):
            slot = h
            if kind == "core":
                slot = cfg if h == 0 else 1 - cfg
            copies.append(
                (h, pltpu.make_async_copy(parts[h], buffer.at[slot, k], sems.at[slot, k]))
            )
    return [copy for h in range(2) for half, copy in copies if half == h]


def up_kernel(requests, around, kinds, *refs):
    blocks, refs = refs[:requests], refs[requests:]
    mod_ref, refs = refs[0], refs[1:]
    pieces = []
    for kind in kinds:
        pieces.append((kind, refs[:2]))
        refs = refs[2:]
    out_ref, own_ref, rows_ref, buffer, sems = refs
    row_count, width = blocks[0].shape[1:]
    depth, hidden = buffer.shape[2:]
    cfg, req = lax.axis_index("cfg"), lax.axis_index("req")
    scale_of_mean = 1.0 / (requests * width)
    for copy in copies_of(pieces, buffer, sems):
        copy.start()
    for q in range(requests):
        total = jnp.zeros((row_count, 1), F32)
        for block in blocks:
            total += jnp.sum(block[q].astype(F32), axis=1, keepdims=True)
        average = total * scale_of_mean
        total = jnp.zeros((row_count, 1), F32)
        for block in blocks:
            centered = block[q].astype(F32) - average
            total += jnp.sum(centered * centered, axis=1, keepdims=True)
        inverse = lax.rsqrt(total * scale_of_mean + EPSILON)
        for dz, block in enumerate(blocks):
            place = z_of(dz)
            at = pl.ds(pl.multiple_of(place * width, 128), width)
            scale = 1.0 + mod_ref[cfg, q, 2:3, at]
            shift = mod_ref[cfg, q, 1:2, at]
            normed = (block[q].astype(F32) - average) * inverse * scale + shift
            normed = normed.astype(BF16)
            for i in range(width // depth):
                rows_ref[
                    place * (width // depth) + i, q * row_count : (q + 1) * row_count, :
                ] = normed[:, i * depth : (i + 1) * depth]
    for dz, block in enumerate(blocks):
        at = pl.ds(pl.multiple_of(z_of(dz) * width, 128), width)
        own_ref[:, at] = block[req]
    step = 256 if hidden % 256 == 0 else hidden
    for h in range(2):
        for c in range(hidden // step):
            total = None
            for k, (dy, dx) in enumerate(around):
                if c == 0:
                    source = pieces[k][1][0]
                    pltpu.make_async_copy(source, buffer.at[h, k], sems.at[h, k]).wait()
                weight = buffer[h, k, :, c * step : (c + 1) * step]
                term = dot(rows_ref[place_of(dx, dy)], weight)
                total = term if total is None else total + term
            out_ref[h, :, c * step : (c + 1) * step] = jax.nn.gelu(
                total, approximate=True
            ).astype(BF16)


def up_products(around, blocks, modulation, pieces):
    requests = len(blocks)
    row_count, slice_width = blocks[0].shape[1:]
    model = requests * slice_width
    depth, hidden = pieces[0][1][0].shape[-2:]
    rows = requests * row_count
    operands = [part for _, parts in pieces for part in parts]
    return pl.pallas_call(
        functools.partial(up_kernel, requests, around, [kind for kind, _ in pieces]),
        out_shape=(
            jax.ShapeDtypeStruct((2, rows, hidden), BF16),
            jax.ShapeDtypeStruct((row_count, model), BF16),
        ),
        in_specs=[whole_spec()] * (requests + 1) + [hbm_spec()] * len(operands),
        out_specs=(whole_spec(), whole_spec()),
        scratch_shapes=[
            pltpu.VMEM((model // depth, rows, depth), BF16),
            pltpu.VMEM((2, len(pieces), depth, hidden), BF16),
            pltpu.SemaphoreType.DMA((2, len(pieces))),
        ],
        compiler_params=params(),
        cost_estimate=cost(8 * rows * model * hidden, 8 * model * hidden),
    )(*blocks, modulation, *operands)


def down_kernel(requests, wide, blocks, weights, earlier, *refs):
    acts, refs = refs[: wide * len(blocks)], refs[wide * len(blocks) :]
    weight_refs, refs = refs[:weights], refs[weights:]
    earlier_refs, refs = refs[: earlier * requests], refs[earlier * requests :]
    out_refs, (scratch_ref, buffer, sems) = refs[:requests], refs[requests:]
    rows, depth = acts[0].shape[1:]
    row_count = rows // requests
    width = buffer.shape[2]
    share = 2 * wide // weights
    for w, weight in enumerate(weight_refs):
        for i in range(share):
            slot = i
            if weights > 1:
                cfg = lax.axis_index("cfg")
                slot = (cfg if w == 0 else 1 - cfg) * share + i
            source = weight.at[pl.ds(i * depth, depth), :]
            pltpu.make_async_copy(source, buffer.at[slot], sems.at[slot]).start()
    for k, ref in enumerate(earlier_refs):
        out_refs[k % requests][len(blocks) + k // requests] = ref[0]
    step = 256 if width % 256 == 0 else width
    for c in range(width // step):
        lanes = slice(c * step, (c + 1) * step)
        total = None
        for far in range(wide):
            for h in range(2):
                slot = 2 * x_of(far) + h
                if c == 0:
                    source = weight_refs[0].at[pl.ds(0, depth), :]
                    pltpu.make_async_copy(source, buffer.at[slot], sems.at[slot]).wait()
                left = [acts[b * wide + far][h] for b in range(len(blocks))]
                left = jnp.concatenate(left, axis=0) if len(left) > 1 else left[0]
                term = dot(left, buffer[slot, :, lanes])
                total = term if total is None else total + term
        scratch_ref[...] = total
        for dz, out_ref in enumerate(out_refs):
            for b in range(len(blocks)):
                first = pl.multiple_of(b * rows + z_of(requests - dz) * row_count, 16)
                out_ref[b, :, lanes] = scratch_ref[pl.ds(first, row_count), :].astype(BF16)


def down_products(blocks, acts, weights, requests, earlier=()):
    rows, depth = acts[0].shape[1:]
    wide = math.isqrt(len(acts))
    width = weights[0].shape[1]
    step = 256 if width % 256 == 0 else width
    shape = (len(blocks) + len(earlier), rows // requests, width)
    done = [part for share in earlier for part in share]
    used = [acts[(e - far) % wide * wide + far] for e in blocks for far in range(wide)]
    return pl.pallas_call(
        functools.partial(down_kernel, requests, wide, blocks, len(weights), len(earlier)),
        out_shape=tuple(jax.ShapeDtypeStruct(shape, BF16) for _ in range(requests)),
        in_specs=[whole_spec()] * len(used)
        + [hbm_spec()] * len(weights)
        + [whole_spec()] * len(done),
        out_specs=tuple(whole_spec() for _ in range(requests)),
        scratch_shapes=[
            pltpu.VMEM((len(blocks) * rows, step), F32),
            pltpu.VMEM((2 * wide, depth, width), BF16),
            pltpu.SemaphoreType.DMA((2 * wide,)),
        ],
        compiler_params=params(),
        cost_estimate=cost(4 * len(used) * rows * depth * width, 4 * wide * depth * width),
    )(*used, *weights, *done)


def per_device(
    queries,
    text_cache,
    image_cache,
    fresh_kv,
    fresh_slots,
    fresh_pos,
    image_len,
    stream,
    modulation,
    out_weight,
    up_weight,
    down_weight,
    final_weight,
    latent,
    step_index,
):
    cfg_id = lax.axis_index("cfg")
    req_id = lax.axis_index("req")
    seq_id = lax.axis_index("seq")
    requests = lax.axis_size("req")
    high, wide = seq_grid(lax.axis_size("seq"))
    y_id, x_id = seq_id // wide, seq_id % wide
    around = [(dy, dx) for dy in range(high) for dx in range(wide)]

    def x_from(step):
        return (x_id - step) % wide

    def y_from(step):
        return (y_id - step) % high

    def seq_from(dy, dx):
        return y_from(dy) * wide + x_from(dx)

    fresh_count = fresh_kv.shape[3]
    padded = -(-fresh_count // 16) * 16
    fresh_pair = rotate_fresh(fresh_kv[0, 0], fresh_pos, padded)
    fresh = [send_seq(fresh_pair, dy, dx) for dy, dx in around]

    out_rows, col_count = out_weight.shape
    seg = col_count // 2
    own_out, _ = lax.optimization_barrier((out_weight, fresh_pair))
    own_out = take(own_out, cfg_id * seg, seg, 1)
    out_y = [send_y(own_out, dy) for dy in range(high)]
    out_x = [send_x(own_out, dx) for dx in range(wide)]

    up_rows, hidden = up_weight.shape
    hidden_x = hidden // wide
    hidden_half = hidden_x // 2
    early_up, _ = lax.optimization_barrier((up_weight, fresh_pair))
    to_x = []
    for dx in range(wide):
        first = (x_id + dx) % wide * hidden_x + cfg_id * hidden_half
        to_x.append(take(early_up, first, hidden_half, 1))
    to_x, out_x, out_y, fresh = lax.optimization_barrier((to_x, out_x, out_y, fresh))
    up_x = [send_x(part, dx) for dx, part in enumerate(to_x)]
    up_y = [send_y(up_x[0], dy) for dy in range(high)]
    out_mine = [send_y(out_x[dx], dy) if dx else out_y[dy] for dy, dx in around]

    length = lax.dynamic_index_in_dim(image_len, req_id, 0, keepdims=False)
    attended = attention(
        around,
        image_len,
        fresh_slots,
        queries[0, 0],
        text_cache[0, 0],
        image_cache[0, 0],
        fresh,
    )
    row_count = queries.shape[2]
    if attended.shape[2] != out_rows:
        attended = jnp.transpose(attended, (1, 0, 2)).reshape(row_count, -1, out_rows)
        attended = jnp.transpose(attended, (1, 0, 2))
    attended_all = [send_z(attended, dz) for dz in range(requests)]
    out_mine, attended, late_up = lax.optimization_barrier((out_mine, attended, up_weight))
    swapped = swap_core(jnp.concatenate(out_mine[1:], axis=0))
    own_up = [
        take(late_up, x_id * hidden_x + h * hidden_half, hidden_half, 1) for h in range(2)
    ]

    attended_all, swapped, up_x, up_y = lax.optimization_barrier(
        (attended_all, swapped, up_x, up_y)
    )
    other_y = [swap_core(part) for part in up_y[1:]]
    residual = residual_columns(
        around,
        attended_all,
        out_weight,
        out_mine[1:],
        swapped,
        stream,
        modulation,
    )
    along_z = [send_z(residual, dz) for dz in range(requests)]
    near = [send_x(residual, dx) for dx in range(wide)]

    up_x[1:], other_y, _ = lax.optimization_barrier((up_x[1:], other_y, residual))
    up_mine = [send_y(up_x[dx], dy) if dx else up_y[dy] for dy, dx in around]

    other_x = [swap_core(part) for part in up_x[1:]]

    down_cols = down_weight.shape[1]
    down_half = hidden // 2
    own_down = take(down_weight, cfg_id * down_half, down_half, 0)
    along_z, near, other_x, up_mine, own_up, own_down = lax.optimization_barrier(
        (along_z, near, other_x, up_mine, own_up, own_down)
    )
    blocks = [
        [send_x(block, dx) if dz else near[dx] for dz, block in enumerate(along_z)]
        for dx in range(wide)
    ]
    down_mine = [send_y(own_down, dy) for dy in range(1, high)]
    up_pieces = [("halves", own_up)]
    for part, (dy, dx) in zip(up_mine[1:], around[1:]):
        if dy and dx:
            other = swap_core(part)
        else:
            other = other_y[dy - 1] if dy else other_x[dx - 1]
        up_pieces.append(("core", [part, other]))

    acts, own_rows = [], []
    for dx in range(wide):
        if acts:
            blocks[dx], acts[0] = lax.optimization_barrier((blocks[dx], acts[0]))
        act, own = up_products(around, blocks[dx], modulation, up_pieces)
        own_rows.append(own.astype(F32))
        acts += [send_x(act, step) for step in range(wide)]

    def sent(share):
        return [send_z(part, dz) for dz, part in enumerate(share)]

    earlier = []
    for e in range(1, wide):
        earlier.append(down_products([e], acts, [down_weight], requests))
        if e == 1:
            acts[-1], earlier[0] = lax.optimization_barrier((acts[-1], earlier[0]))
    share = down_products([0], acts, [down_weight], requests, earlier)
    own_share = sent(share)
    down_mine, _ = lax.optimization_barrier((down_mine, share))
    everything = list(range(wide))
    far_parts = [
        down_products(everything, acts, [mine, swap_core(mine)], requests) for mine in down_mine
    ]
    far_shares = [sent(part) for part in far_parts]
    own_share, _ = lax.optimization_barrier((own_share, far_parts))

    mod_half = lax.dynamic_index_in_dim(modulation, cfg_id, 0, keepdims=False)
    gate_two = lax.dynamic_index_in_dim(mod_half[:, 3, :], req_id, 0, keepdims=False)

    def summed(parts):
        total = parts[0].astype(F32)
        for part in parts[1:]:
            total += part.astype(F32)
        return total

    def finished(total, rows, dy):
        col = seq_from(dy, 0) * down_cols
        block_out = (
            take(rows, col, down_cols, 1) + take(gate_two, col, down_cols, 0)[None, :] * total
        ).astype(BF16)
        return dot(block_out, take(final_weight, col, down_cols, 0))

    total = summed(own_share)
    velocity = [finished(total[e], own_rows[e], 0) for e in range(wide)]
    for dy, share in enumerate(far_shares, 1):
        total = summed(share)
        for e in range(wide):
            velocity[e] += finished(total[e], own_rows[e], dy)

    channels = final_weight.shape[1]
    cfg_count = lax.axis_size("cfg")
    halves = []
    for dc in range(2):
        share = 0.0
        for e in range(wide):
            block = velocity[e].reshape(row_count // 2, 2, channels)
            block = lax.dynamic_index_in_dim(block, cfg_id ^ dc, 1, keepdims=False)
            if dc or e:
                route = [
                    ((c * high + y) * wide + x, ((c ^ dc) * high + y) * wide + (x - e) % wide)
                    for c in range(cfg_count)
                    for y in range(high)
                    for x in range(wide)
                ]
                block = lax.ppermute(block, ("cfg", "seq"), route)
            share += block
        halves.append(share)
    cond_part = jnp.where(cfg_id == 0, halves[0], halves[1])
    uncond_part = jnp.where(cfg_id == 0, halves[1], halves[0])
    guided = uncond_part + GUIDANCE * (cond_part - uncond_part)
    level_now = noise_level(step_index[0])
    level_next = noise_level(step_index[0] + 1)
    token_ids = (
        seq_id * row_count
        + 2 * jnp.arange(row_count // 2, dtype=jnp.int32)[:, None]
        + cfg_id
        + jnp.zeros((1, channels), jnp.int32)
    )
    valid = token_ids < length
    current = latent[0]
    latent_next = jnp.where(valid, current + (level_next - level_now) * guided, current)
    denoised = jnp.where(valid, current - level_now * guided, current)
    return (latent_next[None], denoised[None])


def solution(mesh):
    in_specs = (
        P("cfg", "req", "seq", None),
        P("cfg", "req", None, None, None),
        P("cfg", "req", None, None, None),
        P("cfg", "req", None, "seq", None),
        P("req", None),
        P(None, "req", "seq"),
        P(),
        P("cfg", None, "seq", "req"),
        P(),
        P("seq", "req"),
        P("seq", "req"),
        P("req", "seq"),
        P(),
        P("req", "seq", "cfg"),
        P(),
    )
    out_specs = (P("req", "seq", "cfg"), P("req", "seq", "cfg"))
    return jax.shard_map(
        per_device, mesh=mesh, in_specs=in_specs, out_specs=out_specs, check_vma=False
    )
```

```python
import functools
import math

import jax
import jax.numpy as jnp
import numpy as np
from jax import lax
from jax.experimental import pallas as pl
from jax.experimental.pallas import tpu as pltpu
from jax.sharding import PartitionSpec as P

STEPS = 28
GUIDANCE = 3.0
SHIFT = 3.0
SCALE = 1.0 / math.sqrt(128.0)
EPSILON = 1e-06
HEAD = 128
BF16 = jnp.bfloat16
F32 = jnp.float32
MIB = 1024 * 1024


def noise_level(index):
    fraction = 1.0 - index.astype(jnp.float32) / STEPS
    return SHIFT * fraction / (SHIFT * fraction + 1.0 - fraction)


def lane_frequencies():
    rows = np.zeros((3, HEAD), np.float32)
    lane = 0
    for component, axis_span in ((0, 16), (1, 56), (2, 56)):
        pair_ids = np.arange(axis_span // 2, dtype=np.float32)
        frequency = np.exp(-(2.0 * pair_ids / axis_span) * np.float32(math.log(10000.0)))
        rows[component, lane : lane + axis_span] = np.repeat(frequency, 2)
        lane += axis_span
    return rows


def seq_grid(count):
    columns = 2 ** ((count.bit_length() - 1) // 2)
    return count // columns, columns


def send_x(block, step):
    if step == 0:
        return block
    high, wide = seq_grid(lax.axis_size("seq"))
    route = [(y * wide + x, y * wide + (x + step) % wide) for y in range(high) for x in range(wide)]
    return lax.ppermute(block, "seq", route)


def send_y(block, step):
    if step == 0:
        return block
    high, wide = seq_grid(lax.axis_size("seq"))
    route = [(y * wide + x, (y + step) % high * wide + x) for y in range(high) for x in range(wide)]
    return lax.ppermute(block, "seq", route)


def send_seq(block, dy, dx):
    if dy == 0 and dx == 0:
        return block
    high, wide = seq_grid(lax.axis_size("seq"))
    route = [
        (y * wide + x, (y + dy) % high * wide + (x + dx) % wide)
        for y in range(high)
        for x in range(wide)
    ]
    return lax.ppermute(block, "seq", route)


def send_z(block, step):
    if step == 0:
        return block
    count = lax.axis_size("req")
    return lax.ppermute(block, "req", [(r, (r + step) % count) for r in range(count)])


def swap_core(block):
    return lax.ppermute(block, "cfg", [(0, 1), (1, 0)])


def take(array, start, size, axis):
    return lax.dynamic_slice_in_dim(array, start, size, axis)


def dot(left, right):
    return jnp.dot(left, right, preferred_element_type=jnp.float32)


def hbm_spec():
    return pl.BlockSpec(memory_space=pl.ANY)


def place_of(step_x, step_y=0):
    high, wide = seq_grid(lax.axis_size("seq"))
    seq = lax.axis_index("seq")
    return lax.rem(seq // wide + high - step_y, high) * wide + x_of(step_x)


def x_of(step):
    wide = seq_grid(lax.axis_size("seq"))[1]
    return lax.rem(lax.axis_index("seq") % wide + 2 * wide - step, wide)


def z_of(step):
    count = lax.axis_size("req")
    return lax.rem(lax.axis_index("req") + count - step, count)


def whole_spec():
    return pl.BlockSpec(memory_space=pltpu.VMEM)


def smem_spec():
    return pl.BlockSpec(memory_space=pltpu.SMEM)


def cost(flops, moved):
    return pl.CostEstimate(flops=int(flops), bytes_accessed=int(moved), transcendentals=0)


def params():
    return pltpu.CompilerParams(vmem_limit_bytes=60 * MIB)


def rotate_kernel(kv_ref, pos_ref, freq_ref, out_ref):
    rows, width = kv_ref.shape[1:]
    row_ids = lax.broadcasted_iota(jnp.int32, (rows, HEAD), 0)
    angles = jnp.zeros((rows, HEAD), F32)
    for row in range(rows):
        line = (
            pos_ref[0, 0, row].astype(F32) * freq_ref[0:1, :]
            + pos_ref[1, 0, row].astype(F32) * freq_ref[1:2, :]
            + pos_ref[2, 0, row].astype(F32) * freq_ref[2:3, :]
        )
        angles = jnp.where(row_ids == row, line, angles)
    cosine, sine = jnp.cos(angles), jnp.sin(angles)
    even = lax.broadcasted_iota(jnp.int32, (rows, HEAD), 1) % 2 == 0
    out_ref[...] = jnp.zeros_like(out_ref)
    for first in range(0, width, HEAD):
        keys = kv_ref[0, :, first : first + HEAD].astype(F32)
        after = pltpu.roll(keys, HEAD - 1, 1)
        before = pltpu.roll(keys, 1, 1)
        rotated = cosine * keys + sine * jnp.where(even, -after, before)
        out_ref[0, 0:rows, first : first + HEAD] = rotated.astype(BF16)
    out_ref[1, 0:rows, :] = kv_ref[1]


def rotate_fresh(fresh, positions, padded):
    width = fresh.shape[2]
    return pl.pallas_call(
        rotate_kernel,
        out_shape=jax.ShapeDtypeStruct((2, padded, width), BF16),
        in_specs=[whole_spec(), smem_spec(), whole_spec()],
        out_specs=whole_spec(),
        compiler_params=params(),
    )(fresh, positions, jnp.asarray(lane_frequencies()))


def attention_kernel(around, lengths_ref, slots_ref, q_ref, text_ref, image_ref, *refs):
    pieces = len(around)
    fresh_refs, (out_ref, fresh_ref) = refs[:pieces], refs[pieces:]
    padded = fresh_refs[0].shape[1]
    for i in range(pieces):
        fresh_ref[:, i * padded : (i + 1) * padded, :] = fresh_refs[i][...]
    slots = image_ref.shape[1]
    count = slots_ref.shape[1] // pieces
    length = lengths_ref[lax.axis_index("req")]
    key_ids = lax.broadcasted_iota(jnp.int32, (1, slots), 1)
    fresh_ids = lax.broadcasted_iota(jnp.int32, (1, pieces * padded), 1)
    image_bias = jnp.where(key_ids < length, 0.0, -jnp.inf)
    fresh_bias = jnp.full(fresh_ids.shape, -jnp.inf, F32)
    for i, (dy, dx) in enumerate(around):
        first = place_of(dx, dy) * count
        for j in range(count):
            slot = slots_ref[0, first + j]
            image_bias = jnp.where(key_ids == slot, -jnp.inf, image_bias)
            here = (fresh_ids == i * padded + j) & (slot < length)
            fresh_bias = jnp.where(here, 0.0, fresh_bias)
    over_lanes = (((1,), (1,)), ((), ()))
    for first in range(0, q_ref.shape[1], HEAD):
        head = slice(first, first + HEAD)
        query = q_ref[:, head]

        def scores(keys):
            return lax.dot_general(query, keys, over_lanes, preferred_element_type=F32) * SCALE

        text = scores(text_ref[0, :, head])
        image = scores(image_ref[0, :, head]) + image_bias
        fresh = scores(fresh_ref[0, :, head]) + fresh_bias
        best = jnp.maximum(
            jnp.max(text, axis=1, keepdims=True),
            jnp.maximum(
                jnp.max(image, axis=1, keepdims=True), jnp.max(fresh, axis=1, keepdims=True)
            ),
        )
        text, image, fresh = jnp.exp(text - best), jnp.exp(image - best), jnp.exp(fresh - best)
        total = (
            jnp.sum(text, axis=1, keepdims=True)
            + jnp.sum(image, axis=1, keepdims=True)
            + jnp.sum(fresh, axis=1, keepdims=True)
        )
        mixed = (
            dot(text.astype(BF16), text_ref[1, :, head])
            + dot(image.astype(BF16), image_ref[1, :, head])
            + dot(fresh.astype(BF16), fresh_ref[1, :, head])
        )
        out_ref[0, :, head] = (mixed / total).astype(BF16)


def attention(around, lengths, slot_ids, query, text_kv, image_kv, fresh):
    rows, width = query.shape
    group = 3 * HEAD
    groups = width // group
    text, slots = text_kv.shape[1], image_kv.shape[1]
    pieces, padded = len(fresh), fresh[0].shape[1]
    return pl.pallas_call(
        functools.partial(attention_kernel, around),
        grid=(groups,),
        out_shape=jax.ShapeDtypeStruct((groups, rows, group), BF16),
        in_specs=[
            smem_spec(),
            smem_spec(),
            pl.BlockSpec((rows, group), lambda g: (0, g)),
            pl.BlockSpec((2, text, group), lambda g: (0, 0, g)),
            pl.BlockSpec((2, slots, group), lambda g: (0, 0, g)),
        ]
        + [pl.BlockSpec((2, padded, group), lambda g: (0, 0, g))] * pieces,
        out_specs=pl.BlockSpec((1, rows, group), lambda g: (g, 0, 0)),
        scratch_shapes=[pltpu.VMEM((2, padded * pieces, group), BF16)],
        compiler_params=params(),
    )(lengths, slot_ids, query, text_kv, image_kv, *fresh)


def residual_kernel(requests, around, *refs):
    pieces = len(around)
    attended, refs = refs[:requests], refs[requests:]
    own_ref, mine, refs = refs[0], refs[1:pieces], refs[pieces:]
    swapped_ref, stream_ref, mod_ref, out_ref, rows_ref = refs
    row_count = attended[0].shape[1]
    depth, width = own_ref.shape
    half_width = width // 2
    cfg, req = lax.axis_index("cfg"), lax.axis_index("req")
    places = [place_of(dx, dy) for dy, dx in around]
    for j in range(requests):
        first = pl.multiple_of(z_of(j) * row_count, 16)
        rows_ref[:, pl.ds(first, row_count), :] = attended[j][...]
    at = pl.multiple_of(req * width, 128)
    gates = [mod_ref[cfg, q, 0:1, pl.ds(at, width)] for q in range(requests)]

    def columns(core):
        for role, half in ((0, core), (1, 1 - core)):
            lanes = slice(half * half_width, (half + 1) * half_width)
            total = dot(rows_ref[places[0]], own_ref[:, lanes])
            for k in range(1, pieces):
                piece = swapped_ref[(k - 1) * depth : k * depth, :] if role else mine[k - 1][...]
                total += dot(rows_ref[places[k]], piece)
            for q in range(requests):
                out_ref[q, :, lanes] = (
                    stream_ref[0, q, :, lanes].astype(F32)
                    + gates[q][:, lanes] * total[q * row_count : (q + 1) * row_count]
                ).astype(BF16)

    pl.when(cfg == 0)(functools.partial(columns, 0))
    pl.when(cfg == 1)(functools.partial(columns, 1))


def residual_columns(around, attended, own, mine, swapped, stream, modulation):
    requests, pieces = len(attended), len(mine) + 1
    segments, row_count, seg = attended[0].shape
    return pl.pallas_call(
        functools.partial(residual_kernel, requests, around),
        out_shape=jax.ShapeDtypeStruct(stream.shape[1:], BF16),
        in_specs=[whole_spec()] * (requests + pieces + 3),
        out_specs=whole_spec(),
        scratch_shapes=[pltpu.VMEM((segments, requests * row_count, seg), BF16)],
        compiler_params=params(),
    )(*attended, own, *mine, swapped, stream, modulation)


def copies_of(pieces, buffer, sems):
    cfg = lax.axis_index("cfg")
    copies = []
    for k, (kind, parts) in enumerate(pieces):
        for h in range(2):
            slot = h
            if kind == "core":
                slot = cfg if h == 0 else 1 - cfg
            copies.append(
                (h, pltpu.make_async_copy(parts[h], buffer.at[slot, k], sems.at[slot, k]))
            )
    return [copy for h in range(2) for half, copy in copies if half == h]


def up_kernel(requests, around, kinds, *refs):
    blocks, refs = refs[:requests], refs[requests:]
    mod_ref, refs = refs[0], refs[1:]
    pieces = []
    for kind in kinds:
        pieces.append((kind, refs[:2]))
        refs = refs[2:]
    out_ref, own_ref, rows_ref, buffer, sems = refs
    row_count, width = blocks[0].shape[1:]
    depth, hidden = buffer.shape[2:]
    cfg, req = lax.axis_index("cfg"), lax.axis_index("req")
    scale_of_mean = 1.0 / (requests * width)
    for copy in copies_of(pieces, buffer, sems):
        copy.start()
    for q in range(requests):
        total = jnp.zeros((row_count, 1), F32)
        for block in blocks:
            total += jnp.sum(block[q].astype(F32), axis=1, keepdims=True)
        average = total * scale_of_mean
        total = jnp.zeros((row_count, 1), F32)
        for block in blocks:
            centered = block[q].astype(F32) - average
            total += jnp.sum(centered * centered, axis=1, keepdims=True)
        inverse = lax.rsqrt(total * scale_of_mean + EPSILON)
        for dz, block in enumerate(blocks):
            place = z_of(dz)
            at = pl.ds(pl.multiple_of(place * width, 128), width)
            scale = 1.0 + mod_ref[cfg, q, 2:3, at]
            shift = mod_ref[cfg, q, 1:2, at]
            normed = (block[q].astype(F32) - average) * inverse * scale + shift
            normed = normed.astype(BF16)
            for i in range(width // depth):
                rows_ref[
                    place * (width // depth) + i, q * row_count : (q + 1) * row_count, :
                ] = normed[:, i * depth : (i + 1) * depth]
    for dz, block in enumerate(blocks):
        at = pl.ds(pl.multiple_of(z_of(dz) * width, 128), width)
        own_ref[:, at] = block[req]
    step = 256 if hidden % 256 == 0 else hidden
    for h in range(2):
        for c in range(hidden // step):
            total = None
            for k, (dy, dx) in enumerate(around):
                if c == 0:
                    source = pieces[k][1][0]
                    pltpu.make_async_copy(source, buffer.at[h, k], sems.at[h, k]).wait()
                weight = buffer[h, k, :, c * step : (c + 1) * step]
                term = dot(rows_ref[place_of(dx, dy)], weight)
                total = term if total is None else total + term
            out_ref[h, :, c * step : (c + 1) * step] = jax.nn.gelu(
                total, approximate=True
            ).astype(BF16)


def up_products(around, blocks, modulation, pieces):
    requests = len(blocks)
    row_count, slice_width = blocks[0].shape[1:]
    model = requests * slice_width
    depth, hidden = pieces[0][1][0].shape[-2:]
    rows = requests * row_count
    operands = [part for _, parts in pieces for part in parts]
    return pl.pallas_call(
        functools.partial(up_kernel, requests, around, [kind for kind, _ in pieces]),
        out_shape=(
            jax.ShapeDtypeStruct((2, rows, hidden), BF16),
            jax.ShapeDtypeStruct((row_count, model), BF16),
        ),
        in_specs=[whole_spec()] * (requests + 1) + [hbm_spec()] * len(operands),
        out_specs=(whole_spec(), whole_spec()),
        scratch_shapes=[
            pltpu.VMEM((model // depth, rows, depth), BF16),
            pltpu.VMEM((2, len(pieces), depth, hidden), BF16),
            pltpu.SemaphoreType.DMA((2, len(pieces))),
        ],
        compiler_params=params(),
        cost_estimate=cost(8 * rows * model * hidden, 8 * model * hidden),
    )(*blocks, modulation, *operands)


def down_kernel(requests, wide, blocks, weights, earlier, *refs):
    acts, refs = refs[: wide * len(blocks)], refs[wide * len(blocks) :]
    weight_refs, refs = refs[:weights], refs[weights:]
    earlier_refs, refs = refs[: earlier * requests], refs[earlier * requests :]
    out_refs, (scratch_ref, buffer, sems) = refs[:requests], refs[requests:]
    rows, depth = acts[0].shape[1:]
    row_count = rows // requests
    width = buffer.shape[2]
    share = 2 * wide // weights
    for w, weight in enumerate(weight_refs):
        for i in range(share):
            slot = i
            if weights > 1:
                cfg = lax.axis_index("cfg")
                slot = (cfg if w == 0 else 1 - cfg) * share + i
            source = weight.at[pl.ds(i * depth, depth), :]
            pltpu.make_async_copy(source, buffer.at[slot], sems.at[slot]).start()
    for k, ref in enumerate(earlier_refs):
        out_refs[k % requests][len(blocks) + k // requests] = ref[0]
    step = 256 if width % 256 == 0 else width
    for c in range(width // step):
        lanes = slice(c * step, (c + 1) * step)
        total = None
        for far in range(wide):
            for h in range(2):
                slot = 2 * x_of(far) + h
                if c == 0:
                    source = weight_refs[0].at[pl.ds(0, depth), :]
                    pltpu.make_async_copy(source, buffer.at[slot], sems.at[slot]).wait()
                left = [acts[b * wide + far][h] for b in range(len(blocks))]
                left = jnp.concatenate(left, axis=0) if len(left) > 1 else left[0]
                term = dot(left, buffer[slot, :, lanes])
                total = term if total is None else total + term
        scratch_ref[...] = total
        for dz, out_ref in enumerate(out_refs):
            for b in range(len(blocks)):
                first = pl.multiple_of(b * rows + z_of(requests - dz) * row_count, 16)
                out_ref[b, :, lanes] = scratch_ref[pl.ds(first, row_count), :].astype(BF16)


def down_products(blocks, acts, weights, requests, earlier=()):
    rows, depth = acts[0].shape[1:]
    wide = math.isqrt(len(acts))
    width = weights[0].shape[1]
    step = 256 if width % 256 == 0 else width
    shape = (len(blocks) + len(earlier), rows // requests, width)
    done = [part for share in earlier for part in share]
    used = [acts[(e - far) % wide * wide + far] for e in blocks for far in range(wide)]
    return pl.pallas_call(
        functools.partial(down_kernel, requests, wide, blocks, len(weights), len(earlier)),
        out_shape=tuple(jax.ShapeDtypeStruct(shape, BF16) for _ in range(requests)),
        in_specs=[whole_spec()] * len(used)
        + [hbm_spec()] * len(weights)
        + [whole_spec()] * len(done),
        out_specs=tuple(whole_spec() for _ in range(requests)),
        scratch_shapes=[
            pltpu.VMEM((len(blocks) * rows, step), F32),
            pltpu.VMEM((2 * wide, depth, width), BF16),
            pltpu.SemaphoreType.DMA((2 * wide,)),
        ],
        compiler_params=params(),
        cost_estimate=cost(4 * len(used) * rows * depth * width, 4 * wide * depth * width),
    )(*used, *weights, *done)


def per_device(
    queries,
    text_cache,
    image_cache,
    fresh_kv,
    fresh_slots,
    fresh_pos,
    image_len,
    stream,
    modulation,
    out_weight,
    up_weight,
    down_weight,
    final_weight,
    latent,
    step_index,
):
    cfg_id = lax.axis_index("cfg")
    req_id = lax.axis_index("req")
    seq_id = lax.axis_index("seq")
    requests = lax.axis_size("req")
    high, wide = seq_grid(lax.axis_size("seq"))
    y_id, x_id = seq_id // wide, seq_id % wide
    around = [(dy, dx) for dy in range(high) for dx in range(wide)]

    def x_from(step):
        return (x_id - step) % wide

    def y_from(step):
        return (y_id - step) % high

    def seq_from(dy, dx):
        return y_from(dy) * wide + x_from(dx)

    fresh_count = fresh_kv.shape[3]
    padded = -(-fresh_count // 16) * 16
    fresh_pair = rotate_fresh(fresh_kv[0, 0], fresh_pos, padded)
    fresh = [send_seq(fresh_pair, dy, dx) for dy, dx in around]

    out_rows, col_count = out_weight.shape
    seg = col_count // 2
    own_out, _ = lax.optimization_barrier((out_weight, fresh_pair))
    own_out = take(own_out, cfg_id * seg, seg, 1)
    out_y = [send_y(own_out, dy) for dy in range(high)]
    out_x = [send_x(own_out, dx) for dx in range(wide)]

    up_rows, hidden = up_weight.shape
    hidden_x = hidden // wide
    hidden_half = hidden_x // 2
    early_up, _ = lax.optimization_barrier((up_weight, fresh_pair))
    to_x = []
    for dx in range(wide):
        first = (x_id + dx) % wide * hidden_x + cfg_id * hidden_half
        to_x.append(take(early_up, first, hidden_half, 1))
    to_x, out_x, out_y, fresh = lax.optimization_barrier((to_x, out_x, out_y, fresh))
    up_x = [send_x(part, dx) for dx, part in enumerate(to_x)]
    up_y = [send_y(up_x[0], dy) for dy in range(high)]
    out_mine = [send_y(out_x[dx], dy) if dx else out_y[dy] for dy, dx in around]

    length = lax.dynamic_index_in_dim(image_len, req_id, 0, keepdims=False)
    attended = attention(
        around,
        image_len,
        fresh_slots,
        queries[0, 0],
        text_cache[0, 0],
        image_cache[0, 0],
        fresh,
    )
    row_count = queries.shape[2]
    if attended.shape[2] != out_rows:
        attended = jnp.transpose(attended, (1, 0, 2)).reshape(row_count, -1, out_rows)
        attended = jnp.transpose(attended, (1, 0, 2))
    attended_all = [send_z(attended, dz) for dz in range(requests)]
    out_mine, attended, late_up = lax.optimization_barrier((out_mine, attended, up_weight))
    swapped = swap_core(jnp.concatenate(out_mine[1:], axis=0))
    own_up = [
        take(late_up, x_id * hidden_x + h * hidden_half, hidden_half, 1) for h in range(2)
    ]

    attended_all, swapped, up_x = lax.optimization_barrier((attended_all, swapped, up_x))
    residual = residual_columns(
        around,
        attended_all,
        out_weight,
        out_mine[1:],
        swapped,
        stream,
        modulation,
    )
    along_z = [send_z(residual, dz) for dz in range(requests)]
    near = [send_x(residual, dx) for dx in range(wide)]

    up_x[1:], _ = lax.optimization_barrier((up_x[1:], residual))
    other_y = [swap_core(part) for part in up_y[1:]]
    up_mine = [send_y(up_x[dx], dy) if dx else up_y[dy] for dy, dx in around]


    down_cols = down_weight.shape[1]
    down_half = hidden // 2
    own_down = take(down_weight, cfg_id * down_half, down_half, 0)
    along_z, near, other_y, up_mine, own_up, own_down = lax.optimization_barrier(
        (along_z, near, other_y, up_mine, own_up, own_down)
    )
    blocks = [
        [send_x(block, dx) if dz else near[dx] for dz, block in enumerate(along_z)]
        for dx in range(wide)
    ]
    down_mine = [send_y(own_down, dy) for dy in range(1, high)]
    up_pieces = [("halves", own_up)]
    for part, (dy, dx) in zip(up_mine[1:], around[1:]):
        up_pieces.append(("core", [part, swap_core(part) if dx else other_y[dy - 1]]))

    acts, own_rows = [], []
    for dx in range(wide):
        if acts:
            blocks[dx], acts[0] = lax.optimization_barrier((blocks[dx], acts[0]))
        act, own = up_products(around, blocks[dx], modulation, up_pieces)
        own_rows.append(own)
        acts += [send_x(act, step) for step in range(wide)]

    def sent(share):
        return [send_z(part, dz) for dz, part in enumerate(share)]

    earlier = []
    for e in range(1, wide):
        earlier.append(down_products([e], acts, [down_weight], requests))
        if e == 1:
            acts[-1], earlier[0] = lax.optimization_barrier((acts[-1], earlier[0]))
    share = down_products([0], acts, [down_weight], requests, earlier)
    own_share = sent(share)
    down_mine, _ = lax.optimization_barrier((down_mine, share))
    everything = list(range(wide))
    far_parts = [
        down_products(everything, acts, [mine, swap_core(mine)], requests) for mine in down_mine
    ]
    far_shares = [sent(part) for part in far_parts]
    own_share, _ = lax.optimization_barrier((own_share, far_parts))

    mod_half = lax.dynamic_index_in_dim(modulation, cfg_id, 0, keepdims=False)
    gate_two = lax.dynamic_index_in_dim(mod_half[:, 3, :], req_id, 0, keepdims=False)

    def summed(parts):
        total = parts[0].astype(F32)
        for part in parts[1:]:
            total += part.astype(F32)
        return total

    def finished(total, rows, dy):
        col = seq_from(dy, 0) * down_cols
        block_out = (
            take(rows, col, down_cols, 1).astype(F32)
            + take(gate_two, col, down_cols, 0)[None, :] * total
        ).astype(BF16)
        return dot(block_out, take(final_weight, col, down_cols, 0))

    total = summed(own_share)
    velocity = [finished(total[e], own_rows[e], 0) for e in range(wide)]
    for dy, share in enumerate(far_shares, 1):
        total = summed(share)
        for e in range(wide):
            velocity[e] += finished(total[e], own_rows[e], dy)

    channels = final_weight.shape[1]
    cfg_count = lax.axis_size("cfg")
    halves = []
    for dc in range(2):
        share = 0.0
        for e in range(wide):
            block = velocity[e].reshape(row_count // 2, 2, channels)
            block = lax.dynamic_index_in_dim(block, cfg_id ^ dc, 1, keepdims=False)
            if dc or e:
                route = [
                    ((c * high + y) * wide + x, ((c ^ dc) * high + y) * wide + (x - e) % wide)
                    for c in range(cfg_count)
                    for y in range(high)
                    for x in range(wide)
                ]
                block = lax.ppermute(block, ("cfg", "seq"), route)
            share += block
        halves.append(share)
    cond_part = jnp.where(cfg_id == 0, halves[0], halves[1])
    uncond_part = jnp.where(cfg_id == 0, halves[1], halves[0])
    guided = uncond_part + GUIDANCE * (cond_part - uncond_part)
    level_now = noise_level(step_index[0])
    level_next = noise_level(step_index[0] + 1)
    token_ids = (
        seq_id * row_count
        + 2 * jnp.arange(row_count // 2, dtype=jnp.int32)[:, None]
        + cfg_id
        + jnp.zeros((1, channels), jnp.int32)
    )
    valid = token_ids < length
    current = latent[0]
    latent_next = jnp.where(valid, current + (level_next - level_now) * guided, current)
    denoised = jnp.where(valid, current - level_now * guided, current)
    return (latent_next[None], denoised[None])


def solution(mesh):
    in_specs = (
        P("cfg", "req", "seq", None),
        P("cfg", "req", None, None, None),
        P("cfg", "req", None, None, None),
        P("cfg", "req", None, "seq", None),
        P("req", None),
        P(None, "req", "seq"),
        P(),
        P("cfg", None, "seq", "req"),
        P(),
        P("seq", "req"),
        P("seq", "req"),
        P("req", "seq"),
        P(),
        P("req", "seq", "cfg"),
        P(),
    )
    out_specs = (P("req", "seq", "cfg"), P("req", "seq", "cfg"))
    return jax.shard_map(
        per_device, mesh=mesh, in_specs=in_specs, out_specs=out_specs, check_vma=False
    )
```

```python
import functools
import math

import jax
import jax.numpy as jnp
import numpy as np
from jax import lax
from jax.experimental import pallas as pl
from jax.experimental.pallas import tpu as pltpu
from jax.sharding import PartitionSpec as P

STEPS = 28
GUIDANCE = 3.0
SHIFT = 3.0
SCALE = 1.0 / math.sqrt(128.0)
EPSILON = 1e-06
HEAD = 128
BF16 = jnp.bfloat16
F32 = jnp.float32
MIB = 1024 * 1024


def noise_level(index):
    fraction = 1.0 - index.astype(jnp.float32) / STEPS
    return SHIFT * fraction / (SHIFT * fraction + 1.0 - fraction)


def lane_frequencies():
    rows = np.zeros((3, HEAD), np.float32)
    lane = 0
    for component, axis_span in ((0, 16), (1, 56), (2, 56)):
        pair_ids = np.arange(axis_span // 2, dtype=np.float32)
        frequency = np.exp(-(2.0 * pair_ids / axis_span) * np.float32(math.log(10000.0)))
        rows[component, lane : lane + axis_span] = np.repeat(frequency, 2)
        lane += axis_span
    return rows


def seq_grid(count):
    columns = 2 ** ((count.bit_length() - 1) // 2)
    return count // columns, columns


def send_x(block, step):
    if step == 0:
        return block
    high, wide = seq_grid(lax.axis_size("seq"))
    route = [(y * wide + x, y * wide + (x + step) % wide) for y in range(high) for x in range(wide)]
    return lax.ppermute(block, "seq", route)


def send_y(block, step):
    if step == 0:
        return block
    high, wide = seq_grid(lax.axis_size("seq"))
    route = [(y * wide + x, (y + step) % high * wide + x) for y in range(high) for x in range(wide)]
    return lax.ppermute(block, "seq", route)


def send_seq(block, dy, dx):
    if dy == 0 and dx == 0:
        return block
    high, wide = seq_grid(lax.axis_size("seq"))
    route = [
        (y * wide + x, (y + dy) % high * wide + (x + dx) % wide)
        for y in range(high)
        for x in range(wide)
    ]
    return lax.ppermute(block, "seq", route)


def send_z(block, step):
    if step == 0:
        return block
    count = lax.axis_size("req")
    return lax.ppermute(block, "req", [(r, (r + step) % count) for r in range(count)])


def swap_core(block):
    return lax.ppermute(block, "cfg", [(0, 1), (1, 0)])


def take(array, start, size, axis):
    return lax.dynamic_slice_in_dim(array, start, size, axis)


def dot(left, right):
    return jnp.dot(left, right, preferred_element_type=jnp.float32)


def hbm_spec():
    return pl.BlockSpec(memory_space=pl.ANY)


def place_of(step_x, step_y=0):
    high, wide = seq_grid(lax.axis_size("seq"))
    seq = lax.axis_index("seq")
    return lax.rem(seq // wide + high - step_y, high) * wide + x_of(step_x)


def x_of(step):
    wide = seq_grid(lax.axis_size("seq"))[1]
    return lax.rem(lax.axis_index("seq") % wide + 2 * wide - step, wide)


def z_of(step):
    count = lax.axis_size("req")
    return lax.rem(lax.axis_index("req") + count - step, count)


def whole_spec():
    return pl.BlockSpec(memory_space=pltpu.VMEM)


def smem_spec():
    return pl.BlockSpec(memory_space=pltpu.SMEM)


def cost(flops, moved):
    return pl.CostEstimate(flops=int(flops), bytes_accessed=int(moved), transcendentals=0)


def params():
    return pltpu.CompilerParams(vmem_limit_bytes=60 * MIB)


def rotate_kernel(kv_ref, pos_ref, freq_ref, out_ref):
    rows, width = kv_ref.shape[1:]
    row_ids = lax.broadcasted_iota(jnp.int32, (rows, HEAD), 0)
    angles = jnp.zeros((rows, HEAD), F32)
    for row in range(rows):
        line = (
            pos_ref[0, 0, row].astype(F32) * freq_ref[0:1, :]
            + pos_ref[1, 0, row].astype(F32) * freq_ref[1:2, :]
            + pos_ref[2, 0, row].astype(F32) * freq_ref[2:3, :]
        )
        angles = jnp.where(row_ids == row, line, angles)
    cosine, sine = jnp.cos(angles), jnp.sin(angles)
    even = lax.broadcasted_iota(jnp.int32, (rows, HEAD), 1) % 2 == 0
    out_ref[...] = jnp.zeros_like(out_ref)
    for first in range(0, width, HEAD):
        keys = kv_ref[0, :, first : first + HEAD].astype(F32)
        after = pltpu.roll(keys, HEAD - 1, 1)
        before = pltpu.roll(keys, 1, 1)
        rotated = cosine * keys + sine * jnp.where(even, -after, before)
        out_ref[0, 0:rows, first : first + HEAD] = rotated.astype(BF16)
    out_ref[1, 0:rows, :] = kv_ref[1]


def rotate_fresh(fresh, positions, padded):
    width = fresh.shape[2]
    return pl.pallas_call(
        rotate_kernel,
        out_shape=jax.ShapeDtypeStruct((2, padded, width), BF16),
        in_specs=[whole_spec(), smem_spec(), whole_spec()],
        out_specs=whole_spec(),
        compiler_params=params(),
    )(fresh, positions, jnp.asarray(lane_frequencies()))


def attention_kernel(around, lengths_ref, slots_ref, q_ref, text_ref, image_ref, *refs):
    pieces = len(around)
    fresh_refs, (out_ref, fresh_ref) = refs[:pieces], refs[pieces:]
    padded = fresh_refs[0].shape[1]
    for i in range(pieces):
        fresh_ref[:, i * padded : (i + 1) * padded, :] = fresh_refs[i][...]
    slots = image_ref.shape[1]
    count = slots_ref.shape[1] // pieces
    length = lengths_ref[lax.axis_index("req")]
    key_ids = lax.broadcasted_iota(jnp.int32, (1, slots), 1)
    fresh_ids = lax.broadcasted_iota(jnp.int32, (1, pieces * padded), 1)
    image_bias = jnp.where(key_ids < length, 0.0, -jnp.inf)
    fresh_bias = jnp.full(fresh_ids.shape, -jnp.inf, F32)
    for i, (dy, dx) in enumerate(around):
        first = place_of(dx, dy) * count
        for j in range(count):
            slot = slots_ref[0, first + j]
            image_bias = jnp.where(key_ids == slot, -jnp.inf, image_bias)
            here = (fresh_ids == i * padded + j) & (slot < length)
            fresh_bias = jnp.where(here, 0.0, fresh_bias)
    over_lanes = (((1,), (1,)), ((), ()))
    for first in range(0, q_ref.shape[1], HEAD):
        head = slice(first, first + HEAD)
        query = q_ref[:, head]

        def scores(keys):
            return lax.dot_general(query, keys, over_lanes, preferred_element_type=F32) * SCALE

        text = scores(text_ref[0, :, head])
        image = scores(image_ref[0, :, head]) + image_bias
        fresh = scores(fresh_ref[0, :, head]) + fresh_bias
        best = jnp.maximum(
            jnp.max(text, axis=1, keepdims=True),
            jnp.maximum(
                jnp.max(image, axis=1, keepdims=True), jnp.max(fresh, axis=1, keepdims=True)
            ),
        )
        text, image, fresh = jnp.exp(text - best), jnp.exp(image - best), jnp.exp(fresh - best)
        total = (
            jnp.sum(text, axis=1, keepdims=True)
            + jnp.sum(image, axis=1, keepdims=True)
            + jnp.sum(fresh, axis=1, keepdims=True)
        )
        mixed = (
            dot(text.astype(BF16), text_ref[1, :, head])
            + dot(image.astype(BF16), image_ref[1, :, head])
            + dot(fresh.astype(BF16), fresh_ref[1, :, head])
        )
        out_ref[0, :, head] = (mixed / total).astype(BF16)


def attention(around, lengths, slot_ids, query, text_kv, image_kv, fresh):
    rows, width = query.shape
    group = 3 * HEAD
    groups = width // group
    text, slots = text_kv.shape[1], image_kv.shape[1]
    pieces, padded = len(fresh), fresh[0].shape[1]
    return pl.pallas_call(
        functools.partial(attention_kernel, around),
        grid=(groups,),
        out_shape=jax.ShapeDtypeStruct((groups, rows, group), BF16),
        in_specs=[
            smem_spec(),
            smem_spec(),
            pl.BlockSpec((rows, group), lambda g: (0, g)),
            pl.BlockSpec((2, text, group), lambda g: (0, 0, g)),
            pl.BlockSpec((2, slots, group), lambda g: (0, 0, g)),
        ]
        + [pl.BlockSpec((2, padded, group), lambda g: (0, 0, g))] * pieces,
        out_specs=pl.BlockSpec((1, rows, group), lambda g: (g, 0, 0)),
        scratch_shapes=[pltpu.VMEM((2, padded * pieces, group), BF16)],
        compiler_params=params(),
    )(lengths, slot_ids, query, text_kv, image_kv, *fresh)


def residual_kernel(requests, around, *refs):
    pieces = len(around)
    attended, refs = refs[:requests], refs[requests:]
    own_ref, mine, refs = refs[0], refs[1:pieces], refs[pieces:]
    swapped_ref, stream_ref, mod_ref, out_ref, rows_ref = refs
    row_count = attended[0].shape[1]
    depth, width = own_ref.shape
    half_width = width // 2
    cfg, req = lax.axis_index("cfg"), lax.axis_index("req")
    places = [place_of(dx, dy) for dy, dx in around]
    for j in range(requests):
        first = pl.multiple_of(z_of(j) * row_count, 16)
        rows_ref[:, pl.ds(first, row_count), :] = attended[j][...]
    at = pl.multiple_of(req * width, 128)
    gates = [mod_ref[cfg, q, 0:1, pl.ds(at, width)] for q in range(requests)]

    def columns(core):
        for role, half in ((0, core), (1, 1 - core)):
            lanes = slice(half * half_width, (half + 1) * half_width)
            total = dot(rows_ref[places[0]], own_ref[:, lanes])
            for k in range(1, pieces):
                piece = swapped_ref[(k - 1) * depth : k * depth, :] if role else mine[k - 1][...]
                total += dot(rows_ref[places[k]], piece)
            for q in range(requests):
                out_ref[q, :, lanes] = (
                    stream_ref[0, q, :, lanes].astype(F32)
                    + gates[q][:, lanes] * total[q * row_count : (q + 1) * row_count]
                ).astype(BF16)

    pl.when(cfg == 0)(functools.partial(columns, 0))
    pl.when(cfg == 1)(functools.partial(columns, 1))


def residual_columns(around, attended, own, mine, swapped, stream, modulation):
    requests, pieces = len(attended), len(mine) + 1
    segments, row_count, seg = attended[0].shape
    return pl.pallas_call(
        functools.partial(residual_kernel, requests, around),
        out_shape=jax.ShapeDtypeStruct(stream.shape[1:], BF16),
        in_specs=[whole_spec()] * (requests + pieces + 3),
        out_specs=whole_spec(),
        scratch_shapes=[pltpu.VMEM((segments, requests * row_count, seg), BF16)],
        compiler_params=params(),
    )(*attended, own, *mine, swapped, stream, modulation)


def copies_of(pieces, buffer, sems):
    cfg = lax.axis_index("cfg")
    copies = []
    for k, (kind, parts) in enumerate(pieces):
        for h in range(2):
            slot = h
            if kind == "core":
                slot = cfg if h == 0 else 1 - cfg
            copies.append(
                (h, pltpu.make_async_copy(parts[h], buffer.at[slot, k], sems.at[slot, k]))
            )
    return [copy for h in range(2) for half, copy in copies if half == h]


def up_kernel(requests, around, kinds, *refs):
    blocks, refs = refs[:requests], refs[requests:]
    mod_ref, refs = refs[0], refs[1:]
    pieces = []
    for kind in kinds:
        pieces.append((kind, refs[:2]))
        refs = refs[2:]
    out_ref, own_ref, rows_ref, buffer, sems = refs
    row_count, width = blocks[0].shape[1:]
    depth, hidden = buffer.shape[2:]
    cfg, req = lax.axis_index("cfg"), lax.axis_index("req")
    scale_of_mean = 1.0 / (requests * width)
    for copy in copies_of(pieces, buffer, sems):
        copy.start()
    for q in range(requests):
        total = jnp.zeros((row_count, 1), F32)
        for block in blocks:
            total += jnp.sum(block[q].astype(F32), axis=1, keepdims=True)
        average = total * scale_of_mean
        total = jnp.zeros((row_count, 1), F32)
        for block in blocks:
            centered = block[q].astype(F32) - average
            total += jnp.sum(centered * centered, axis=1, keepdims=True)
        inverse = lax.rsqrt(total * scale_of_mean + EPSILON)
        for dz, block in enumerate(blocks):
            place = z_of(dz)
            at = pl.ds(pl.multiple_of(place * width, 128), width)
            scale = 1.0 + mod_ref[cfg, q, 2:3, at]
            shift = mod_ref[cfg, q, 1:2, at]
            normed = (block[q].astype(F32) - average) * inverse * scale + shift
            normed = normed.astype(BF16)
            for i in range(width // depth):
                rows_ref[
                    place * (width // depth) + i, q * row_count : (q + 1) * row_count, :
                ] = normed[:, i * depth : (i + 1) * depth]
    for dz, block in enumerate(blocks):
        at = pl.ds(pl.multiple_of(z_of(dz) * width, 128), width)
        own_ref[:, at] = block[req]
    step = 256 if hidden % 256 == 0 else hidden
    for h in range(2):
        for c in range(hidden // step):
            total = None
            for k, (dy, dx) in enumerate(around):
                if c == 0:
                    source = pieces[k][1][0]
                    pltpu.make_async_copy(source, buffer.at[h, k], sems.at[h, k]).wait()
                weight = buffer[h, k, :, c * step : (c + 1) * step]
                term = dot(rows_ref[place_of(dx, dy)], weight)
                total = term if total is None else total + term
            out_ref[h, :, c * step : (c + 1) * step] = jax.nn.gelu(
                total, approximate=True
            ).astype(BF16)


def up_products(around, blocks, modulation, pieces):
    requests = len(blocks)
    row_count, slice_width = blocks[0].shape[1:]
    model = requests * slice_width
    depth, hidden = pieces[0][1][0].shape[-2:]
    rows = requests * row_count
    operands = [part for _, parts in pieces for part in parts]
    return pl.pallas_call(
        functools.partial(up_kernel, requests, around, [kind for kind, _ in pieces]),
        out_shape=(
            jax.ShapeDtypeStruct((2, rows, hidden), BF16),
            jax.ShapeDtypeStruct((row_count, model), BF16),
        ),
        in_specs=[whole_spec()] * (requests + 1) + [hbm_spec()] * len(operands),
        out_specs=(whole_spec(), whole_spec()),
        scratch_shapes=[
            pltpu.VMEM((model // depth, rows, depth), BF16),
            pltpu.VMEM((2, len(pieces), depth, hidden), BF16),
            pltpu.SemaphoreType.DMA((2, len(pieces))),
        ],
        compiler_params=params(),
        cost_estimate=cost(8 * rows * model * hidden, 8 * model * hidden),
    )(*blocks, modulation, *operands)


def down_kernel(requests, wide, blocks, weights, earlier, *refs):
    acts, refs = refs[: wide * len(blocks)], refs[wide * len(blocks) :]
    weight_refs, refs = refs[:weights], refs[weights:]
    earlier_refs, refs = refs[: earlier * requests], refs[earlier * requests :]
    out_refs, (scratch_ref, buffer, sems) = refs[:requests], refs[requests:]
    rows, depth = acts[0].shape[1:]
    row_count = rows // requests
    width = buffer.shape[2]
    share = 2 * wide // weights
    for w, weight in enumerate(weight_refs):
        for i in range(share):
            slot = i
            if weights > 1:
                cfg = lax.axis_index("cfg")
                slot = (cfg if w == 0 else 1 - cfg) * share + i
            source = weight.at[pl.ds(i * depth, depth), :]
            pltpu.make_async_copy(source, buffer.at[slot], sems.at[slot]).start()
    for k, ref in enumerate(earlier_refs):
        out_refs[k % requests][len(blocks) + k // requests] = ref[0]
    step = 256 if width % 256 == 0 else width
    for c in range(width // step):
        lanes = slice(c * step, (c + 1) * step)
        total = None
        for far in range(wide):
            for h in range(2):
                slot = 2 * x_of(far) + h
                if c == 0:
                    source = weight_refs[0].at[pl.ds(0, depth), :]
                    pltpu.make_async_copy(source, buffer.at[slot], sems.at[slot]).wait()
                left = [acts[b * wide + far][h] for b in range(len(blocks))]
                left = jnp.concatenate(left, axis=0) if len(left) > 1 else left[0]
                term = dot(left, buffer[slot, :, lanes])
                total = term if total is None else total + term
        scratch_ref[...] = total
        for dz, out_ref in enumerate(out_refs):
            for b in range(len(blocks)):
                first = pl.multiple_of(b * rows + z_of(requests - dz) * row_count, 16)
                out_ref[b, :, lanes] = scratch_ref[pl.ds(first, row_count), :].astype(BF16)


def down_products(blocks, acts, weights, requests, earlier=()):
    rows, depth = acts[0].shape[1:]
    wide = math.isqrt(len(acts))
    width = weights[0].shape[1]
    step = 256 if width % 256 == 0 else width
    shape = (len(blocks) + len(earlier), rows // requests, width)
    done = [part for share in earlier for part in share]
    used = [acts[(e - far) % wide * wide + far] for e in blocks for far in range(wide)]
    return pl.pallas_call(
        functools.partial(down_kernel, requests, wide, blocks, len(weights), len(earlier)),
        out_shape=tuple(jax.ShapeDtypeStruct(shape, BF16) for _ in range(requests)),
        in_specs=[whole_spec()] * len(used)
        + [hbm_spec()] * len(weights)
        + [whole_spec()] * len(done),
        out_specs=tuple(whole_spec() for _ in range(requests)),
        scratch_shapes=[
            pltpu.VMEM((len(blocks) * rows, step), F32),
            pltpu.VMEM((2 * wide, depth, width), BF16),
            pltpu.SemaphoreType.DMA((2 * wide,)),
        ],
        compiler_params=params(),
        cost_estimate=cost(4 * len(used) * rows * depth * width, 4 * wide * depth * width),
    )(*used, *weights, *done)


def per_device(
    queries,
    text_cache,
    image_cache,
    fresh_kv,
    fresh_slots,
    fresh_pos,
    image_len,
    stream,
    modulation,
    out_weight,
    up_weight,
    down_weight,
    final_weight,
    latent,
    step_index,
):
    cfg_id = lax.axis_index("cfg")
    req_id = lax.axis_index("req")
    seq_id = lax.axis_index("seq")
    requests = lax.axis_size("req")
    high, wide = seq_grid(lax.axis_size("seq"))
    y_id, x_id = seq_id // wide, seq_id % wide
    around = [(dy, dx) for dy in range(high) for dx in range(wide)]

    def x_from(step):
        return (x_id - step) % wide

    def y_from(step):
        return (y_id - step) % high

    def seq_from(dy, dx):
        return y_from(dy) * wide + x_from(dx)

    fresh_count = fresh_kv.shape[3]
    padded = -(-fresh_count // 16) * 16
    fresh_pair = rotate_fresh(fresh_kv[0, 0], fresh_pos, padded)
    fresh = [send_seq(fresh_pair, dy, dx) for dy, dx in around]

    out_rows, col_count = out_weight.shape
    seg = col_count // 2
    own_out, _ = lax.optimization_barrier((out_weight, fresh_pair))
    own_out = take(own_out, cfg_id * seg, seg, 1)
    out_y = [send_y(own_out, dy) for dy in range(high)]
    out_x = [send_x(own_out, dx) for dx in range(wide)]

    up_rows, hidden = up_weight.shape
    hidden_x = hidden // wide
    hidden_half = hidden_x // 2
    early_up, _ = lax.optimization_barrier((up_weight, fresh_pair))
    to_x = []
    for dx in range(wide):
        first = (x_id + dx) % wide * hidden_x + cfg_id * hidden_half
        to_x.append(take(early_up, first, hidden_half, 1))
    to_x, out_x, out_y, fresh = lax.optimization_barrier((to_x, out_x, out_y, fresh))
    up_x = [send_x(part, dx) for dx, part in enumerate(to_x)]
    up_y = [send_y(up_x[0], dy) for dy in range(high)]
    out_mine = [send_y(out_x[dx], dy) if dx else out_y[dy] for dy, dx in around]

    length = lax.dynamic_index_in_dim(image_len, req_id, 0, keepdims=False)
    attended = attention(
        around,
        image_len,
        fresh_slots,
        queries[0, 0],
        text_cache[0, 0],
        image_cache[0, 0],
        fresh,
    )
    row_count = queries.shape[2]
    if attended.shape[2] != out_rows:
        attended = jnp.transpose(attended, (1, 0, 2)).reshape(row_count, -1, out_rows)
        attended = jnp.transpose(attended, (1, 0, 2))
    attended_all = [send_z(attended, dz) for dz in range(requests)]
    out_mine, attended, late_up = lax.optimization_barrier((out_mine, attended, up_weight))
    swapped = swap_core(jnp.concatenate(out_mine[1:], axis=0))
    own_up = [
        take(late_up, x_id * hidden_x + h * hidden_half, hidden_half, 1) for h in range(2)
    ]

    attended_all, swapped, up_x, own_up = lax.optimization_barrier(
        (attended_all, swapped, up_x, own_up)
    )
    residual = residual_columns(
        around,
        attended_all,
        out_weight,
        out_mine[1:],
        swapped,
        stream,
        modulation,
    )
    along_z = [send_z(residual, dz) for dz in range(requests)]
    near = [send_x(residual, dx) for dx in range(wide)]

    up_x[1:], _ = lax.optimization_barrier((up_x[1:], residual))
    other_y = [swap_core(part) for part in up_y[1:]]
    up_mine = [send_y(up_x[dx], dy) if dx else up_y[dy] for dy, dx in around]

    down_cols = down_weight.shape[1]
    down_half = hidden // 2
    own_down = take(down_weight, cfg_id * down_half, down_half, 0)
    along_z, near, other_y, up_mine, own_down = lax.optimization_barrier(
        (along_z, near, other_y, up_mine, own_down)
    )
    blocks = [
        [send_x(block, dx) if dz else near[dx] for dz, block in enumerate(along_z)]
        for dx in range(wide)
    ]
    down_mine = [send_y(own_down, dy) for dy in range(1, high)]
    up_pieces = [("halves", own_up)]
    for part, (dy, dx) in zip(up_mine[1:], around[1:]):
        up_pieces.append(("core", [part, swap_core(part) if dx else other_y[dy - 1]]))

    acts, own_rows = [], []
    for dx in range(wide):
        if acts:
            blocks[dx], acts[0] = lax.optimization_barrier((blocks[dx], acts[0]))
        act, own = up_products(around, blocks[dx], modulation, up_pieces)
        own_rows.append(own)
        acts += [send_x(act, step) for step in range(wide)]

    def sent(share):
        return [send_z(part, dz) for dz, part in enumerate(share)]

    earlier = []
    for e in range(1, wide):
        earlier.append(down_products([e], acts, [down_weight], requests))
        if e == 1:
            acts[-1], earlier[0] = lax.optimization_barrier((acts[-1], earlier[0]))
    share = down_products([0], acts, [down_weight], requests, earlier)
    own_share = sent(share)
    down_mine, _ = lax.optimization_barrier((down_mine, share))
    everything = list(range(wide))
    far_parts = [
        down_products(everything, acts, [mine, swap_core(mine)], requests) for mine in down_mine
    ]
    far_shares = [sent(part) for part in far_parts]
    own_share, _ = lax.optimization_barrier((own_share, far_parts))

    mod_half = lax.dynamic_index_in_dim(modulation, cfg_id, 0, keepdims=False)
    gate_two = lax.dynamic_index_in_dim(mod_half[:, 3, :], req_id, 0, keepdims=False)

    def summed(parts):
        total = parts[0].astype(F32)
        for part in parts[1:]:
            total += part.astype(F32)
        return total

    def finished(total, rows, dy):
        col = seq_from(dy, 0) * down_cols
        block_out = (
            take(rows, col, down_cols, 1).astype(F32)
            + take(gate_two, col, down_cols, 0)[None, :] * total
        ).astype(BF16)
        return dot(block_out, take(final_weight, col, down_cols, 0))

    total = summed(own_share)
    velocity = [finished(total[e], own_rows[e], 0) for e in range(wide)]
    for dy, share in enumerate(far_shares, 1):
        total = summed(share)
        for e in range(wide):
            velocity[e] += finished(total[e], own_rows[e], dy)

    channels = final_weight.shape[1]
    cfg_count = lax.axis_size("cfg")
    halves = []
    for dc in range(2):
        share = 0.0
        for e in range(wide):
            block = velocity[e].reshape(row_count // 2, 2, channels)
            block = lax.dynamic_index_in_dim(block, cfg_id ^ dc, 1, keepdims=False)
            if dc or e:
                route = [
                    ((c * high + y) * wide + x, ((c ^ dc) * high + y) * wide + (x - e) % wide)
                    for c in range(cfg_count)
                    for y in range(high)
                    for x in range(wide)
                ]
                block = lax.ppermute(block, ("cfg", "seq"), route)
            share += block
        halves.append(share)
    cond_part = jnp.where(cfg_id == 0, halves[0], halves[1])
    uncond_part = jnp.where(cfg_id == 0, halves[1], halves[0])
    guided = uncond_part + GUIDANCE * (cond_part - uncond_part)
    level_now = noise_level(step_index[0])
    level_next = noise_level(step_index[0] + 1)
    token_ids = (
        seq_id * row_count
        + 2 * jnp.arange(row_count // 2, dtype=jnp.int32)[:, None]
        + cfg_id
        + jnp.zeros((1, channels), jnp.int32)
    )
    valid = token_ids < length
    current = latent[0]
    latent_next = jnp.where(valid, current + (level_next - level_now) * guided, current)
    denoised = jnp.where(valid, current - level_now * guided, current)
    return (latent_next[None], denoised[None])


def solution(mesh):
    in_specs = (
        P("cfg", "req", "seq", None),
        P("cfg", "req", None, None, None),
        P("cfg", "req", None, None, None),
        P("cfg", "req", None, "seq", None),
        P("req", None),
        P(None, "req", "seq"),
        P(),
        P("cfg", None, "seq", "req"),
        P(),
        P("seq", "req"),
        P("seq", "req"),
        P("req", "seq"),
        P(),
        P("req", "seq", "cfg"),
        P(),
    )
    out_specs = (P("req", "seq", "cfg"), P("req", "seq", "cfg"))
    return jax.shard_map(
        per_device, mesh=mesh, in_specs=in_specs, out_specs=out_specs, check_vma=False
    )
```

```python
import functools
import math

import jax
import jax.numpy as jnp
import numpy as np
from jax import lax
from jax.experimental import pallas as pl
from jax.experimental.pallas import tpu as pltpu
from jax.sharding import PartitionSpec as P

STEPS = 28
GUIDANCE = 3.0
SHIFT = 3.0
SCALE = 1.0 / math.sqrt(128.0)
EPSILON = 1e-06
HEAD = 128
BF16 = jnp.bfloat16
F32 = jnp.float32
MIB = 1024 * 1024


def noise_level(index):
    fraction = 1.0 - index.astype(jnp.float32) / STEPS
    return SHIFT * fraction / (SHIFT * fraction + 1.0 - fraction)


def lane_frequencies():
    rows = np.zeros((3, HEAD), np.float32)
    lane = 0
    for component, axis_span in ((0, 16), (1, 56), (2, 56)):
        pair_ids = np.arange(axis_span // 2, dtype=np.float32)
        frequency = np.exp(-(2.0 * pair_ids / axis_span) * np.float32(math.log(10000.0)))
        rows[component, lane : lane + axis_span] = np.repeat(frequency, 2)
        lane += axis_span
    return rows


def seq_grid(count):
    columns = 2 ** ((count.bit_length() - 1) // 2)
    return count // columns, columns


def send_x(block, step):
    if step == 0:
        return block
    high, wide = seq_grid(lax.axis_size("seq"))
    route = [(y * wide + x, y * wide + (x + step) % wide) for y in range(high) for x in range(wide)]
    return lax.ppermute(block, "seq", route)


def send_y(block, step):
    if step == 0:
        return block
    high, wide = seq_grid(lax.axis_size("seq"))
    route = [(y * wide + x, (y + step) % high * wide + x) for y in range(high) for x in range(wide)]
    return lax.ppermute(block, "seq", route)


def send_seq(block, dy, dx):
    if dy == 0 and dx == 0:
        return block
    high, wide = seq_grid(lax.axis_size("seq"))
    route = [
        (y * wide + x, (y + dy) % high * wide + (x + dx) % wide)
        for y in range(high)
        for x in range(wide)
    ]
    return lax.ppermute(block, "seq", route)


def send_z(block, step):
    if step == 0:
        return block
    count = lax.axis_size("req")
    return lax.ppermute(block, "req", [(r, (r + step) % count) for r in range(count)])


def swap_core(block):
    return lax.ppermute(block, "cfg", [(0, 1), (1, 0)])


def take(array, start, size, axis):
    return lax.dynamic_slice_in_dim(array, start, size, axis)


def dot(left, right):
    return jnp.dot(left, right, preferred_element_type=jnp.float32)


def hbm_spec():
    return pl.BlockSpec(memory_space=pl.ANY)


def place_of(step_x, step_y=0):
    high, wide = seq_grid(lax.axis_size("seq"))
    seq = lax.axis_index("seq")
    return lax.rem(seq // wide + high - step_y, high) * wide + x_of(step_x)


def x_of(step):
    wide = seq_grid(lax.axis_size("seq"))[1]
    return lax.rem(lax.axis_index("seq") % wide + 2 * wide - step, wide)


def z_of(step):
    count = lax.axis_size("req")
    return lax.rem(lax.axis_index("req") + count - step, count)


def whole_spec():
    return pl.BlockSpec(memory_space=pltpu.VMEM)


def smem_spec():
    return pl.BlockSpec(memory_space=pltpu.SMEM)


def cost(flops, moved):
    return pl.CostEstimate(flops=int(flops), bytes_accessed=int(moved), transcendentals=0)


def params():
    return pltpu.CompilerParams(vmem_limit_bytes=60 * MIB)


def rotate_kernel(kv_ref, pos_ref, freq_ref, out_ref):
    rows, width = kv_ref.shape[1:]
    row_ids = lax.broadcasted_iota(jnp.int32, (rows, HEAD), 0)
    angles = jnp.zeros((rows, HEAD), F32)
    for row in range(rows):
        line = (
            pos_ref[0, 0, row].astype(F32) * freq_ref[0:1, :]
            + pos_ref[1, 0, row].astype(F32) * freq_ref[1:2, :]
            + pos_ref[2, 0, row].astype(F32) * freq_ref[2:3, :]
        )
        angles = jnp.where(row_ids == row, line, angles)
    cosine, sine = jnp.cos(angles), jnp.sin(angles)
    even = lax.broadcasted_iota(jnp.int32, (rows, HEAD), 1) % 2 == 0
    out_ref[...] = jnp.zeros_like(out_ref)
    for first in range(0, width, HEAD):
        keys = kv_ref[0, :, first : first + HEAD].astype(F32)
        after = pltpu.roll(keys, HEAD - 1, 1)
        before = pltpu.roll(keys, 1, 1)
        rotated = cosine * keys + sine * jnp.where(even, -after, before)
        out_ref[0, 0:rows, first : first + HEAD] = rotated.astype(BF16)
    out_ref[1, 0:rows, :] = kv_ref[1]


def rotate_fresh(fresh, positions, padded):
    width = fresh.shape[2]
    return pl.pallas_call(
        rotate_kernel,
        out_shape=jax.ShapeDtypeStruct((2, padded, width), BF16),
        in_specs=[whole_spec(), smem_spec(), whole_spec()],
        out_specs=whole_spec(),
        compiler_params=params(),
    )(fresh, positions, jnp.asarray(lane_frequencies()))


def attention_kernel(around, lengths_ref, slots_ref, q_ref, text_ref, image_ref, *refs):
    pieces = len(around)
    fresh_refs, (out_ref, fresh_ref) = refs[:pieces], refs[pieces:]
    padded = fresh_refs[0].shape[1]
    for i in range(pieces):
        fresh_ref[:, i * padded : (i + 1) * padded, :] = fresh_refs[i][...]
    slots = image_ref.shape[1]
    count = slots_ref.shape[1] // pieces
    length = lengths_ref[lax.axis_index("req")]
    key_ids = lax.broadcasted_iota(jnp.int32, (1, slots), 1)
    fresh_ids = lax.broadcasted_iota(jnp.int32, (1, pieces * padded), 1)
    image_bias = jnp.where(key_ids < length, 0.0, -jnp.inf)
    fresh_bias = jnp.full(fresh_ids.shape, -jnp.inf, F32)
    for i, (dy, dx) in enumerate(around):
        first = place_of(dx, dy) * count
        for j in range(count):
            slot = slots_ref[0, first + j]
            image_bias = jnp.where(key_ids == slot, -jnp.inf, image_bias)
            here = (fresh_ids == i * padded + j) & (slot < length)
            fresh_bias = jnp.where(here, 0.0, fresh_bias)
    over_lanes = (((1,), (1,)), ((), ()))
    for first in range(0, q_ref.shape[1], HEAD):
        head = slice(first, first + HEAD)
        query = q_ref[:, head]

        def scores(keys):
            return lax.dot_general(query, keys, over_lanes, preferred_element_type=F32) * SCALE

        text = scores(text_ref[0, :, head])
        image = scores(image_ref[0, :, head]) + image_bias
        fresh = scores(fresh_ref[0, :, head]) + fresh_bias
        best = jnp.maximum(
            jnp.max(text, axis=1, keepdims=True),
            jnp.maximum(
                jnp.max(image, axis=1, keepdims=True), jnp.max(fresh, axis=1, keepdims=True)
            ),
        )
        text, image, fresh = jnp.exp(text - best), jnp.exp(image - best), jnp.exp(fresh - best)
        total = (
            jnp.sum(text, axis=1, keepdims=True)
            + jnp.sum(image, axis=1, keepdims=True)
            + jnp.sum(fresh, axis=1, keepdims=True)
        )
        mixed = (
            dot(text.astype(BF16), text_ref[1, :, head])
            + dot(image.astype(BF16), image_ref[1, :, head])
            + dot(fresh.astype(BF16), fresh_ref[1, :, head])
        )
        out_ref[0, :, head] = (mixed / total).astype(BF16)


def attention(around, lengths, slot_ids, query, text_kv, image_kv, fresh):
    rows, width = query.shape
    group = 3 * HEAD
    groups = width // group
    text, slots = text_kv.shape[1], image_kv.shape[1]
    pieces, padded = len(fresh), fresh[0].shape[1]
    return pl.pallas_call(
        functools.partial(attention_kernel, around),
        grid=(groups,),
        out_shape=jax.ShapeDtypeStruct((groups, rows, group), BF16),
        in_specs=[
            smem_spec(),
            smem_spec(),
            pl.BlockSpec((rows, group), lambda g: (0, g)),
            pl.BlockSpec((2, text, group), lambda g: (0, 0, g)),
            pl.BlockSpec((2, slots, group), lambda g: (0, 0, g)),
        ]
        + [pl.BlockSpec((2, padded, group), lambda g: (0, 0, g))] * pieces,
        out_specs=pl.BlockSpec((1, rows, group), lambda g: (g, 0, 0)),
        scratch_shapes=[pltpu.VMEM((2, padded * pieces, group), BF16)],
        compiler_params=params(),
    )(lengths, slot_ids, query, text_kv, image_kv, *fresh)


def residual_kernel(requests, around, *refs):
    pieces = len(around)
    attended, refs = refs[:requests], refs[requests:]
    own_ref, mine, refs = refs[0], refs[1:pieces], refs[pieces:]
    swapped_ref, stream_ref, mod_ref, out_ref, rows_ref = refs
    row_count = attended[0].shape[1]
    depth, width = own_ref.shape
    half_width = width // 2
    cfg, req = lax.axis_index("cfg"), lax.axis_index("req")
    places = [place_of(dx, dy) for dy, dx in around]
    for j in range(requests):
        first = pl.multiple_of(z_of(j) * row_count, 16)
        rows_ref[:, pl.ds(first, row_count), :] = attended[j][...]
    at = pl.multiple_of(req * width, 128)
    gates = [mod_ref[cfg, q, 0:1, pl.ds(at, width)] for q in range(requests)]

    def columns(core):
        for role, half in ((0, core), (1, 1 - core)):
            lanes = slice(half * half_width, (half + 1) * half_width)
            total = dot(rows_ref[places[0]], own_ref[:, lanes])
            for k in range(1, pieces):
                piece = swapped_ref[(k - 1) * depth : k * depth, :] if role else mine[k - 1][...]
                total += dot(rows_ref[places[k]], piece)
            for q in range(requests):
                out_ref[q, :, lanes] = (
                    stream_ref[0, q, :, lanes].astype(F32)
                    + gates[q][:, lanes] * total[q * row_count : (q + 1) * row_count]
                ).astype(BF16)

    pl.when(cfg == 0)(functools.partial(columns, 0))
    pl.when(cfg == 1)(functools.partial(columns, 1))


def residual_columns(around, attended, own, mine, swapped, stream, modulation):
    requests, pieces = len(attended), len(mine) + 1
    segments, row_count, seg = attended[0].shape
    return pl.pallas_call(
        functools.partial(residual_kernel, requests, around),
        out_shape=jax.ShapeDtypeStruct(stream.shape[1:], BF16),
        in_specs=[whole_spec()] * (requests + pieces + 3),
        out_specs=whole_spec(),
        scratch_shapes=[pltpu.VMEM((segments, requests * row_count, seg), BF16)],
        compiler_params=params(),
    )(*attended, own, *mine, swapped, stream, modulation)


def copies_of(pieces, buffer, sems):
    cfg = lax.axis_index("cfg")
    copies = []
    for k, (kind, parts) in enumerate(pieces):
        for h in range(2):
            slot = h
            if kind == "core":
                slot = cfg if h == 0 else 1 - cfg
            copies.append(
                (h, pltpu.make_async_copy(parts[h], buffer.at[slot, k], sems.at[slot, k]))
            )
    return [copy for h in range(2) for half, copy in copies if half == h]


def up_kernel(requests, around, kinds, *refs):
    blocks, refs = refs[:requests], refs[requests:]
    mod_ref, refs = refs[0], refs[1:]
    pieces = []
    for kind in kinds:
        pieces.append((kind, refs[:2]))
        refs = refs[2:]
    out_ref, own_ref, rows_ref, buffer, sems = refs
    row_count, width = blocks[0].shape[1:]
    depth, hidden = buffer.shape[2:]
    cfg, req = lax.axis_index("cfg"), lax.axis_index("req")
    scale_of_mean = 1.0 / (requests * width)
    for copy in copies_of(pieces, buffer, sems):
        copy.start()
    for q in range(requests):
        total = jnp.zeros((row_count, 1), F32)
        for block in blocks:
            total += jnp.sum(block[q].astype(F32), axis=1, keepdims=True)
        average = total * scale_of_mean
        total = jnp.zeros((row_count, 1), F32)
        for block in blocks:
            centered = block[q].astype(F32) - average
            total += jnp.sum(centered * centered, axis=1, keepdims=True)
        inverse = lax.rsqrt(total * scale_of_mean + EPSILON)
        for dz, block in enumerate(blocks):
            place = z_of(dz)
            at = pl.ds(pl.multiple_of(place * width, 128), width)
            scale = 1.0 + mod_ref[cfg, q, 2:3, at]
            shift = mod_ref[cfg, q, 1:2, at]
            normed = (block[q].astype(F32) - average) * inverse * scale + shift
            normed = normed.astype(BF16)
            for i in range(width // depth):
                rows_ref[
                    place * (width // depth) + i, q * row_count : (q + 1) * row_count, :
                ] = normed[:, i * depth : (i + 1) * depth]
    for dz, block in enumerate(blocks):
        at = pl.ds(pl.multiple_of(z_of(dz) * width, 128), width)
        own_ref[:, at] = block[req]
    step = 256 if hidden % 256 == 0 else hidden
    for h in range(2):
        for c in range(hidden // step):
            total = None
            for k, (dy, dx) in enumerate(around):
                if c == 0:
                    source = pieces[k][1][0]
                    pltpu.make_async_copy(source, buffer.at[h, k], sems.at[h, k]).wait()
                weight = buffer[h, k, :, c * step : (c + 1) * step]
                term = dot(rows_ref[place_of(dx, dy)], weight)
                total = term if total is None else total + term
            out_ref[h, :, c * step : (c + 1) * step] = jax.nn.gelu(
                total, approximate=True
            ).astype(BF16)


def up_products(around, blocks, modulation, pieces):
    requests = len(blocks)
    row_count, slice_width = blocks[0].shape[1:]
    model = requests * slice_width
    depth, hidden = pieces[0][1][0].shape[-2:]
    rows = requests * row_count
    operands = [part for _, parts in pieces for part in parts]
    return pl.pallas_call(
        functools.partial(up_kernel, requests, around, [kind for kind, _ in pieces]),
        out_shape=(
            jax.ShapeDtypeStruct((2, rows, hidden), BF16),
            jax.ShapeDtypeStruct((row_count, model), BF16),
        ),
        in_specs=[whole_spec()] * (requests + 1) + [hbm_spec()] * len(operands),
        out_specs=(whole_spec(), whole_spec()),
        scratch_shapes=[
            pltpu.VMEM((model // depth, rows, depth), BF16),
            pltpu.VMEM((2, len(pieces), depth, hidden), BF16),
            pltpu.SemaphoreType.DMA((2, len(pieces))),
        ],
        compiler_params=params(),
        cost_estimate=cost(8 * rows * model * hidden, 8 * model * hidden),
    )(*blocks, modulation, *operands)


def down_kernel(requests, wide, blocks, weights, earlier, *refs):
    acts, refs = refs[: wide * len(blocks)], refs[wide * len(blocks) :]
    weight_refs, refs = refs[:weights], refs[weights:]
    earlier_refs, refs = refs[: earlier * requests], refs[earlier * requests :]
    out_refs, (scratch_ref, buffer, sems) = refs[:requests], refs[requests:]
    rows, depth = acts[0].shape[1:]
    row_count = rows // requests
    width = buffer.shape[2]
    share = 2 * wide // weights
    for w, weight in enumerate(weight_refs):
        for i in range(share):
            slot = i
            if weights > 1:
                cfg = lax.axis_index("cfg")
                slot = (cfg if w == 0 else 1 - cfg) * share + i
            source = weight.at[pl.ds(i * depth, depth), :]
            pltpu.make_async_copy(source, buffer.at[slot], sems.at[slot]).start()
    for k, ref in enumerate(earlier_refs):
        out_refs[k % requests][len(blocks) + k // requests] = ref[0]
    step = 256 if width % 256 == 0 else width
    for c in range(width // step):
        lanes = slice(c * step, (c + 1) * step)
        total = None
        for far in range(wide):
            for h in range(2):
                slot = 2 * x_of(far) + h
                if c == 0:
                    source = weight_refs[0].at[pl.ds(0, depth), :]
                    pltpu.make_async_copy(source, buffer.at[slot], sems.at[slot]).wait()
                left = [acts[b * wide + far][h] for b in range(len(blocks))]
                left = jnp.concatenate(left, axis=0) if len(left) > 1 else left[0]
                term = dot(left, buffer[slot, :, lanes])
                total = term if total is None else total + term
        scratch_ref[...] = total
        for dz, out_ref in enumerate(out_refs):
            for b in range(len(blocks)):
                first = pl.multiple_of(b * rows + z_of(requests - dz) * row_count, 16)
                out_ref[b, :, lanes] = scratch_ref[pl.ds(first, row_count), :].astype(BF16)


def down_products(blocks, acts, weights, requests, earlier=()):
    rows, depth = acts[0].shape[1:]
    wide = math.isqrt(len(acts))
    width = weights[0].shape[1]
    step = 256 if width % 256 == 0 else width
    shape = (len(blocks) + len(earlier), rows // requests, width)
    done = [part for share in earlier for part in share]
    used = [acts[(e - far) % wide * wide + far] for e in blocks for far in range(wide)]
    return pl.pallas_call(
        functools.partial(down_kernel, requests, wide, blocks, len(weights), len(earlier)),
        out_shape=tuple(jax.ShapeDtypeStruct(shape, BF16) for _ in range(requests)),
        in_specs=[whole_spec()] * len(used)
        + [hbm_spec()] * len(weights)
        + [whole_spec()] * len(done),
        out_specs=tuple(whole_spec() for _ in range(requests)),
        scratch_shapes=[
            pltpu.VMEM((len(blocks) * rows, step), F32),
            pltpu.VMEM((2 * wide, depth, width), BF16),
            pltpu.SemaphoreType.DMA((2 * wide,)),
        ],
        compiler_params=params(),
        cost_estimate=cost(4 * len(used) * rows * depth * width, 4 * wide * depth * width),
    )(*used, *weights, *done)


def per_device(
    queries,
    text_cache,
    image_cache,
    fresh_kv,
    fresh_slots,
    fresh_pos,
    image_len,
    stream,
    modulation,
    out_weight,
    up_weight,
    down_weight,
    final_weight,
    latent,
    step_index,
):
    cfg_id = lax.axis_index("cfg")
    req_id = lax.axis_index("req")
    seq_id = lax.axis_index("seq")
    requests = lax.axis_size("req")
    high, wide = seq_grid(lax.axis_size("seq"))
    y_id, x_id = seq_id // wide, seq_id % wide
    around = [(dy, dx) for dy in range(high) for dx in range(wide)]

    def x_from(step):
        return (x_id - step) % wide

    def y_from(step):
        return (y_id - step) % high

    def seq_from(dy, dx):
        return y_from(dy) * wide + x_from(dx)

    fresh_count = fresh_kv.shape[3]
    padded = -(-fresh_count // 16) * 16
    fresh_pair = rotate_fresh(fresh_kv[0, 0], fresh_pos, padded)
    fresh = [send_seq(fresh_pair, dy, dx) for dy, dx in around]

    out_rows, col_count = out_weight.shape
    seg = col_count // 2
    own_out, _ = lax.optimization_barrier((out_weight, fresh_pair))
    own_out = take(own_out, cfg_id * seg, seg, 1)
    out_y = [send_y(own_out, dy) for dy in range(high)]
    out_x = [send_x(own_out, dx) for dx in range(wide)]

    up_rows, hidden = up_weight.shape
    hidden_x = hidden // wide
    hidden_half = hidden_x // 2
    early_up, _ = lax.optimization_barrier((up_weight, fresh_pair))
    to_x = []
    for dx in range(wide):
        first = (x_id + dx) % wide * hidden_x + cfg_id * hidden_half
        to_x.append(take(early_up, first, hidden_half, 1))
    to_x, out_x, out_y, fresh = lax.optimization_barrier((to_x, out_x, out_y, fresh))
    up_x = [send_x(part, dx) for dx, part in enumerate(to_x)]
    up_y = [send_y(up_x[0], dy) for dy in range(high)]
    out_mine = [send_y(out_x[dx], dy) if dx else out_y[dy] for dy, dx in around]

    length = lax.dynamic_index_in_dim(image_len, req_id, 0, keepdims=False)
    attended = attention(
        around,
        image_len,
        fresh_slots,
        queries[0, 0],
        text_cache[0, 0],
        image_cache[0, 0],
        fresh,
    )
    row_count = queries.shape[2]
    if attended.shape[2] != out_rows:
        attended = jnp.transpose(attended, (1, 0, 2)).reshape(row_count, -1, out_rows)
        attended = jnp.transpose(attended, (1, 0, 2))
    attended_all = [send_z(attended, dz) for dz in range(requests)]
    out_mine, attended, late_up = lax.optimization_barrier((out_mine, attended, up_weight))
    swapped = swap_core(jnp.concatenate(out_mine[1:], axis=0))
    own_up = [
        take(late_up, x_id * hidden_x + h * hidden_half, hidden_half, 1) for h in range(2)
    ]

    attended_all, swapped, up_x, own_up = lax.optimization_barrier(
        (attended_all, swapped, up_x, own_up)
    )
    residual = residual_columns(
        around,
        attended_all,
        out_weight,
        out_mine[1:],
        swapped,
        stream,
        modulation,
    )
    along_z = [send_z(residual, dz) for dz in range(requests)]
    along_z[0] = residual
    near = [[send_x(block, dx) for block in along_z[:2]] for dx in range(1, wide)]

    up_x[1:], _ = lax.optimization_barrier((up_x[1:], residual))
    up_mine = [send_y(up_x[dx], dy) if dx else up_y[dy] for dy, dx in around]

    down_cols = down_weight.shape[1]
    down_half = hidden // 2
    own_down = take(down_weight, cfg_id * down_half, down_half, 0)
    along_z, near, up_mine, own_down = lax.optimization_barrier(
        (along_z, near, up_mine, own_down)
    )
    blocks = [along_z]
    blocks += [
        near[dx - 1] + [send_x(block, dx) for block in along_z[2:]] for dx in range(1, wide)
    ]
    down_mine = [send_y(own_down, dy) for dy in range(1, high)]
    up_pieces = [("halves", own_up)]
    for part, (dy, dx) in zip(up_mine[1:], around[1:]):
        up_pieces.append(("core", [part, swap_core(part)]))

    acts, own_rows = [], []
    for dx in range(wide):
        if acts:
            blocks[dx], acts[0] = lax.optimization_barrier((blocks[dx], acts[0]))
        act, own = up_products(around, blocks[dx], modulation, up_pieces)
        own_rows.append(own)
        acts += [send_x(act, step) for step in range(wide)]

    def sent(share):
        return [send_z(part, dz) for dz, part in enumerate(share)]

    earlier = []
    for e in range(1, wide):
        earlier.append(down_products([e], acts, [down_weight], requests))
        if e == 1:
            acts[-1], earlier[0] = lax.optimization_barrier((acts[-1], earlier[0]))
    share = down_products([0], acts, [down_weight], requests, earlier)
    own_share = sent(share)
    down_mine, _ = lax.optimization_barrier((down_mine, share))
    everything = list(range(wide))
    far_parts = [
        down_products(everything, acts, [mine, swap_core(mine)], requests) for mine in down_mine
    ]
    far_shares = [sent(part) for part in far_parts]
    own_share, _ = lax.optimization_barrier((own_share, far_parts))

    mod_half = lax.dynamic_index_in_dim(modulation, cfg_id, 0, keepdims=False)
    gate_two = lax.dynamic_index_in_dim(mod_half[:, 3, :], req_id, 0, keepdims=False)

    def summed(parts):
        total = parts[0].astype(F32)
        for part in parts[1:]:
            total += part.astype(F32)
        return total

    def finished(total, rows, dy):
        col = seq_from(dy, 0) * down_cols
        block_out = (
            take(rows, col, down_cols, 1).astype(F32)
            + take(gate_two, col, down_cols, 0)[None, :] * total
        ).astype(BF16)
        return dot(block_out, take(final_weight, col, down_cols, 0))

    total = summed(own_share)
    velocity = [finished(total[e], own_rows[e], 0) for e in range(wide)]
    for dy, share in enumerate(far_shares, 1):
        total = summed(share)
        for e in range(wide):
            velocity[e] += finished(total[e], own_rows[e], dy)

    channels = final_weight.shape[1]
    cfg_count = lax.axis_size("cfg")
    halves = []
    for dc in range(2):
        share = 0.0
        for e in range(wide):
            block = velocity[e].reshape(row_count // 2, 2, channels)
            block = lax.dynamic_index_in_dim(block, cfg_id ^ dc, 1, keepdims=False)
            if dc or e:
                route = [
                    ((c * high + y) * wide + x, ((c ^ dc) * high + y) * wide + (x - e) % wide)
                    for c in range(cfg_count)
                    for y in range(high)
                    for x in range(wide)
                ]
                block = lax.ppermute(block, ("cfg", "seq"), route)
            share += block
        halves.append(share)
    cond_part = jnp.where(cfg_id == 0, halves[0], halves[1])
    uncond_part = jnp.where(cfg_id == 0, halves[1], halves[0])
    guided = uncond_part + GUIDANCE * (cond_part - uncond_part)
    level_now = noise_level(step_index[0])
    level_next = noise_level(step_index[0] + 1)
    token_ids = (
        seq_id * row_count
        + 2 * jnp.arange(row_count // 2, dtype=jnp.int32)[:, None]
        + cfg_id
        + jnp.zeros((1, channels), jnp.int32)
    )
    valid = token_ids < length
    current = latent[0]
    latent_next = jnp.where(valid, current + (level_next - level_now) * guided, current)
    denoised = jnp.where(valid, current - level_now * guided, current)
    return (latent_next[None], denoised[None])


def solution(mesh):
    in_specs = (
        P("cfg", "req", "seq", None),
        P("cfg", "req", None, None, None),
        P("cfg", "req", None, None, None),
        P("cfg", "req", None, "seq", None),
        P("req", None),
        P(None, "req", "seq"),
        P(),
        P("cfg", None, "seq", "req"),
        P(),
        P("seq", "req"),
        P("seq", "req"),
        P("req", "seq"),
        P(),
        P("req", "seq", "cfg"),
        P(),
    )
    out_specs = (P("req", "seq", "cfg"), P("req", "seq", "cfg"))
    return jax.shard_map(
        per_device, mesh=mesh, in_specs=in_specs, out_specs=out_specs, check_vma=False
    )
```

```python
import functools
import math

import jax
import jax.numpy as jnp
import numpy as np
from jax import lax
from jax.experimental import pallas as pl
from jax.experimental.pallas import tpu as pltpu
from jax.sharding import PartitionSpec as P

STEPS = 28
GUIDANCE = 3.0
SHIFT = 3.0
SCALE = 1.0 / math.sqrt(128.0)
EPSILON = 1e-06
HEAD = 128
BF16 = jnp.bfloat16
F32 = jnp.float32
MIB = 1024 * 1024


def noise_level(index):
    fraction = 1.0 - index.astype(jnp.float32) / STEPS
    return SHIFT * fraction / (SHIFT * fraction + 1.0 - fraction)


def lane_frequencies():
    rows = np.zeros((3, HEAD), np.float32)
    lane = 0
    for component, axis_span in ((0, 16), (1, 56), (2, 56)):
        pair_ids = np.arange(axis_span // 2, dtype=np.float32)
        frequency = np.exp(-(2.0 * pair_ids / axis_span) * np.float32(math.log(10000.0)))
        rows[component, lane : lane + axis_span] = np.repeat(frequency, 2)
        lane += axis_span
    return rows


def seq_grid(count):
    columns = 2 ** ((count.bit_length() - 1) // 2)
    return count // columns, columns


def send_x(block, step):
    if step == 0:
        return block
    high, wide = seq_grid(lax.axis_size("seq"))
    route = [(y * wide + x, y * wide + (x + step) % wide) for y in range(high) for x in range(wide)]
    return lax.ppermute(block, "seq", route)


def send_y(block, step):
    if step == 0:
        return block
    high, wide = seq_grid(lax.axis_size("seq"))
    route = [(y * wide + x, (y + step) % high * wide + x) for y in range(high) for x in range(wide)]
    return lax.ppermute(block, "seq", route)


def send_seq(block, dy, dx):
    if dy == 0 and dx == 0:
        return block
    high, wide = seq_grid(lax.axis_size("seq"))
    route = [
        (y * wide + x, (y + dy) % high * wide + (x + dx) % wide)
        for y in range(high)
        for x in range(wide)
    ]
    return lax.ppermute(block, "seq", route)


def send_z(block, step):
    if step == 0:
        return block
    count = lax.axis_size("req")
    return lax.ppermute(block, "req", [(r, (r + step) % count) for r in range(count)])


def swap_core(block):
    return lax.ppermute(block, "cfg", [(0, 1), (1, 0)])


def take(array, start, size, axis):
    return lax.dynamic_slice_in_dim(array, start, size, axis)


def dot(left, right):
    return jnp.dot(left, right, preferred_element_type=jnp.float32)


def hbm_spec():
    return pl.BlockSpec(memory_space=pl.ANY)


def place_of(step_x, step_y=0):
    high, wide = seq_grid(lax.axis_size("seq"))
    seq = lax.axis_index("seq")
    return lax.rem(seq // wide + high - step_y, high) * wide + x_of(step_x)


def x_of(step):
    wide = seq_grid(lax.axis_size("seq"))[1]
    return lax.rem(lax.axis_index("seq") % wide + 2 * wide - step, wide)


def z_of(step):
    count = lax.axis_size("req")
    return lax.rem(lax.axis_index("req") + count - step, count)


def whole_spec():
    return pl.BlockSpec(memory_space=pltpu.VMEM)


def smem_spec():
    return pl.BlockSpec(memory_space=pltpu.SMEM)


def cost(flops, moved):
    return pl.CostEstimate(flops=int(flops), bytes_accessed=int(moved), transcendentals=0)


def params():
    return pltpu.CompilerParams(vmem_limit_bytes=60 * MIB)


def rotate_kernel(kv_ref, pos_ref, freq_ref, out_ref):
    rows, width = kv_ref.shape[1:]
    row_ids = lax.broadcasted_iota(jnp.int32, (rows, HEAD), 0)
    angles = jnp.zeros((rows, HEAD), F32)
    for row in range(rows):
        line = (
            pos_ref[0, 0, row].astype(F32) * freq_ref[0:1, :]
            + pos_ref[1, 0, row].astype(F32) * freq_ref[1:2, :]
            + pos_ref[2, 0, row].astype(F32) * freq_ref[2:3, :]
        )
        angles = jnp.where(row_ids == row, line, angles)
    cosine, sine = jnp.cos(angles), jnp.sin(angles)
    even = lax.broadcasted_iota(jnp.int32, (rows, HEAD), 1) % 2 == 0
    out_ref[...] = jnp.zeros_like(out_ref)
    for first in range(0, width, HEAD):
        keys = kv_ref[0, :, first : first + HEAD].astype(F32)
        after = pltpu.roll(keys, HEAD - 1, 1)
        before = pltpu.roll(keys, 1, 1)
        rotated = cosine * keys + sine * jnp.where(even, -after, before)
        out_ref[0, 0:rows, first : first + HEAD] = rotated.astype(BF16)
    out_ref[1, 0:rows, :] = kv_ref[1]


def rotate_fresh(fresh, positions, padded):
    width = fresh.shape[2]
    return pl.pallas_call(
        rotate_kernel,
        out_shape=jax.ShapeDtypeStruct((2, padded, width), BF16),
        in_specs=[whole_spec(), smem_spec(), whole_spec()],
        out_specs=whole_spec(),
        compiler_params=params(),
    )(fresh, positions, jnp.asarray(lane_frequencies()))


def attention_kernel(around, lengths_ref, slots_ref, q_ref, text_ref, image_ref, *refs):
    pieces = len(around)
    fresh_refs, (out_ref, fresh_ref) = refs[:pieces], refs[pieces:]
    padded = fresh_refs[0].shape[1]
    for i in range(pieces):
        fresh_ref[:, i * padded : (i + 1) * padded, :] = fresh_refs[i][...]
    slots = image_ref.shape[1]
    count = slots_ref.shape[1] // pieces
    length = lengths_ref[lax.axis_index("req")]
    key_ids = lax.broadcasted_iota(jnp.int32, (1, slots), 1)
    fresh_ids = lax.broadcasted_iota(jnp.int32, (1, pieces * padded), 1)
    image_bias = jnp.where(key_ids < length, 0.0, -jnp.inf)
    fresh_bias = jnp.full(fresh_ids.shape, -jnp.inf, F32)
    for i, (dy, dx) in enumerate(around):
        first = place_of(dx, dy) * count
        for j in range(count):
            slot = slots_ref[0, first + j]
            image_bias = jnp.where(key_ids == slot, -jnp.inf, image_bias)
            here = (fresh_ids == i * padded + j) & (slot < length)
            fresh_bias = jnp.where(here, 0.0, fresh_bias)
    over_lanes = (((1,), (1,)), ((), ()))
    for first in range(0, q_ref.shape[1], HEAD):
        head = slice(first, first + HEAD)
        query = q_ref[:, head]

        def scores(keys):
            return lax.dot_general(query, keys, over_lanes, preferred_element_type=F32) * SCALE

        text = scores(text_ref[0, :, head])
        image = scores(image_ref[0, :, head]) + image_bias
        fresh = scores(fresh_ref[0, :, head]) + fresh_bias
        best = jnp.maximum(
            jnp.max(text, axis=1, keepdims=True),
            jnp.maximum(
                jnp.max(image, axis=1, keepdims=True), jnp.max(fresh, axis=1, keepdims=True)
            ),
        )
        text, image, fresh = jnp.exp(text - best), jnp.exp(image - best), jnp.exp(fresh - best)
        total = (
            jnp.sum(text, axis=1, keepdims=True)
            + jnp.sum(image, axis=1, keepdims=True)
            + jnp.sum(fresh, axis=1, keepdims=True)
        )
        mixed = (
            dot(text.astype(BF16), text_ref[1, :, head])
            + dot(image.astype(BF16), image_ref[1, :, head])
            + dot(fresh.astype(BF16), fresh_ref[1, :, head])
        )
        out_ref[0, :, head] = (mixed / total).astype(BF16)


def attention(around, lengths, slot_ids, query, text_kv, image_kv, fresh):
    rows, width = query.shape
    group = 3 * HEAD
    groups = width // group
    text, slots = text_kv.shape[1], image_kv.shape[1]
    pieces, padded = len(fresh), fresh[0].shape[1]
    return pl.pallas_call(
        functools.partial(attention_kernel, around),
        grid=(groups,),
        out_shape=jax.ShapeDtypeStruct((groups, rows, group), BF16),
        in_specs=[
            smem_spec(),
            smem_spec(),
            pl.BlockSpec((rows, group), lambda g: (0, g)),
            pl.BlockSpec((2, text, group), lambda g: (0, 0, g)),
            pl.BlockSpec((2, slots, group), lambda g: (0, 0, g)),
        ]
        + [pl.BlockSpec((2, padded, group), lambda g: (0, 0, g))] * pieces,
        out_specs=pl.BlockSpec((1, rows, group), lambda g: (g, 0, 0)),
        scratch_shapes=[pltpu.VMEM((2, padded * pieces, group), BF16)],
        compiler_params=params(),
    )(lengths, slot_ids, query, text_kv, image_kv, *fresh)


def residual_kernel(requests, around, *refs):
    pieces = len(around)
    attended, refs = refs[:requests], refs[requests:]
    own_ref, mine, refs = refs[0], refs[1:pieces], refs[pieces:]
    swapped_ref, stream_ref, mod_ref, out_ref, rows_ref = refs
    row_count = attended[0].shape[1]
    depth, width = own_ref.shape
    half_width = width // 2
    cfg, req = lax.axis_index("cfg"), lax.axis_index("req")
    places = [place_of(dx, dy) for dy, dx in around]
    for j in range(requests):
        first = pl.multiple_of(z_of(j) * row_count, 16)
        rows_ref[:, pl.ds(first, row_count), :] = attended[j][...]
    at = pl.multiple_of(req * width, 128)
    gates = [mod_ref[cfg, q, 0:1, pl.ds(at, width)] for q in range(requests)]

    def columns(core):
        for role, half in ((0, core), (1, 1 - core)):
            lanes = slice(half * half_width, (half + 1) * half_width)
            total = dot(rows_ref[places[0]], own_ref[:, lanes])
            for k in range(1, pieces):
                piece = swapped_ref[(k - 1) * depth : k * depth, :] if role else mine[k - 1][...]
                total += dot(rows_ref[places[k]], piece)
            for q in range(requests):
                out_ref[q, :, lanes] = (
                    stream_ref[0, q, :, lanes].astype(F32)
                    + gates[q][:, lanes] * total[q * row_count : (q + 1) * row_count]
                ).astype(BF16)

    pl.when(cfg == 0)(functools.partial(columns, 0))
    pl.when(cfg == 1)(functools.partial(columns, 1))


def residual_columns(around, attended, own, mine, swapped, stream, modulation):
    requests, pieces = len(attended), len(mine) + 1
    segments, row_count, seg = attended[0].shape
    return pl.pallas_call(
        functools.partial(residual_kernel, requests, around),
        out_shape=jax.ShapeDtypeStruct(stream.shape[1:], BF16),
        in_specs=[whole_spec()] * (requests + pieces + 3),
        out_specs=whole_spec(),
        scratch_shapes=[pltpu.VMEM((segments, requests * row_count, seg), BF16)],
        compiler_params=params(),
    )(*attended, own, *mine, swapped, stream, modulation)


def copies_of(pieces, buffer, sems):
    cfg = lax.axis_index("cfg")
    copies = []
    for k, (kind, parts) in enumerate(pieces):
        for h in range(2):
            slot = h
            if kind == "core":
                slot = cfg if h == 0 else 1 - cfg
            copies.append(
                (h, pltpu.make_async_copy(parts[h], buffer.at[slot, k], sems.at[slot, k]))
            )
    return [copy for h in range(2) for half, copy in copies if half == h]


def up_kernel(requests, around, kinds, *refs):
    blocks, refs = refs[:requests], refs[requests:]
    mod_ref, refs = refs[0], refs[1:]
    pieces = []
    for kind in kinds:
        pieces.append((kind, refs[:2]))
        refs = refs[2:]
    out_ref, own_ref, rows_ref, buffer, sems = refs
    row_count, width = blocks[0].shape[1:]
    depth, hidden = buffer.shape[2:]
    cfg, req = lax.axis_index("cfg"), lax.axis_index("req")
    scale_of_mean = 1.0 / (requests * width)
    for copy in copies_of(pieces, buffer, sems):
        copy.start()
    for q in range(requests):
        total = jnp.zeros((row_count, 1), F32)
        for block in blocks:
            total += jnp.sum(block[q].astype(F32), axis=1, keepdims=True)
        average = total * scale_of_mean
        total = jnp.zeros((row_count, 1), F32)
        for block in blocks:
            centered = block[q].astype(F32) - average
            total += jnp.sum(centered * centered, axis=1, keepdims=True)
        inverse = lax.rsqrt(total * scale_of_mean + EPSILON)
        for dz, block in enumerate(blocks):
            place = z_of(dz)
            at = pl.ds(pl.multiple_of(place * width, 128), width)
            scale = 1.0 + mod_ref[cfg, q, 2:3, at]
            shift = mod_ref[cfg, q, 1:2, at]
            normed = (block[q].astype(F32) - average) * inverse * scale + shift
            normed = normed.astype(BF16)
            for i in range(width // depth):
                rows_ref[
                    place * (width // depth) + i, q * row_count : (q + 1) * row_count, :
                ] = normed[:, i * depth : (i + 1) * depth]
    for dz, block in enumerate(blocks):
        at = pl.ds(pl.multiple_of(z_of(dz) * width, 128), width)
        own_ref[:, at] = block[req]
    step = 256 if hidden % 256 == 0 else hidden
    for h in range(2):
        for c in range(hidden // step):
            total = None
            for k, (dy, dx) in enumerate(around):
                if c == 0:
                    source = pieces[k][1][0]
                    pltpu.make_async_copy(source, buffer.at[h, k], sems.at[h, k]).wait()
                weight = buffer[h, k, :, c * step : (c + 1) * step]
                term = dot(rows_ref[place_of(dx, dy)], weight)
                total = term if total is None else total + term
            out_ref[h, :, c * step : (c + 1) * step] = jax.nn.gelu(
                total, approximate=True
            ).astype(BF16)


def up_products(around, blocks, modulation, pieces):
    requests = len(blocks)
    row_count, slice_width = blocks[0].shape[1:]
    model = requests * slice_width
    depth, hidden = pieces[0][1][0].shape[-2:]
    rows = requests * row_count
    operands = [part for _, parts in pieces for part in parts]
    return pl.pallas_call(
        functools.partial(up_kernel, requests, around, [kind for kind, _ in pieces]),
        out_shape=(
            jax.ShapeDtypeStruct((2, rows, hidden), BF16),
            jax.ShapeDtypeStruct((row_count, model), BF16),
        ),
        in_specs=[whole_spec()] * (requests + 1) + [hbm_spec()] * len(operands),
        out_specs=(whole_spec(), whole_spec()),
        scratch_shapes=[
            pltpu.VMEM((model // depth, rows, depth), BF16),
            pltpu.VMEM((2, len(pieces), depth, hidden), BF16),
            pltpu.SemaphoreType.DMA((2, len(pieces))),
        ],
        compiler_params=params(),
        cost_estimate=cost(8 * rows * model * hidden, 8 * model * hidden),
    )(*blocks, modulation, *operands)


def down_kernel(requests, wide, blocks, weights, earlier, *refs):
    acts, refs = refs[: wide * len(blocks)], refs[wide * len(blocks) :]
    weight_refs, refs = refs[:weights], refs[weights:]
    earlier_refs, refs = refs[: earlier * requests], refs[earlier * requests :]
    out_refs, (scratch_ref, buffer, sems) = refs[:requests], refs[requests:]
    rows, depth = acts[0].shape[1:]
    row_count = rows // requests
    width = buffer.shape[2]
    share = 2 * wide // weights
    for w, weight in enumerate(weight_refs):
        for i in range(share):
            slot = i
            if weights > 1:
                cfg = lax.axis_index("cfg")
                slot = (cfg if w == 0 else 1 - cfg) * share + i
            source = weight.at[pl.ds(i * depth, depth), :]
            pltpu.make_async_copy(source, buffer.at[slot], sems.at[slot]).start()
    for k, ref in enumerate(earlier_refs):
        out_refs[k % requests][len(blocks) + k // requests] = ref[0]
    step = 256 if width % 256 == 0 else width
    for c in range(width // step):
        lanes = slice(c * step, (c + 1) * step)
        total = None
        for far in range(wide):
            for h in range(2):
                slot = 2 * x_of(far) + h
                if c == 0:
                    source = weight_refs[0].at[pl.ds(0, depth), :]
                    pltpu.make_async_copy(source, buffer.at[slot], sems.at[slot]).wait()
                left = [acts[b * wide + far][h] for b in range(len(blocks))]
                left = jnp.concatenate(left, axis=0) if len(left) > 1 else left[0]
                term = dot(left, buffer[slot, :, lanes])
                total = term if total is None else total + term
        scratch_ref[...] = total
        for dz, out_ref in enumerate(out_refs):
            for b in range(len(blocks)):
                first = pl.multiple_of(b * rows + z_of(requests - dz) * row_count, 16)
                out_ref[b, :, lanes] = scratch_ref[pl.ds(first, row_count), :].astype(BF16)


def down_products(blocks, acts, weights, requests, earlier=()):
    rows, depth = acts[0].shape[1:]
    wide = math.isqrt(len(acts))
    width = weights[0].shape[1]
    step = 256 if width % 256 == 0 else width
    shape = (len(blocks) + len(earlier), rows // requests, width)
    done = [part for share in earlier for part in share]
    used = [acts[(e - far) % wide * wide + far] for e in blocks for far in range(wide)]
    return pl.pallas_call(
        functools.partial(down_kernel, requests, wide, blocks, len(weights), len(earlier)),
        out_shape=tuple(jax.ShapeDtypeStruct(shape, BF16) for _ in range(requests)),
        in_specs=[whole_spec()] * len(used)
        + [hbm_spec()] * len(weights)
        + [whole_spec()] * len(done),
        out_specs=tuple(whole_spec() for _ in range(requests)),
        scratch_shapes=[
            pltpu.VMEM((len(blocks) * rows, step), F32),
            pltpu.VMEM((2 * wide, depth, width), BF16),
            pltpu.SemaphoreType.DMA((2 * wide,)),
        ],
        compiler_params=params(),
        cost_estimate=cost(4 * len(used) * rows * depth * width, 4 * wide * depth * width),
    )(*used, *weights, *done)


def per_device(
    queries,
    text_cache,
    image_cache,
    fresh_kv,
    fresh_slots,
    fresh_pos,
    image_len,
    stream,
    modulation,
    out_weight,
    up_weight,
    down_weight,
    final_weight,
    latent,
    step_index,
):
    cfg_id = lax.axis_index("cfg")
    req_id = lax.axis_index("req")
    seq_id = lax.axis_index("seq")
    requests = lax.axis_size("req")
    high, wide = seq_grid(lax.axis_size("seq"))
    y_id, x_id = seq_id // wide, seq_id % wide
    around = [(dy, dx) for dy in range(high) for dx in range(wide)]

    def x_from(step):
        return (x_id - step) % wide

    def y_from(step):
        return (y_id - step) % high

    def seq_from(dy, dx):
        return y_from(dy) * wide + x_from(dx)

    fresh_count = fresh_kv.shape[3]
    padded = -(-fresh_count // 16) * 16
    fresh_pair = rotate_fresh(fresh_kv[0, 0], fresh_pos, padded)
    fresh = [send_seq(fresh_pair, dy, dx) for dy, dx in around]

    out_rows, col_count = out_weight.shape
    seg = col_count // 2
    own_out, _ = lax.optimization_barrier((out_weight, fresh_pair))
    own_out = take(own_out, cfg_id * seg, seg, 1)
    out_y = [send_y(own_out, dy) for dy in range(high)]
    out_x = [send_x(own_out, dx) for dx in range(wide)]

    up_rows, hidden = up_weight.shape
    hidden_x = hidden // wide
    hidden_half = hidden_x // 2
    early_up, _ = lax.optimization_barrier((up_weight, fresh_pair))
    to_x = []
    for dx in range(wide):
        first = (x_id + dx) % wide * hidden_x + cfg_id * hidden_half
        to_x.append(take(early_up, first, hidden_half, 1))
    to_x, out_x, out_y, fresh = lax.optimization_barrier((to_x, out_x, out_y, fresh))
    up_x = [send_x(part, dx) for dx, part in enumerate(to_x)]
    up_y = [send_y(up_x[0], dy) for dy in range(high)]
    out_mine = [send_y(out_x[dx], dy) if dx else out_y[dy] for dy, dx in around]

    length = lax.dynamic_index_in_dim(image_len, req_id, 0, keepdims=False)
    attended = attention(
        around,
        image_len,
        fresh_slots,
        queries[0, 0],
        text_cache[0, 0],
        image_cache[0, 0],
        fresh,
    )
    row_count = queries.shape[2]
    if attended.shape[2] != out_rows:
        attended = jnp.transpose(attended, (1, 0, 2)).reshape(row_count, -1, out_rows)
        attended = jnp.transpose(attended, (1, 0, 2))
    attended_all = [send_z(attended, dz) for dz in range(requests)]
    out_mine, attended, late_up = lax.optimization_barrier((out_mine, attended, up_weight))
    swapped = swap_core(jnp.concatenate(out_mine[1:], axis=0))
    own_up = [
        take(late_up, x_id * hidden_x + h * hidden_half, hidden_half, 1) for h in range(2)
    ]

    attended_all, swapped, up_x, own_up = lax.optimization_barrier(
        (attended_all, swapped, up_x, own_up)
    )
    residual = residual_columns(
        around,
        attended_all,
        out_weight,
        out_mine[1:],
        swapped,
        stream,
        modulation,
    )
    along_z = [send_z(residual, dz) for dz in range(requests)]
    along_z[0] = residual
    near = [[send_x(block, dx) for block in along_z[:2]] for dx in range(1, wide)]

    up_x[1:], up_y[1:], _ = lax.optimization_barrier((up_x[1:], up_y[1:], residual))
    up_mine = [send_y(up_x[dx], dy) if dx else up_y[dy] for dy, dx in around]

    down_cols = down_weight.shape[1]
    down_half = hidden // 2
    own_down = take(down_weight, cfg_id * down_half, down_half, 0)
    along_z, near, up_mine, own_down = lax.optimization_barrier(
        (along_z, near, up_mine, own_down)
    )
    blocks = [along_z]
    blocks += [
        near[dx - 1] + [send_x(block, dx) for block in along_z[2:]] for dx in range(1, wide)
    ]
    down_mine = [send_y(own_down, dy) for dy in range(1, high)]
    up_pieces = [("halves", own_up)]
    for part, (dy, dx) in zip(up_mine[1:], around[1:]):
        up_pieces.append(("core", [part, swap_core(part)]))

    acts, own_rows = [], []
    for dx in range(wide):
        if acts:
            blocks[dx], acts[0] = lax.optimization_barrier((blocks[dx], acts[0]))
        act, own = up_products(around, blocks[dx], modulation, up_pieces)
        own_rows.append(own)
        acts += [send_x(act, step) for step in range(wide)]

    def sent(share):
        return [send_z(part, dz) for dz, part in enumerate(share)]

    earlier = []
    for e in range(1, wide):
        earlier.append(down_products([e], acts, [down_weight], requests))
        if e == 1:
            acts[-1], earlier[0] = lax.optimization_barrier((acts[-1], earlier[0]))
    share = down_products([0], acts, [down_weight], requests, earlier)
    own_share = sent(share)
    down_mine, _ = lax.optimization_barrier((down_mine, share))
    everything = list(range(wide))
    far_parts = [
        down_products(everything, acts, [mine, swap_core(mine)], requests) for mine in down_mine
    ]
    far_shares = [sent(part) for part in far_parts]
    own_share, _ = lax.optimization_barrier((own_share, far_parts))

    mod_half = lax.dynamic_index_in_dim(modulation, cfg_id, 0, keepdims=False)
    gate_two = lax.dynamic_index_in_dim(mod_half[:, 3, :], req_id, 0, keepdims=False)

    def summed(parts):
        total = parts[0].astype(F32)
        for part in parts[1:]:
            total += part.astype(F32)
        return total

    def finished(total, rows, dy):
        col = seq_from(dy, 0) * down_cols
        block_out = (
            take(rows, col, down_cols, 1).astype(F32)
            + take(gate_two, col, down_cols, 0)[None, :] * total
        ).astype(BF16)
        return dot(block_out, take(final_weight, col, down_cols, 0))

    total = summed(own_share)
    velocity = [finished(total[e], own_rows[e], 0) for e in range(wide)]
    for dy, share in enumerate(far_shares, 1):
        total = summed(share)
        for e in range(wide):
            velocity[e] += finished(total[e], own_rows[e], dy)

    channels = final_weight.shape[1]
    cfg_count = lax.axis_size("cfg")
    halves = []
    for dc in range(2):
        share = 0.0
        for e in range(wide):
            block = velocity[e].reshape(row_count // 2, 2, channels)
            block = lax.dynamic_index_in_dim(block, cfg_id ^ dc, 1, keepdims=False)
            if dc or e:
                route = [
                    ((c * high + y) * wide + x, ((c ^ dc) * high + y) * wide + (x - e) % wide)
                    for c in range(cfg_count)
                    for y in range(high)
                    for x in range(wide)
                ]
                block = lax.ppermute(block, ("cfg", "seq"), route)
            share += block
        halves.append(share)
    cond_part = jnp.where(cfg_id == 0, halves[0], halves[1])
    uncond_part = jnp.where(cfg_id == 0, halves[1], halves[0])
    guided = uncond_part + GUIDANCE * (cond_part - uncond_part)
    level_now = noise_level(step_index[0])
    level_next = noise_level(step_index[0] + 1)
    token_ids = (
        seq_id * row_count
        + 2 * jnp.arange(row_count // 2, dtype=jnp.int32)[:, None]
        + cfg_id
        + jnp.zeros((1, channels), jnp.int32)
    )
    valid = token_ids < length
    current = latent[0]
    latent_next = jnp.where(valid, current + (level_next - level_now) * guided, current)
    denoised = jnp.where(valid, current - level_now * guided, current)
    return (latent_next[None], denoised[None])


def solution(mesh):
    in_specs = (
        P("cfg", "req", "seq", None),
        P("cfg", "req", None, None, None),
        P("cfg", "req", None, None, None),
        P("cfg", "req", None, "seq", None),
        P("req", None),
        P(None, "req", "seq"),
        P(),
        P("cfg", None, "seq", "req"),
        P(),
        P("seq", "req"),
        P("seq", "req"),
        P("req", "seq"),
        P(),
        P("req", "seq", "cfg"),
        P(),
    )
    out_specs = (P("req", "seq", "cfg"), P("req", "seq", "cfg"))
    return jax.shard_map(
        per_device, mesh=mesh, in_specs=in_specs, out_specs=out_specs, check_vma=False
    )
```
